32 devices in a mesh: section: 2 (over core), seq: 16 (over z, y, x).
Axes of the slice: x: 2, y: 2, z: 4, core: 2. Of those that a mesh axis runs over, the one named last changes fastest.
Arguments:
- boundary: bfloat16 [2, 2, 1536, 1024], P('section', None, 'seq'), may hold values from -6 to 6
- lengths: int32 [2], replicated, may hold values from 1 to 1536, as said below
- norm_gains: bfloat16 [2, 2, 1024], P('section', None, 'seq'), may hold values from 0.5 to 1.5
- w_qkv: bfloat16 [2, 1024, 768], P('section', 'seq'), may hold values from -0.25 to 0.25
- w_attn: bfloat16 [2, 512, 1024], P('section', 'seq'), may hold values from -1 to 1
- w_in: bfloat16 [2, 1024, 3328], P('section', 'seq'), may hold values from -0.1875 to 0.1875
- w_dt: bfloat16 [2, 1024, 24], P('section', 'seq'), may hold values from -0.1875 to 0.1875
- conv_params: bfloat16 [2, 5, 1792], P('section', None, 'seq'), may hold values from -3 to 3
- head_params: float32 [2, 3, 24], P('section'), may hold values from -13 to 2.5
- w_out: bfloat16 [2, 1536, 1024], P('section', 'seq'), may hold values from -0.4375 to 0.4375
- w_gate_up: bfloat16 [2, 1024, 4096], P('section', 'seq'), may hold values from -0.1875 to 0.1875
- w_down: bfloat16 [2, 2048, 1024], P('section', 'seq'), may hold values from -0.1875 to 0.1875
Outputs:
- ends: float32 [2, 2, 1536, 1024], P('section', None, 'seq')
- grad_gains: float32 [2, 2, 1024], P('section', None, 'seq')
- grad_qkv: float32 [2, 1024, 768], P('section', 'seq')
- grad_attn: float32 [2, 512, 1024], P('section', 'seq')
- grad_in: float32 [2, 1024, 3328], P('section', 'seq')
- grad_dt: float32 [2, 1024, 24], P('section', 'seq')
- grad_conv: float32 [2, 5, 1792], P('section', None, 'seq')
- grad_heads: float32 [2, 3, 24], P('section')
- grad_out: float32 [2, 1536, 1024], P('section', 'seq')
- grad_gate_up: float32 [2, 1024, 4096], P('section', 'seq')
- grad_down: float32 [2, 2048, 1024], P('section', 'seq')
The draws below stay inside these ranges and needn't reach their ends.
Inputs may be any that keep to these rules, and one draw needn't show every extreme that they name: `lengths`: some sequence has length 1536.
All inputs are finite; a program needn't handle non-finite values.
Results may differ from the reference program's by a relative error of at most 0.02.
Values may be sent and summed in bfloat16 or wider, within the bound.
No kernel may reach another device: no remote copies, remote signals or barrier semaphores. Data moves between devices by JAX's collectives and lax.ppermute only.
A program may use at most 384 MiB of HBM per device.

```python
import jax
import jax.numpy as jnp
from jax import lax

D = 1024
QUERY_HEADS = 8
KEY_VALUE_HEADS = 2
HEAD_SIZE = 64
SH = 24
P_SIZE = 64
N = 128
FF = 2048
CONV = 4
L = 1536
SEQS = 2
QKV = 768
DSSM = 1536
XBC = 1792


def draw_lengths(key, part):
    key = jax.random.fold_in(key, 1)
    base_key, pick_key = jax.random.split(key)
    drawn = jax.random.randint(base_key, (SEQS,), 1, L + 1, dtype=jnp.int32)
    chosen = jax.random.randint(pick_key, (), 0, SEQS, dtype=jnp.int32)
    return jnp.where(jnp.arange(SEQS, dtype=jnp.int32) == chosen, L, drawn).astype(jnp.int32)


def draw_head_params(key, part):
    key = jax.random.fold_in(key, 2)
    rate_key, decay_key, skip_key = jax.random.split(key, 3)
    rate_low, rate_high, skip_low, skip_high = (0.3 / L, 1.0 / 32.0, 0.5, 1.5)
    log_rate = jax.random.uniform(rate_key, (2, SH), jnp.float32, jnp.log(rate_low), jnp.log(rate_high))
    decay_log = jax.random.uniform(decay_key, (2, SH), jnp.float32, 0.0, 2.5)
    step_bias = jnp.log(jnp.expm1(jnp.exp(log_rate) / jnp.exp(decay_log)))
    skip_weight = jax.random.uniform(skip_key, (2, SH), jnp.float32, skip_low, skip_high)
    return jnp.stack([step_bias, decay_log, skip_weight], axis=1).astype(jnp.float32)


def block_scale(rng, extent, shards, smallest, largest):
    def one(axis_at, blocks):
        draws = jax.random.uniform(jax.random.fold_in(jax.random.fold_in(rng, 6), axis_at), (blocks,), jnp.float32, smallest / len(shards), largest / len(shards))
        return jnp.repeat(jnp.exp(draws), extent[axis_at] // blocks).reshape((-1,) + (1,) * (len(extent) - axis_at - 1))

    factor_of = one(*shards[0])
    for cut in shards[1:]:
        factor_of = factor_of * one(*cut)
    return factor_of


def noise(stream_key, extent, width, limit, pieces=(), held_as=jnp.bfloat16):
    values = width * jax.random.normal(stream_key, extent, jnp.float32)
    if pieces:
        values = values * block_scale(stream_key, extent, pieces, -0.22, 0.18)
    return jnp.clip(values, -limit, limit).astype(held_as)


def setup_inputs(seed: int = 0) -> dict:
    key_list = jax.random.split(jax.random.key(seed), 13)
    boundary = noise(key_list[0], (2, SEQS, L, D), 1.0, 6.0, ((0, 2), (2, 16)))
    lengths = draw_lengths(jax.random.fold_in(key_list[12], 71), 0)
    norm_gains = jnp.clip(1.0 + 0.1 * jax.random.normal(key_list[2], (2, 2, D), jnp.float32), 0.5, 1.5).astype(jnp.bfloat16)
    w_qkv = noise(key_list[3], (2, D, QKV), (D // 2) ** -0.5, 0.25, ((0, 2), (1, 16)))
    w_attn = noise(key_list[4], (2, QUERY_HEADS * HEAD_SIZE, D), (QUERY_HEADS * HEAD_SIZE // 16) ** -0.5, 1.0, ((0, 2), (1, 16)))
    w_in = noise(key_list[5], (2, D, DSSM + XBC), D ** -0.5, 0.1875, ((0, 2), (1, 16)))
    w_dt = noise(key_list[6], (2, D, SH), D ** -0.5, 0.1875, ((0, 2), (1, 16)))
    conv_params = noise(key_list[7], (2, CONV + 1, XBC), 0.5, 3.0, ((0, 2), (2, 16)))
    head_params = draw_head_params(jax.random.fold_in(key_list[12], 71), 0)
    w_out = noise(key_list[9], (2, DSSM, D), (DSSM // 8) ** -0.5, 0.4375, ((0, 2), (1, 16)))
    w_gate_up = noise(key_list[10], (2, D, 2 * FF), D ** -0.5, 0.1875, ((0, 2), (1, 16)))
    w_down = noise(key_list[11], (2, FF, D), (FF // 2) ** -0.5, 0.1875, ((0, 2), (1, 16)))
    return {"boundary": boundary, "lengths": lengths, "norm_gains": norm_gains, "w_qkv": w_qkv, "w_attn": w_attn, "w_in": w_in, "w_dt": w_dt, "conv_params": conv_params, "head_params": head_params, "w_out": w_out, "w_gate_up": w_gate_up, "w_down": w_down}


eps = 1e-05
ROPE_BASE = 100000000000.0
HIGHEST = lax.Precision.HIGHEST

@jax.custom_vjp
def low(v):
    return lax.optimization_barrier(v.astype(jnp.bfloat16)).astype(jnp.float32)

@jax.custom_vjp
def low_back(v):
    return v

def low_keep(v):
    return (low(v), None)

def low_pass(kept, grad):
    return (grad,)

def back_keep(v):
    return (v, None)

def back_low(kept, grad):
    return (low(grad),)
low.defvjp(low_keep, low_pass)
low_back.defvjp(back_keep, back_low)

def rms_scale(hidden, gain):
    return hidden * lax.rsqrt(lax.optimization_barrier(jnp.mean(hidden * hidden, axis=-1, keepdims=True)) + eps) * gain

def apply_rotation(heads_in, token_positions):
    half_width = heads_in.shape[-1] // 2
    frequency = ROPE_BASE ** (-jnp.arange(half_width, dtype=jnp.float32) / half_width)
    angles = token_positions.astype(jnp.float32)[:, None] * frequency[None, :]
    cosine = jnp.cos(angles)[:, None, :]
    sine_table = jnp.sin(angles)[:, None, :]
    lower_half = heads_in[..., :half_width]
    upper_half = heads_in[..., half_width:]
    return jnp.concatenate([lower_half * cosine - upper_half * sine_table, upper_half * cosine + lower_half * sine_table], axis=-1)

def project_heads(query_key_value, token_positions):
    leading_axes = query_key_value.shape[:-1]
    query_width = QUERY_HEADS * HEAD_SIZE
    key_value_width = KEY_VALUE_HEADS * HEAD_SIZE
    query_rows = apply_rotation(query_key_value[..., :query_width].reshape(leading_axes + (QUERY_HEADS, HEAD_SIZE)), token_positions).reshape(leading_axes + (query_width,))
    key_row_block = apply_rotation(query_key_value[..., query_width:query_width + key_value_width].reshape(leading_axes + (KEY_VALUE_HEADS, HEAD_SIZE)), token_positions).reshape(leading_axes + (key_value_width,))
    return (query_rows, key_row_block, query_key_value[..., query_width + key_value_width:])

def convolve(extended, conv_params):
    span_length = extended.shape[1] - (CONV - 1)
    summed = conv_params[CONV]
    for offset in range(CONV):
        summed = summed + conv_params[offset] * extended[:, offset:offset + span_length]
    return jax.nn.silu(summed)

def ssd_inputs(conv_out, dt_raw, heads_row):
    leading_axes = conv_out.shape[:2]
    inputs_x = conv_out[..., :DSSM].reshape(leading_axes + (SH, P_SIZE))
    b_proj = conv_out[..., DSSM:DSSM + N]
    c_proj = conv_out[..., DSSM + N:]
    step_size = jax.nn.softplus(dt_raw + heads_row[0])
    log_decay = -step_size * jnp.exp(heads_row[1])
    return (inputs_x, inputs_x * step_size[..., None], b_proj, c_proj, log_decay)

def intra_terms(dt_x, b_proj, c_proj, cumulative):
    block_len = cumulative.shape[1]
    position = jnp.arange(block_len, dtype=jnp.int32)
    causal = (position[:, None] >= position[None, :])[None, :, :, None]
    gap_matrix = cumulative[:, :, None, :] - cumulative[:, None, :, :]
    decays = jnp.exp(jnp.where(causal, gap_matrix, -1e+30))
    inner_cb = jnp.einsum('stn,sun->stu', c_proj, b_proj, precision=HIGHEST)
    mixing = inner_cb[..., None] * decays
    outputs = jnp.einsum('stuh,suhp->sthp', mixing, dt_x, precision=HIGHEST)
    final_cum = cumulative[:, -1]
    tail_decay = jnp.exp(final_cum[:, None, :] - cumulative)
    end_state = jnp.einsum('suhp,sun->shpn', dt_x * tail_decay[..., None], b_proj, precision=HIGHEST)
    return (outputs, end_state)

def inter_term(c_proj, cumulative, carried):
    return jnp.einsum('stn,shpn->sthp', c_proj, carried, precision=HIGHEST) * jnp.exp(cumulative)[..., None]

def scan_states(dt_x, b_proj, c_proj, log_decay):
    sequence_count, sequence_length = (dt_x.shape[0], dt_x.shape[1])
    span_length = min(64, sequence_length)
    block_list = sequence_length // span_length

    def to_blocks(source):
        return source.reshape((sequence_count, block_list, span_length) + source.shape[2:]).swapaxes(0, 1)

    @jax.checkpoint
    def one_block(carried, block_parts):
        dt_block, b_block, c_block, decay_block = block_parts
        cumulative = jnp.cumsum(decay_block, axis=1)
        inner_out, end_state = intra_terms(dt_block, b_block, c_block, cumulative)
        outputs = inner_out + inter_term(c_block, cumulative, carried)
        return (carried * jnp.exp(cumulative[:, -1])[:, :, None, None] + end_state, outputs)
    start_state = jnp.zeros((sequence_count, SH, P_SIZE, N), jnp.float32)
    final_state, outputs = lax.scan(one_block, start_state, (to_blocks(dt_x), to_blocks(b_proj), to_blocks(c_proj), to_blocks(log_decay)))
    return outputs.swapaxes(0, 1).reshape((sequence_count, sequence_length) + dt_x.shape[2:])

def attend(query_rows, key_row_block, value_row_block):
    sequence_count, sequence_length = (query_rows.shape[0], query_rows.shape[1])
    span_length = min(512, sequence_length)
    group_count = QUERY_HEADS // KEY_VALUE_HEADS
    block_list = sequence_length // span_length
    query_block_list = query_rows.reshape(sequence_count, block_list, span_length, KEY_VALUE_HEADS, group_count, HEAD_SIZE).transpose(1, 0, 2, 3, 4, 5)
    complete_keys = key_row_block.reshape(sequence_count, sequence_length, KEY_VALUE_HEADS, HEAD_SIZE)
    complete_values = value_row_block.reshape(sequence_count, sequence_length, KEY_VALUE_HEADS, HEAD_SIZE)
    starts = jnp.arange(block_list, dtype=jnp.int32) * span_length
    key_place = jnp.arange(sequence_length, dtype=jnp.int32)

    @jax.checkpoint
    def one_block(block_parts):
        q_block, row_start = block_parts
        scores = low_back(jnp.einsum('sigrd,sjgd->sgrij', q_block, complete_keys, precision=HIGHEST) * HEAD_SIZE ** (-0.5))
        rows_here = row_start + jnp.arange(span_length, dtype=jnp.int32)
        scores = jnp.where(rows_here[:, None] >= key_place[None, :], scores, -1e+30)
        probability = low(jax.nn.softmax(scores, axis=-1))
        return jnp.einsum('sgrij,sjgd->sigrd', probability, complete_values, precision=HIGHEST)
    gathered = lax.map(one_block, (query_block_list, starts))
    return gathered.transpose(1, 0, 2, 3, 4, 5).reshape(sequence_count, sequence_length, QUERY_HEADS * HEAD_SIZE)

def layer(hidden, weights, heads_row):
    norm_gains, w_qkv, w_attn, w_in, w_dt, conv_params, w_out, w_gate_up, w_down = weights
    token_positions = jnp.arange(hidden.shape[1], dtype=jnp.int32)
    normed = low(rms_scale(hidden, norm_gains[0]))
    query_key_value = low_back(jnp.dot(normed, w_qkv, precision=HIGHEST))
    query_rows, key_row_block, value_row_block = project_heads(query_key_value, token_positions)
    attended = attend(low(query_rows), low(key_row_block), low(value_row_block))
    attended = low(low_back(attended))
    branch_attn = low_back(jnp.dot(attended, w_attn, precision=HIGHEST))
    mixed = low(low_back(jnp.dot(normed, w_in, precision=HIGHEST)))
    gate_z = mixed[..., :DSSM]
    padded = jnp.pad(mixed[..., DSSM:], ((0, 0), (CONV - 1, 0), (0, 0)))
    dt_raw = low_back(jnp.dot(normed, w_dt, precision=HIGHEST))
    conv_out = convolve(padded, conv_params)
    inputs_x, dt_x, b_proj, c_proj, log_decay = ssd_inputs(conv_out, dt_raw, heads_row)
    state_out = scan_states(dt_x, b_proj, c_proj, log_decay) + heads_row[2][:, None] * inputs_x
    gated = state_out.reshape(gate_z.shape) * jax.nn.silu(gate_z)
    branch_ssm = low_back(jnp.dot(low(gated), w_out, precision=HIGHEST))
    middle = hidden + branch_attn + branch_ssm
    normed_two = low(rms_scale(middle, norm_gains[1]))
    gate_up = low_back(jnp.dot(normed_two, w_gate_up, precision=HIGHEST))
    activated = low(jax.nn.silu(gate_up[..., :FF]) * gate_up[..., FF:])
    return middle + low_back(jnp.dot(activated, w_down, precision=HIGHEST))

def reference(boundary, lengths, norm_gains, w_qkv, w_attn, w_in, w_dt, conv_params, head_params, w_out, w_gate_up, w_down):
    inputs = boundary[0].astype(jnp.float32)
    cotangent = boundary[1].astype(jnp.float32)
    live_mask = (jnp.arange(inputs.shape[1], dtype=jnp.int32)[None, :] < lengths[:, None]).astype(jnp.float32)
    params = tuple((member.astype(jnp.float32) for member in (norm_gains, w_qkv, w_attn, w_in, w_dt, conv_params, w_out, w_gate_up, w_down)))
    heads_all = head_params.astype(jnp.float32)

    def forward(inputs, params, heads_all):
        hidden = layer(inputs, [member[0] for member in params], heads_all[0])
        hidden = low_back(low(hidden))
        return layer(hidden, [member[1] for member in params], heads_all[1])
    result, pull = jax.vjp(forward, inputs, params, heads_all)
    grad_inputs, weight_grads, grad_heads = pull(cotangent * live_mask[..., None])
    ends = jnp.stack([grad_inputs, result])
    return (ends,) + tuple(weight_grads[:6]) + (grad_heads,) + tuple(weight_grads[6:])
```

```python
from functools import partial
from math import isqrt

import jax
import jax.numpy as jnp
from jax import lax
from jax.sharding import PartitionSpec as P

D = 1024
HEAD_SIZE = 64
SH = 24
P_SIZE = 64
N = 128
CONV = 4
QH = 4
HEADS = SH // 2
QW = QH * HEAD_SIZE
DI = HEADS * P_SIZE
FFH = 1024
HALF = D // 2

eps = 1e-05
ROPE_BASE = 100000000000.0
HIGHEST = lax.Precision.HIGHEST
BF = jnp.bfloat16
F32 = jnp.float32

Z_Y_X = (0, 1, 2)
Z_X_Y = (0, 2, 1)


def grid_of(count):
    side = isqrt(count // 4)
    return (count // (side * side), side, side)


def place_on(axis):
    dims = grid_of(lax.axis_size("seq"))
    strides = (dims[1] * dims[2], dims[2], 1)
    return lax.axis_index("seq") // strides[axis] % dims[axis], dims[axis], strides[axis]


def hop(value, axis, moves):
    count = lax.axis_size("seq")
    _, length, stride = place_on(axis)
    pairs = []
    for source in range(count):
        at = source // stride % length
        if at in moves:
            pairs.append((source, source + (moves[at] - at) * stride))
    return lax.ppermute(value, "seq", pairs)


NEXT = {0: 1, 1: 0, 2: 3, 3: 2}
INNER = {1: 2, 2: 1}
OUTWARD = {1: 0, 2: 3}
INWARD = {0: 1, 3: 2}


def swap(value):
    return lax.ppermute(value, "section", [(0, 1), (1, 0)])


def both_cores(value):
    return value + swap(value)


def line_gather(part, axis):
    at, length, _ = place_on(axis)
    if length == 1:
        return part[None]
    got = hop(part, axis, {k: v for k, v in NEXT.items() if k < length})
    even = at % 2 == 0
    pair = jnp.stack([jnp.where(even, part, got), jnp.where(even, got, part)])
    if length == 2:
        return pair
    over = hop(pair, axis, INNER)
    rest = hop(over, axis, OUTWARD)
    far = jnp.where((at == 1) | (at == 2), over, rest)
    return jnp.concatenate([jnp.where(at < 2, pair, far), jnp.where(at < 2, far, pair)])


def gather(part, order):
    shape = part.shape
    held = []
    for axis in order:
        part = line_gather(part, axis)
        part = jnp.moveaxis(part, 0, sum(1 for other in held if other < axis))
        held = held + [axis]
    return part.reshape((-1,) + shape)


def line_reduce(parts, axis, dim, last):
    at, length, _ = place_on(axis)
    if length == 1:
        return jnp.squeeze(parts, dim)

    def pick(array, index):
        return lax.dynamic_index_in_dim(array, index, dim, False)

    def add(a, b, kind):
        return (a.astype(F32) + b.astype(F32)).astype(kind)

    if length == 4:
        halves = parts.reshape(parts.shape[:dim] + (2, 2) + parts.shape[dim + 1 :])
        far, near = pick(halves, 1 - at // 2), pick(halves, at // 2)
        far = add(far, hop(far, axis, INWARD), BF)
        parts = add(near, hop(far, axis, INNER), BF)
    got = hop(pick(parts, 1 - at % 2), axis, {k: v for k, v in NEXT.items() if k < length})
    return add(pick(parts, at % 2), got, F32 if last else BF)


def reduce_to_owner(whole, order):
    count = lax.axis_size("seq")
    shape = whole.shape[1:]
    part = whole.reshape(grid_of(count) + shape)
    held = [0, 1, 2]
    for axis in reversed(order):
        part = line_reduce(part, axis, held.index(axis), len(held) == 1)
        held.remove(axis)
    return part


def to_all(blocks):
    return lax.all_to_all(blocks, "seq", 0, 0, tiled=True)


def rms_scale(hidden, gain):
    return hidden * lax.rsqrt(jnp.mean(hidden * hidden, axis=-1, keepdims=True) + eps) * gain


def rotation_tables(positions, heads):
    half = HEAD_SIZE // 2
    frequency = ROPE_BASE ** (-jnp.arange(half, dtype=F32) / half)
    angles = positions.astype(F32)[:, None] * frequency[None, :]
    cosine, sine = jnp.cos(angles), jnp.sin(angles)
    return (
        jnp.tile(jnp.concatenate([cosine, cosine], axis=1), (1, heads)),
        jnp.tile(jnp.concatenate([-sine, sine], axis=1), (1, heads)),
    )


def rotate(rows, tables):
    cosine, sine = tables
    width = rows.shape[-1]
    half = HEAD_SIZE // 2
    low = (jnp.arange(width) // half) % 2 == 0
    swapped = jnp.where(low, jnp.roll(rows, -half, axis=-1), jnp.roll(rows, half, axis=-1))
    return rows * cosine[:, :width] + swapped * sine[:, :width]


def rotate_back(rows, tables):
    cosine, sine = tables
    return rotate(rows, (cosine, -sine))


def convolve(extended, taps):
    span = extended.shape[1] - (CONV - 1)
    summed = taps[CONV]
    for offset in range(CONV):
        summed = summed + taps[offset] * extended[:, offset : offset + span]
    return jax.nn.silu(summed)


def ssd_inputs(conv_out, dt_raw, heads_row):
    lead = conv_out.shape[:2]
    inputs_x = conv_out[..., :DI].reshape(lead + (HEADS, P_SIZE))
    b_proj = conv_out[..., DI : DI + N]
    c_proj = conv_out[..., DI + N :]
    step_size = jax.nn.softplus(dt_raw + heads_row[0])
    log_decay = -step_size * jnp.exp(heads_row[1])
    return (inputs_x, inputs_x * step_size[..., None], b_proj, c_proj, log_decay)


def intra_terms(dt_x, b_proj, c_proj, cumulative):
    block_len = cumulative.shape[1]
    position = jnp.arange(block_len, dtype=jnp.int32)
    causal = (position[:, None] >= position[None, :])[None, None]
    by_head = cumulative.swapaxes(1, 2)
    gap_matrix = by_head[:, :, :, None] - by_head[:, :, None, :]
    decays = jnp.exp(jnp.where(causal, gap_matrix, -1e30))
    inner_cb = jnp.einsum("stn,sun->stu", c_proj, b_proj, precision=HIGHEST)
    mixing = inner_cb[:, None] * decays
    outputs = jnp.einsum("shtu,suhp->sthp", mixing, dt_x, precision=HIGHEST)
    tail_decay = jnp.exp(cumulative[:, -1][:, None, :] - cumulative)
    end_state = jnp.einsum(
        "suhp,sun->shpn", dt_x * tail_decay[..., None], b_proj, precision=HIGHEST
    )
    return (outputs, end_state)


def inter_term(c_proj, cumulative, carried):
    return (
        jnp.einsum("stn,shpn->sthp", c_proj, carried, precision=HIGHEST)
        * jnp.exp(cumulative)[..., None]
    )


def mixer(conv_out, dt_raw, heads_row, carried):
    inputs_x, dt_x, b_proj, c_proj, log_decay = ssd_inputs(conv_out, dt_raw, heads_row)
    cumulative = jnp.cumsum(log_decay, axis=1)
    inner_out, end_state = intra_terms(dt_x, b_proj, c_proj, cumulative)
    state_out = (
        inner_out + inter_term(c_proj, cumulative, carried) + heads_row[2][:, None] * inputs_x
    )
    return (state_out, end_state, jnp.exp(cumulative[:, -1]))


def gate_state(values, gate_z):
    return values * jax.nn.silu(gate_z)


def swiglu(gate_up):
    return jax.nn.silu(gate_up[..., :FFH]) * gate_up[..., FFH:]


def mat_mul(operand, weight):
    return jnp.dot(operand, weight, preferred_element_type=F32)


def back_dot(grad_rows, weight):
    return lax.dot_general(grad_rows, weight, (((1,), (1,)), ((), ())), preferred_element_type=F32)


def weight_grad(operand, grad_rows):
    return lax.dot_general(
        operand, grad_rows, (((0,), (0,)), ((), ())), preferred_element_type=F32
    ).astype(BF)


def score_rows(queries, keys, positions):
    scores = jnp.einsum(
        "sihd,sjd->shij", queries, keys, preferred_element_type=F32
    ) * HEAD_SIZE ** (-0.5)
    allowed = positions[:, None] >= jnp.arange(keys.shape[1], dtype=jnp.int32)[None, :]
    return jnp.where(allowed, scores, -1e30)


def attend_forward(queries, keys, values, positions):
    scores = score_rows(queries, keys, positions)
    row_max = jnp.max(scores, axis=-1, keepdims=True)
    shifted = jnp.exp(scores - row_max)
    row_total = jnp.sum(shifted, axis=-1, keepdims=True)
    probability = (shifted / row_total).astype(BF)
    output = jnp.einsum("shij,sjd->sihd", probability, values, preferred_element_type=F32)
    return output, row_max + jnp.log(row_total)


def attend_backward(queries, keys, values, log_total, gradient, positions):
    probability = jnp.exp(score_rows(queries, keys, positions) - log_total)
    value_gradient = jnp.einsum(
        "shij,sihd->sjd", probability.astype(BF), gradient, preferred_element_type=F32
    )
    grad_probs = jnp.einsum("sihd,sjd->shij", gradient, values, preferred_element_type=F32)
    row_inner = jnp.sum(probability * grad_probs, axis=-1, keepdims=True)
    grad_scores = (probability * (grad_probs - row_inner)).astype(BF)
    scale = HEAD_SIZE ** (-0.5)
    grad_queries = (
        jnp.einsum("shij,sjd->sihd", grad_scores, keys, preferred_element_type=F32) * scale
    )
    key_gradient = (
        jnp.einsum("shij,sihd->sjd", grad_scores, queries, preferred_element_type=F32) * scale
    )
    return grad_queries, jnp.concatenate([key_gradient, value_gradient], axis=-1)


def state_rows(count):
    return 2 * HEADS * P_SIZE // count


def exchange_states(states, log_total):
    count = lax.axis_size("seq")
    rows = state_rows(count)
    blocks = states.astype(BF).reshape(count, rows, N)
    high = lax.reduce_precision(log_total, 8, 7)
    middle = lax.reduce_precision(log_total - high, 8, 7)
    low = log_total - high - middle
    logs = jnp.stack([high, middle, low]).reshape(-1)
    logs = jnp.pad(logs, (0, N - logs.shape[0])).astype(BF)
    logs = jnp.broadcast_to(logs, (count, 16, N))
    arrived = to_all(jnp.concatenate([blocks, logs], axis=1))
    decays = arrived[:, rows, : 6 * HEADS].astype(F32).reshape(count, 3, 2 * HEADS)
    return arrived[:, :rows], jnp.sum(decays, axis=1)


def chain_weights(decays):
    count = lax.axis_size("seq")
    rows = state_rows(count)
    here = lax.axis_index("seq")
    chips = jnp.arange(count)
    between = (chips[None, None, :] > chips[None, :, None]) & (
        chips[None, None, :] < chips[:, None, None]
    )
    logs = jnp.einsum("ijk,kh->ijh", between.astype(F32), decays, precision=HIGHEST)
    per_row = jnp.repeat(logs, P_SIZE, axis=2)
    logs = lax.dynamic_slice_in_dim(per_row, here * rows, rows, 2)
    earlier = (chips[:, None] > chips[None, :])[:, :, None]
    return jnp.where(earlier, jnp.exp(logs), 0.0)


def return_states(weights, blocks):
    mixed = jnp.sum(weights[..., None] * blocks.astype(F32)[None], axis=1)
    return to_all(mixed.astype(BF)).reshape(2, HEADS, P_SIZE, N).astype(F32)


def chip_order(att, out, count):
    lead = att.shape[0]
    half = count // 2
    both = jnp.concatenate([att.reshape(lead, half, -1), out.reshape(lead, half, -1)], axis=2)
    return both.reshape(lead, -1)


def chip_order_back(both, count):
    lead = both.shape[0]
    half = count // 2
    parts = both.reshape(lead, half, -1)
    width = QW // half
    return parts[:, :, :width].reshape(lead, -1), parts[:, :, width:].reshape(lead, -1)


def side_dot(rows, pair, core):
    own, other = mat_mul(rows, pair[0]), mat_mul(rows, pair[1])
    return jnp.concatenate(
        [jnp.where(core == 0, own, other), jnp.where(core == 0, other, own)], axis=1
    )


def side_back(rows, pair, core):
    first, second = rows[:, :HALF], rows[:, HALF:]
    own, other = jnp.where(core == 0, first, second), jnp.where(core == 0, second, first)
    return back_dot(own, pair[0]) + back_dot(other, pair[1])


def layer_forward(hidden, weights, gains, taps, heads_row, tables, positions):
    w_rest, w_z, w_xs, w_mix, w_gu, w_down = weights
    core = lax.axis_index("section")
    here = lax.axis_index("seq")
    count = lax.axis_size("seq")
    rows = hidden.shape[0]
    span = rows // 2
    normed = rms_scale(hidden, gains[0]).astype(BF)
    rest = mat_mul(normed, w_rest)
    queries = rotate(rest[:, :QW], tables).astype(BF)
    keys = rotate(rest[:, QW : QW + HEAD_SIZE], tables).astype(BF)
    kv = jnp.concatenate([keys, rest[:, QW + HEAD_SIZE : QW + 2 * HEAD_SIZE].astype(BF)], axis=1)
    kv = kv.reshape(2, span, 2 * HEAD_SIZE)
    all_kv = to_all(jnp.broadcast_to(kv[None], (count,) + kv.shape))
    all_kv = all_kv.swapaxes(0, 1).reshape(2, count * span, 2 * HEAD_SIZE)
    bc_at = QW + 2 * HEAD_SIZE
    raw = jnp.concatenate(
        [mat_mul(normed, w_xs).astype(BF), rest[:, bc_at : bc_at + 2 * N].astype(BF)], axis=1
    ).reshape(2, span, DI + 2 * N)
    gate_z = mat_mul(normed, w_z).astype(BF)
    dt_raw = rest[:, bc_at + 2 * N : bc_at + 2 * N + HEADS].reshape(2, span, HEADS)
    edge = lax.ppermute(
        raw[:, span - (CONV - 1) :], "seq", [(k, k + 1) for k in range(count - 1)]
    )
    extended = jnp.concatenate([edge, raw], axis=1)
    conv_out = convolve(extended.astype(F32), taps)
    inputs_x, dt_x, b_proj, c_proj, log_decay = ssd_inputs(conv_out, dt_raw, heads_row)
    cumulative = jnp.cumsum(log_decay, axis=1)
    inner_out, end_state = intra_terms(dt_x, b_proj, c_proj, cumulative)
    blocks, decays = exchange_states(end_state, cumulative[:, -1])
    chain = chain_weights(decays)
    carried = return_states(chain, blocks)
    attended, log_total = attend_forward(
        queries.reshape(2, span, QH, HEAD_SIZE),
        all_kv[..., :HEAD_SIZE],
        all_kv[..., HEAD_SIZE:],
        positions,
    )
    attended = attended.astype(BF).reshape(rows, QW)
    state_out = (
        inner_out + inter_term(c_proj, cumulative, carried) + heads_row[2][:, None] * inputs_x
    ).reshape(rows, DI)
    gated = gate_state(state_out, gate_z.astype(F32)).astype(BF)
    mix_in = chip_order(attended, gated, count)
    middle = hidden + both_cores(side_dot(mix_in, w_mix, core))
    normed_two = rms_scale(middle, gains[1]).astype(BF)
    gate_up = mat_mul(normed_two, w_gu)
    activated = swiglu(gate_up).astype(BF)
    result = middle + both_cores(side_dot(activated, w_down, core))
    kept = (
        hidden, normed, queries, all_kv, log_total, extended, conv_out, dt_raw, chain, carried,
        state_out, gate_z, mix_in, middle, normed_two, gate_up, activated,
    )
    return result, kept


def layer_backward(grad_result, kept, weights, gains, taps, heads_row, tables, positions, send):
    (
        hidden, normed, queries, all_kv, log_total, extended, conv_out, dt_raw, chain, carried,
        state_out, gate_z, mix_in, middle, normed_two, gate_up, activated,
    ) = kept
    w_rest, w_z, w_xs, w_mix, w_gu, w_down = weights
    core = lax.axis_index("section")
    here = lax.axis_index("seq")
    count = lax.axis_size("seq")
    rows = hidden.shape[0]
    span = rows // 2
    grads = {}
    grad_low = grad_result.astype(BF)
    grads["down"] = send["down"](weight_grad(activated, grad_low))
    grad_activated = side_back(grad_low, w_down, core)
    grad_gu = jax.vjp(swiglu, gate_up)[1](grad_activated)[0].astype(BF)
    grads["gu"] = send["gu"](weight_grad(normed_two, grad_gu))
    grad_normed = both_cores(back_dot(grad_gu, w_gu))
    grad_norm, grad_gain_two = jax.vjp(rms_scale, middle, gains[1])[1](grad_normed)
    grad_middle = grad_result + grad_norm
    branch_low = grad_middle.astype(BF)
    grad_att, grad_gated = chip_order_back(side_back(branch_low, w_mix, core), count)
    grads["mix"] = send["mix"](weight_grad(mix_in, branch_low))
    grad_state, grad_z = jax.vjp(gate_state, state_out, gate_z.astype(F32))[1](grad_gated)
    grad_z = grad_z.astype(BF)
    grads["z"] = send["z"](weight_grad(normed, grad_z))
    grad_state = grad_state.reshape(2, span, HEADS, P_SIZE)
    inputs_x, dt_x, b_proj, c_proj, log_decay = ssd_inputs(conv_out, dt_raw, heads_row)
    cumulative = jnp.cumsum(log_decay, axis=1)
    local_in = jnp.einsum(
        "sthp,stn->shpn", grad_state * jnp.exp(cumulative)[..., None], c_proj, precision=HIGHEST
    )
    blocks = to_all(local_in.astype(BF).reshape(count, state_rows(count), N))
    later = return_states(chain.swapaxes(0, 1), blocks)
    grad_decay = jnp.sum(later * carried, axis=(2, 3))
    grad_q, grad_kv = attend_backward(
        queries.reshape(2, span, QH, HEAD_SIZE),
        all_kv[..., :HEAD_SIZE],
        all_kv[..., HEAD_SIZE:],
        log_total,
        grad_att.astype(BF).reshape(2, span, QH, HEAD_SIZE),
        positions,
    )
    grad_kv = grad_kv.astype(BF).reshape(2, count, span, 2 * HEAD_SIZE).swapaxes(0, 1)
    grad_kv = jnp.sum(to_all(grad_kv).astype(F32), axis=0).reshape(rows, 2 * HEAD_SIZE)
    grad_conv_out, grad_dt, grad_heads = jax.vjp(
        partial(mixer, carried=carried), conv_out, dt_raw, heads_row
    )[1]((grad_state, later, grad_decay))
    grad_extended, grad_taps = jax.vjp(convolve, extended.astype(F32), taps)[1](grad_conv_out)
    edge = lax.ppermute(
        grad_extended[:, : CONV - 1].astype(BF), "seq", [(k + 1, k) for k in range(count - 1)]
    ).astype(F32)
    body = grad_extended[:, CONV - 1 :]
    cut = span - (CONV - 1)
    grad_raw = jnp.concatenate([body[:, :cut], body[:, cut:] + edge], axis=1)
    grad_raw = grad_raw.astype(BF).reshape(rows, DI + 2 * N)
    grad_xs = grad_raw[:, :DI]
    grads["xs"] = send["xs"](weight_grad(normed, grad_xs))
    grad_dt = jnp.pad(grad_dt.astype(BF).reshape(rows, HEADS), ((0, 0), (0, N - HEADS)))
    grad_rest = jnp.concatenate(
        [
            rotate_back(grad_q.reshape(rows, QW), tables).astype(BF),
            rotate_back(grad_kv[:, :HEAD_SIZE], tables).astype(BF),
            grad_kv[:, HEAD_SIZE:].astype(BF),
            grad_raw[:, DI:],
            grad_dt,
        ],
        axis=1,
    )
    grads["rest"] = send["rest"](weight_grad(normed, grad_rest))
    grad_normed = both_cores(
        back_dot(grad_rest, w_rest) + back_dot(grad_z, w_z) + back_dot(grad_xs, w_xs)
    )
    grad_norm, grad_gain_one = jax.vjp(rms_scale, hidden, gains[0])[1](grad_normed)
    return (
        grad_middle + grad_norm,
        grads,
        (jnp.stack([grad_gain_one, grad_gain_two]), grad_taps, grad_heads),
    )


def halves(array, sizes, at):
    out = []
    for core in (0, 1):
        parts, start = [], at
        for width in sizes:
            half = width // 2
            parts.append(array[:, start + core * half : start + (core + 1) * half])
            start += width
        out.append(parts)
    return out


ORDERS = (
    {"rest": Z_Y_X, "z": Z_X_Y, "xs": Z_Y_X, "mix": Z_X_Y, "gu": Z_Y_X, "down": Z_X_Y},
    {"rest": Z_X_Y, "z": Z_Y_X, "xs": Z_X_Y, "mix": Z_Y_X, "gu": Z_X_Y, "down": Z_Y_X},
)
BACK = {"rest": Z_Y_X, "z": Z_Y_X, "xs": Z_X_Y, "mix": Z_X_Y, "gu": Z_Y_X, "down": Z_X_Y}
NAMES = ("rest", "z", "xs", "mix", "gu", "down")


def per_device(
    boundary, lengths, norm_gains, w_qkv, w_attn, w_in, w_dt, conv_params, head_params, w_out, w_gate_up, w_down,
):
    core = lax.axis_index("section")
    here = lax.axis_index("seq")
    count = lax.axis_size("seq")
    first = core == 0
    span = boundary.shape[2]
    rows = 2 * span

    qkv = halves(w_qkv[0], (QW * 2, 2 * HEAD_SIZE, 2 * HEAD_SIZE), 0)
    into = halves(w_in[0], (2 * DI, 2 * DI), 0)
    both_bc = w_in[0][:, 4 * DI :]
    steps = halves(w_dt[0], (SH,), 0)
    ups = halves(w_gate_up[0], (2 * FFH, 2 * FFH), 0)
    mix = jnp.concatenate([w_attn[0], w_out[0]], axis=0)
    cut = []
    for k in (0, 1):
        step = jnp.pad(steps[k][0], ((0, 0), (0, N - HEADS)))
        cut.append(
            {
                "rest": jnp.concatenate(qkv[k] + [both_bc, step], axis=1),
                "z": into[k][0],
                "xs": into[k][1],
                "mix": mix[:, k * HALF : (k + 1) * HALF],
                "gu": jnp.concatenate(ups[k], axis=1),
                "down": w_down[0][:, k * HALF : (k + 1) * HALF],
            }
        )
    layers = ({}, {})
    for name in NAMES:
        own = jnp.where(first, cut[0][name], cut[1][name])
        got = swap(jnp.where(first, cut[1][name], cut[0][name]))
        layers[0][name] = jnp.where(first, own, got)
        layers[1][name] = jnp.where(first, got, own)

    small = jnp.concatenate([norm_gains[0].reshape(-1), conv_params[0].reshape(-1)])
    small = lax.all_gather(small, ("section", "seq"), axis=0).reshape(2, count, -1).astype(F32)
    width = norm_gains.shape[2]
    gains = small[:, :, : 2 * width].reshape(2, count, 2, width).swapaxes(1, 2).reshape(2, 2, D)
    taps = small[:, :, 2 * width :].reshape(2, count, CONV + 1, -1).swapaxes(1, 2)
    taps = taps.reshape(2, CONV + 1, 4 * DI // 2 + 2 * N)
    taps = jnp.concatenate(
        [jnp.where(first, taps[..., :DI], taps[..., DI : 2 * DI]), taps[..., 2 * DI :]], axis=-1
    )
    heads_other = swap(head_params[0])
    heads = jnp.stack(
        [
            jnp.where(first, head_params[0], heads_other),
            jnp.where(first, heads_other, head_params[0]),
        ]
    )
    heads = jnp.where(first, heads[..., :HEADS], heads[..., HEADS:])

    other = swap(boundary[0])
    inputs = jnp.where(first, boundary[0], other).reshape(rows, D).astype(F32)
    positions = here * span + jnp.arange(span, dtype=jnp.int32)
    live = (positions[None, :] < lengths[:, None]).astype(F32)
    cotangent = jnp.where(first, other, boundary[0]).astype(F32) * live[..., None]
    cotangent = cotangent.reshape(rows, D)
    tables = tuple(jnp.tile(t, (2, 1)) for t in rotation_tables(positions, QH))

    def collect(layer):
        held = []
        for name in NAMES:
            whole = gather(layers[layer][name], ORDERS[layer][name])
            if name in ("mix", "down"):
                blocks = whole.reshape((2, count // 2) + whole.shape[1:])
                keep = lax.dynamic_index_in_dim(blocks, core, 0, False)
                away = lax.dynamic_index_in_dim(blocks, 1 - core, 0, False)
                held.append(
                    (keep.reshape(-1, HALF), swap(away).reshape(-1, HALF))
                )
            else:
                held.append(whole.reshape(D, -1))
        return held

    def columns_home(whole):
        blocks = whole.reshape(count // 2, -1, D)
        left, right = blocks[..., :HALF], blocks[..., HALF:]
        keep = jnp.where(first, left, right)
        got = swap(jnp.where(first, right, left))
        return jnp.concatenate([jnp.where(first, keep, got), jnp.where(first, got, keep)], axis=0)

    send = {}
    for name in NAMES:
        if name in ("mix", "down"):
            send[name] = lambda g, name=name: reduce_to_owner(columns_home(g), BACK[name])
        else:
            send[name] = lambda g, name=name: reduce_to_owner(
                g.reshape(count, D // count, -1), BACK[name]
            )

    weights = (collect(0), collect(1))
    middle, kept_0 = layer_forward(
        inputs, weights[0], gains[0], taps[0], heads[0], tables, positions
    )
    handed = middle.astype(BF).astype(F32)
    result, kept_1 = layer_forward(
        handed, weights[1], gains[1], taps[1], heads[1], tables, positions
    )
    grad_handed, grads_1, small_1 = layer_backward(
        cotangent, kept_1, weights[1], gains[1], taps[1], heads[1], tables, positions, send
    )
    grad_inputs, grads_0, small_0 = layer_backward(
        grad_handed.astype(BF).astype(F32),
        kept_0, weights[0], gains[0], taps[0], heads[0], tables, positions, send,
    )

    shares = {}
    for name in NAMES:
        to_second = lax.ppermute(grads_1[name].astype(BF), "section", [(0, 1)])
        to_first = lax.ppermute(grads_0[name].astype(BF), "section", [(1, 0)])
        own = jnp.where(first, grads_0[name], grads_1[name])
        got = jnp.where(first, to_first, to_second).astype(F32)
        shares[name] = (jnp.where(first, own, got), jnp.where(first, got, own))

    def joined(name, start, width):
        return [half[:, start : start + width] for half in shares[name]]

    rest = shares["rest"]
    bc_at = QW + 2 * HEAD_SIZE
    dt_at = bc_at + 2 * N
    grad_qkv = jnp.concatenate(
        joined("rest", 0, QW) + joined("rest", QW, HEAD_SIZE)
        + joined("rest", QW + HEAD_SIZE, HEAD_SIZE), axis=1,
    )
    grad_in = jnp.concatenate(
        list(shares["z"]) + list(shares["xs"])
        + [rest[0][:, bc_at:dt_at] + rest[1][:, bc_at:dt_at]], axis=1,
    )
    grad_dt = jnp.concatenate(joined("rest", dt_at, HEADS), axis=1)
    grad_mix = jnp.concatenate(shares["mix"], axis=1)
    attn_rows = w_attn.shape[1]
    grad_gu = jnp.concatenate(joined("gu", 0, FFH) + joined("gu", FFH, FFH), axis=1)
    grad_down = jnp.concatenate(shares["down"], axis=1)

    def small_sum(parts):
        grad_gains, grad_taps, grad_heads = parts
        zeros = jnp.zeros((CONV + 1, DI), F32)
        xs_part = grad_taps[:, :DI]
        wide = jnp.concatenate(
            [jnp.where(first, xs_part, zeros), jnp.where(first, zeros, xs_part), grad_taps[:, DI:]],
            axis=1,
        )
        none = jnp.zeros((3, HEADS), F32)
        head_wide = jnp.concatenate(
            [jnp.where(first, grad_heads, none), jnp.where(first, none, grad_heads)], axis=1
        )
        gains_once = jnp.where(first, grad_gains, 0.0)
        flat = jnp.concatenate([gains_once.reshape(-1), wide.reshape(-1), head_wide.reshape(-1)])
        return lax.psum(flat, ("section", "seq"))

    flat_1 = small_sum(small_1)
    flat_0 = small_sum(small_0)
    flat = jnp.where(first, flat_0, flat_1)
    conv_width = conv_params.shape[2]
    total_gains = flat[: 2 * D].reshape(2, D)
    total_taps = flat[2 * D : 2 * D + (CONV + 1) * (2 * DI + 2 * N)].reshape(CONV + 1, -1)
    total_heads = flat[2 * D + (CONV + 1) * (2 * DI + 2 * N) :].reshape(3, SH)
    grad_gains = lax.dynamic_slice_in_dim(total_gains, here * width, width, 1)
    grad_conv = lax.dynamic_slice_in_dim(total_taps, here * conv_width, conv_width, 1)

    ends = jnp.where(first, grad_inputs, result).reshape(2, span, D)
    outs = (
        ends, grad_gains, grad_qkv, grad_mix[:attn_rows], grad_in, grad_dt, grad_conv,
        total_heads, grad_mix[attn_rows:], grad_gu, grad_down,
    )
    return tuple(out[None] for out in outs)


def solution(mesh):
    by_rows = P("section", "seq", None)
    by_columns = P("section", None, "seq")
    whole = P("section", None, None)
    ends = P("section", None, "seq", None)
    in_specs = (
        ends, P(), by_columns, by_rows, by_rows, by_rows, by_rows, by_columns, whole, by_rows,
        by_rows, by_rows,
    )
    out_specs = (
        ends, by_columns, by_rows, by_rows, by_rows, by_rows, by_columns, whole, by_rows, by_rows,
        by_rows,
    )
    return jax.shard_map(
        per_device, mesh=mesh, in_specs=in_specs, out_specs=out_specs, check_vma=False
    )
```

```python
from functools import partial
from math import isqrt

import jax
import jax.numpy as jnp
from jax import lax
from jax.experimental import pallas as pl
from jax.experimental.pallas import tpu as pltpu
from jax.sharding import PartitionSpec as P

D = 1024
HEAD_SIZE = 64
SH = 24
P_SIZE = 64
N = 128
CONV = 4
QH = 4
HEADS = SH // 2
QW = QH * HEAD_SIZE
DI = HEADS * P_SIZE
FFH = 1024
HALF = D // 2
REST = QW + 2 * HEAD_SIZE + 2 * N + N

eps = 1e-05
ROPE_BASE = 100000000000.0
HIGHEST = lax.Precision.HIGHEST
BF = jnp.bfloat16
F32 = jnp.float32
VMEM_BYTES = 56 * 2**20


def grid_of(count):
    side = isqrt(count // 4)
    return (count // (side * side), side, side)


def place_on(axis):
    dims = grid_of(lax.axis_size("seq"))
    strides = (dims[1] * dims[2], dims[2], 1)
    return lax.axis_index("seq") // strides[axis] % dims[axis], dims[axis], strides[axis]


def hop(value, axis, moves):
    count = lax.axis_size("seq")
    _, length, stride = place_on(axis)
    pairs = []
    for source in range(count):
        at = source // stride % length
        if at in moves and moves[at] < length:
            pairs.append((source, source + (moves[at] - at) * stride))
    return lax.ppermute(value, "seq", pairs)


NEXT = {0: 1, 1: 0, 2: 3, 3: 2}
INNER = {1: 2, 2: 1}
OUTWARD = {1: 0, 2: 3}
INWARD = {0: 1, 3: 2}


def swap(value):
    return lax.ppermute(value, "section", [(0, 1), (1, 0)])


def both_cores(value):
    return value + swap(value)


def after(values, others):
    if not others:
        return values
    return list(lax.optimization_barrier((tuple(values), tuple(others)))[0])


def line_gather(part, axis, dim):
    at, length, _ = place_on(axis)
    got = hop(part, axis, NEXT)
    even = at % 2 == 0
    pair = jnp.stack([jnp.where(even, part, got), jnp.where(even, got, part)], axis=dim)
    if length == 2:
        return pair
    over = hop(pair, axis, INNER)
    rest = hop(over, axis, OUTWARD)
    far = jnp.where((at == 1) | (at == 2), over, rest)
    return jnp.concatenate(
        [jnp.where(at < 2, pair, far), jnp.where(at < 2, far, pair)], axis=dim
    )


class Gathers:
    def __init__(self, pairs):
        self.pairs = pairs
        self.along_z = [None] * len(pairs)
        self.token = []
        self.done = []
        self.half = None
        self.start_z(0, [])

    def start_z(self, at, others):
        if at < len(self.pairs) and self.along_z[at] is None:
            (stacked,) = after([jnp.stack(self.pairs[at])], others)
            whole = line_gather(stacked, 0, 0)
            self.along_z[at] = [whole[:, 0], whole[:, 1]]

    def step(self, *others):
        at = len(self.done)
        if at == len(self.pairs):
            return
        if self.half is None:
            first, second = after(self.along_z[at], self.token + list(others))
            self.start_z(at + 1, [first])
            self.half = [line_gather(first, 1, 1), line_gather(second, 2, 1)]
            self.token = [v[:, :, :1] for v in self.half]
        else:
            first, second = after(self.half, list(others))
            first, second = line_gather(first, 2, 2), line_gather(second, 1, 1)
            self.token = [v[:, :, :, :1] for v in (first, second)]
            self.half = None
            self.done.append([v.reshape((-1,) + v.shape[3:]) for v in (first, second)])

    def get(self, at):
        while len(self.done) <= at:
            self.step()
        return self.done[at]


def add(a, b, kind):
    return (a.astype(F32) + b.astype(F32)).astype(kind)


def line_reduce(parts, axis, dim):
    at, length, _ = place_on(axis)

    def pick(array, index):
        return lax.dynamic_index_in_dim(array, index, dim, False)

    if length == 4:
        halves = parts.reshape(parts.shape[:dim] + (2, 2) + parts.shape[dim + 1 :])
        far, near = pick(halves, 1 - at // 2), pick(halves, at // 2)
        far = add(far, hop(far, axis, INWARD), BF)
        parts = add(near, hop(far, axis, INNER), BF)
    got = hop(pick(parts, 1 - at % 2), axis, NEXT)
    return pick(parts, at % 2), got


def z_groups():
    count = lax.axis_size("seq")
    depth, side, _ = grid_of(count)
    plane = side * side
    return [[z * plane + k for z in range(depth)] for k in range(plane)]


class Reduces:
    def __init__(self):
        self.token = []

    def pair(self, first, second):
        dims = grid_of(lax.axis_size("seq"))
        first, second = (v.reshape(dims + v.shape[1:]) for v in (first, second))
        first, second = after([first, second], self.token)
        keep_1, got_1 = line_reduce(first, 2, 2)
        keep_2, got_2 = line_reduce(second, 1, 1)
        first, second = add(keep_1, got_1, BF), add(keep_2, got_2, BF)
        keep_1, got_1 = line_reduce(first, 1, 1)
        keep_2, got_2 = line_reduce(second, 2, 1)
        self.token = [got_1[:, :1], got_2[:, :1]]
        both = jnp.stack([add(keep_1, got_1, BF), add(keep_2, got_2, BF)], axis=1)
        both = lax.all_to_all(both, "seq", 0, 0, tiled=True, axis_index_groups=z_groups())
        both = jnp.sum(both.astype(F32), axis=0)
        return both[0], both[1]


def to_all(blocks):
    return lax.all_to_all(blocks, "seq", 0, 0, tiled=True)


def kernel(body, outs, *args, flops=0):
    out_shape = [jax.ShapeDtypeStruct(shape, kind) for shape, kind in outs]
    moved = sum(v.size * v.dtype.itemsize for v in list(args) + out_shape)
    return pl.pallas_call(
        body,
        out_shape=out_shape,
        in_specs=[
            pl.BlockSpec(memory_space=pltpu.SMEM if v.dtype == jnp.int32 else pltpu.VMEM)
            for v in args
        ],
        out_specs=[pl.BlockSpec(memory_space=pltpu.VMEM) for _ in outs],
        compiler_params=pltpu.CompilerParams(vmem_limit_bytes=VMEM_BYTES),
        cost_estimate=pl.CostEstimate(flops=flops, bytes_accessed=moved, transcendentals=0),
    )(*args)


def dot(a, b, precision=None):
    return jnp.dot(a, b, preferred_element_type=F32, precision=precision)


def dot_t(a, b, precision=None):
    return lax.dot_general(
        a, b, (((1,), (1,)), ((), ())), preferred_element_type=F32, precision=precision
    )


def t_dot(a, b, precision=None):
    return lax.dot_general(
        a, b, (((0,), (0,)), ((), ())), preferred_element_type=F32, precision=precision
    )


def sigmoid(v):
    return 1.0 / (1.0 + jnp.exp(-v))


def softplus(v):
    return jnp.maximum(v, 0.0) + jnp.log1p(jnp.exp(-jnp.abs(v)))


def lanes(shape):
    return lax.broadcasted_iota(jnp.int32, shape, len(shape) - 1)


def rows_of(shape):
    return lax.broadcasted_iota(jnp.int32, shape, len(shape) - 2)


def rotate(rows, cosine, sine):
    width = rows.shape[-1]
    half = HEAD_SIZE // 2
    low = (lanes(rows.shape) // half) % 2 == 0
    turned = jnp.where(
        low, pltpu.roll(rows, width - half, 1), pltpu.roll(rows, half, 1)
    )
    return rows * cosine + turned * sine


def inverse_rms(rows):
    return lax.rsqrt(jnp.mean(rows * rows, axis=-1, keepdims=True) + eps)


def rms_back(grad, rows, gain):
    scale = inverse_rms(rows)
    scaled = grad * gain
    inner = jnp.mean(rows * scaled, axis=-1, keepdims=True)
    return (
        scale * scaled - rows * (scale * scale * scale * inner),
        jnp.sum(grad * rows * scale, axis=0, keepdims=True),
    )


def pair_wide(columns, pair):
    shape = (columns.shape[0], 2 * P_SIZE)
    return jnp.where(
        lanes(shape) < P_SIZE,
        jnp.broadcast_to(columns[:, 2 * pair : 2 * pair + 1], shape),
        jnp.broadcast_to(columns[:, 2 * pair + 1 : 2 * pair + 2], shape),
    )


def block(pair):
    return slice(2 * P_SIZE * pair, 2 * P_SIZE * (pair + 1))


def convolved(raw, edge, taps):
    span = raw.shape[0]
    extended = jnp.concatenate([edge.astype(F32), raw.astype(F32)], axis=0)
    at = edge.shape[0] - (CONV - 1)
    summed = jnp.broadcast_to(taps[CONV : CONV + 1], raw.shape)
    for k in range(CONV):
        summed = summed + taps[k : k + 1] * extended[at + k : at + k + span]
    return extended, summed


def decay_of(steps_raw, heads):
    span = steps_raw.shape[0]
    steps = softplus(steps_raw)
    logs = -steps * jnp.exp(heads[1:2])
    square = (span, span)
    lower = (lanes(square) <= rows_of(square)).astype(F32)
    upper = (lanes(square) >= rows_of(square)).astype(F32)
    return steps, logs, dot(lower, logs, HIGHEST), t_dot(logs, upper, HIGHEST)


def decays_between(running, running_t, head):
    span = running.shape[0]
    gap = running[:, head : head + 1] - running_t[head : head + 1, :]
    square = (span, span)
    return jnp.exp(jnp.where(lanes(square) <= rows_of(square), gap, -1e30))


def enter_body(
    hidden, gain, w_a, w_b, cosine, sine, heads, normed_o, q_o, kv_o, raw_o, z_o, steps_o
):
    rows = hidden[...]
    normed = (rows * inverse_rms(rows) * gain[...]).astype(BF)
    normed_o[...] = normed
    a, b = dot(normed, w_a[...]), dot(normed, w_b[...])
    turned = rotate(a[:, : QW + 2 * HEAD_SIZE], cosine[...], sine[...])
    q_o[...] = turned[:, :QW].astype(BF)
    kv = turned[:, QW:].astype(BF)
    bc_at = QW + 2 * HEAD_SIZE
    z_a = w_a.shape[1] - REST
    z_o[:, :z_a] = a[:, REST:].astype(BF)
    z_o[:, z_a:] = b[:, : DI - z_a].astype(BF)
    raw_o[:, :DI] = b[:, DI - z_a :].astype(BF)
    raw_o[:, DI:] = a[:, bc_at : bc_at + 2 * N].astype(BF)
    steps_raw = a[:, bc_at + 2 * N : REST] + heads[0:1]
    steps_o[...] = steps_raw
    logs = -softplus(steps_raw) * jnp.exp(heads[1:2])
    span = rows.shape[0] // 2
    for s in (0, 1):
        total = jnp.sum(logs[s * span : (s + 1) * span], axis=0, keepdims=True)
        high = total.astype(BF).astype(F32)
        middle = (total - high).astype(BF).astype(F32)
        low = total - high - middle
        at = rows_of((16, N))
        packed = jnp.where(
            at == 0, high, jnp.where(at == 1, middle, jnp.where(at == 2, low, 0.0))
        ).astype(BF)
        for chip in range(kv_o.shape[0]):
            kv_o[chip, s, :span] = kv[s * span : (s + 1) * span]
            kv_o[chip, s, span:] = packed


def local_body(raw, edge, taps, steps_raw, heads, y_o, c_o, state_o, running_o):
    span = raw.shape[0] // 2
    for s in (0, 1):
        at = slice(s * span, (s + 1) * span)
        _, summed = convolved(raw[at], edge[s], taps[...])
        conv = summed * sigmoid(summed)
        steps, _, running, running_t = decay_of(steps_raw[at], heads[...])
        running_o[at] = running
        b_low, c_low = conv[:, DI : DI + N].astype(BF), conv[:, DI + N :].astype(BF)
        c_o[at] = c_low
        inner = dot_t(c_low, b_low)
        tail = jnp.exp(running[span - 1 : span] - running)
        low_half = lanes((span, 2 * P_SIZE)) < P_SIZE
        for pair in range(HEADS // 2):
            xs = conv[:, block(pair)]
            dt_x = xs * pair_wide(steps, pair)
            dt_low = dt_x.astype(BF)
            mixed = [
                dot((inner * decays_between(running, running_t, h)).astype(BF), dt_low)
                for h in (2 * pair, 2 * pair + 1)
            ]
            skip = pair_wide(heads[2:3], pair)
            y_o[at, block(pair)] = jnp.where(low_half, mixed[0], mixed[1]) + skip * xs
            end = t_dot((dt_x * pair_wide(tail, pair)).astype(BF), b_low)
            state_o[s * DI + 2 * P_SIZE * pair : s * DI + 2 * P_SIZE * (pair + 1)] = end.astype(BF)


def head_rows(rows, head, upper):
    half = rows[:, block(head // 2)].astype(F32)
    if (head % 2 == 1) != upper:
        half = pltpu.roll(half, P_SIZE, 1)
    keep = lanes(half.shape) >= P_SIZE if upper else lanes(half.shape) < P_SIZE
    return jnp.where(keep, half, 0.0)


def heads_joined(parts, upper):
    out = []
    for even, odd in zip(parts[::2], parts[1::2]):
        low_half = lanes(even.shape) < P_SIZE
        if upper:
            out.append(jnp.where(low_half, pltpu.roll(even, P_SIZE, 1), odd))
        else:
            out.append(jnp.where(low_half, even, pltpu.roll(odd, P_SIZE, 1)))
    return jnp.concatenate(out, axis=1)


def head_groups(chips):
    size = QH if chips <= 16 else 1
    return [list(range(k, k + size)) for k in range(0, QH, size)]


def probabilities(queries, keys, first_row, span):
    scores = dot_t(queries, keys) * HEAD_SIZE ** (-0.5)
    shape = (span, keys.shape[0])
    allowed = lanes(shape) <= rows_of(shape) + first_row
    bias = jnp.where(allowed, 0.0, -1e30)
    scores = scores + jnp.concatenate([bias] * (queries.shape[0] // span), axis=0)
    shifted = jnp.exp(scores - jnp.max(scores, axis=-1, keepdims=True))
    return shifted / jnp.sum(shifted, axis=-1, keepdims=True)


def attend_body(first_row, q, kv, att_o, logs_o):
    chips, _, height, _ = kv.shape
    span = q.shape[0] // 2
    for s in (0, 1):
        keys = kv[:, s, :span].reshape(chips * span, 2 * HEAD_SIZE)
        parts = []
        for group in head_groups(chips):
            rows = [head_rows(q[s * span : (s + 1) * span], h, False) for h in group]
            rows = jnp.concatenate(rows, axis=0).astype(BF)
            prob = probabilities(rows, keys, first_row[0], span)
            out = dot(prob.astype(BF), keys)
            parts += [out[k * span : (k + 1) * span] for k in range(len(group))]
        att_o[s * span : (s + 1) * span] = heads_joined(parts, True).astype(BF)
        for chip in range(chips):
            logs = kv[chip, s, span:height].astype(F32)
            logs_o[chip : chip + 1, s * N : (s + 1) * N] = jnp.sum(logs, axis=0, keepdims=True)


def chain_body(reverse, here, blocks, logs, out):
    chips, rows, _ = blocks.shape
    shape = (rows, 2 * N)
    head = lax.shift_right_logical(rows_of(shape) + here[0] * rows, 6)
    column = jnp.where(head >= HEADS, head + (N - HEADS), head)
    chosen = (lanes(shape) == column).astype(F32)
    decay = jnp.exp(dot_t(chosen, logs[...], HIGHEST))
    carry = jnp.zeros((rows, N), F32)
    for chip in reversed(range(chips)) if reverse else range(chips):
        out[chip] = carry.astype(BF)
        carry = decay[:, chip : chip + 1] * carry + blocks[chip].astype(F32)


def mix_body(y_in, running, c_low, carried, z, att, w_attn, w_out, y_o, g_o, part_o):
    span = y_in.shape[0] // 2
    for s in (0, 1):
        at = slice(s * span, (s + 1) * span)
        from_state = dot_t(c_low[at], carried[s * DI : (s + 1) * DI])
        grown = jnp.exp(running[at])
        for pair in range(HEADS // 2):
            y_o[at, block(pair)] = (
                y_in[at, block(pair)] + from_state[:, block(pair)] * pair_wide(grown, pair)
            )
    gate = z[...].astype(F32)
    gated = (y_o[...] * (gate * sigmoid(gate))).astype(BF)
    g_o[...] = gated
    part_o[...] = dot(att[...], w_attn[...]) + dot(gated, w_out[...])


def feed_body(
    hidden, part, other, gain, w_gate, w_up, w_down, mid_o, normed_o, gate_o, up_o, act_o, part_o
):
    middle = hidden[...] + (part[...] + other[...])
    mid_o[...] = middle
    normed = (middle * inverse_rms(middle) * gain[...]).astype(BF)
    normed_o[...] = normed
    gate, up = dot(normed, w_gate[...]), dot(normed, w_up[...])
    gate_o[...] = gate
    up_o[...] = up
    act = (gate * sigmoid(gate) * up).astype(BF)
    act_o[...] = act
    part_o[...] = dot(act, w_down[...])


def feed_back_body(grad, gate, up, w_gate, w_up, w_down, low_o, dgate_o, dup_o, part_o):
    low = grad[...].astype(BF)
    low_o[...] = low
    dact = dot_t(low, w_down[...])
    gates = gate[...]
    share = sigmoid(gates)
    dgate = (dact * up[...] * (share * (1.0 + gates * (1.0 - share)))).astype(BF)
    dup = (dact * (gates * share)).astype(BF)
    dgate_o[...] = dgate
    dup_o[...] = dup
    part_o[...] = dot_t(dgate, w_gate[...]) + dot_t(dup, w_up[...])


def mix_back_body(
    grad, part, other, middle, gain, w_attn, w_out, z, y, c_low, running,
    dmid_o, low_o, datt_o, dy_o, dz_o, state_o, dgain_o,
):
    dnorm, dgain = rms_back(part[...] + other[...], middle[...], gain[...])
    dgain_o[...] = dgain
    dmid = grad[...] + dnorm
    dmid_o[...] = dmid
    low = dmid.astype(BF)
    low_o[...] = low
    datt_o[...] = dot_t(low, w_attn[...]).astype(BF)
    dgated = dot_t(low, w_out[...])
    gate = z[...].astype(F32)
    share = sigmoid(gate)
    dz_o[...] = (dgated * y[...] * (share * (1.0 + gate * (1.0 - share)))).astype(BF)
    dy_o[...] = dgated * (gate * share)
    span = y.shape[0] // 2
    for s in (0, 1):
        at = slice(s * span, (s + 1) * span)
        grown = jnp.exp(running[at])
        for pair in range(HEADS // 2):
            dy = dy_o[at, block(pair)] * pair_wide(grown, pair)
            into = t_dot(dy.astype(BF), c_low[at])
            state_o[s * DI + 2 * P_SIZE * pair : s * DI + 2 * P_SIZE * (pair + 1)] = into.astype(BF)


def attend_back_body(first_row, q, kv, datt, cosine, sine, dq_o, dkv_o):
    chips = kv.shape[0]
    span = q.shape[0] // 2
    scale = HEAD_SIZE ** (-0.5)
    for s in (0, 1):
        at = slice(s * span, (s + 1) * span)
        keys = kv[:, s, :span].reshape(chips * span, 2 * HEAD_SIZE)
        parts = []
        dkv = jnp.zeros((chips * span, 2 * HEAD_SIZE), F32)
        for group in head_groups(chips):
            rows = [head_rows(q[at], h, False) for h in group]
            rows = jnp.concatenate(rows, axis=0).astype(BF)
            grads = [head_rows(datt[at], h, True) for h in group]
            grads = jnp.concatenate(grads, axis=0).astype(BF)
            prob = probabilities(rows, keys, first_row[0], span)
            dprob = dot_t(grads, keys)
            inner = jnp.sum(prob * dprob, axis=-1, keepdims=True)
            dscores = (prob * (dprob - inner)).astype(BF)
            dq = dot(dscores, keys) * scale
            parts += [dq[k * span : (k + 1) * span] for k in range(len(group))]
            dkv = dkv + t_dot(dscores, rows) * scale + t_dot(prob.astype(BF), grads)
        dq = heads_joined(parts, False)
        dq_o[at] = rotate(dq, cosine[at, :QW], -sine[at, :QW]).astype(BF)
        dkv_o[:, s] = dkv.astype(BF).reshape(chips, span, 2 * HEAD_SIZE)


def scan_back_body(
    raw, edge, taps, steps_raw, heads, carried, later, dy_in,
    draw_o, dedge_o, dtaps_o, dsteps_o, dheads_o,
):
    span = raw.shape[0] // 2
    wide = (DI, N)
    head_of = (lax.shift_right_logical(rows_of(wide), 6) == lanes(wide)).astype(F32)
    dtaps = [jnp.zeros((1, taps.shape[1]), F32) for _ in range(CONV + 1)]
    dheads = [jnp.zeros((1, N), F32) for _ in range(3)]
    for s in (0, 1):
        at = slice(s * span, (s + 1) * span)
        extended, summed = convolved(raw[at], edge[s], taps[...])
        share = sigmoid(summed)
        conv = summed * share
        steps, logs, running, running_t = decay_of(steps_raw[at], heads[...])
        b_low, c_low = conv[:, DI : DI + N].astype(BF), conv[:, DI + N :].astype(BF)
        inner = dot_t(c_low, b_low)
        grown = jnp.exp(running)
        tail = jnp.exp(running[span - 1 : span] - running)
        low_half = lanes((span, 2 * P_SIZE)) < P_SIZE
        dinner = jnp.zeros((span, span), F32)
        db = jnp.zeros((span, N), F32)
        dc = jnp.zeros((span, N), F32)
        to_running, to_steps, to_tail, to_skip, dxs = [], [], [], [], []
        for pair in range(HEADS // 2):
            state_rows = slice(s * DI + 2 * P_SIZE * pair, s * DI + 2 * P_SIZE * (pair + 1))
            xs = conv[:, block(pair)]
            dy = dy_in[at, block(pair)]
            dy_low = dy.astype(BF)
            steps_wide = pair_wide(steps, pair)
            dt_x = xs * steps_wide
            dt_low = dt_x.astype(BF)
            y_parts, dx_parts = [], []
            for k in (0, 1):
                decays = decays_between(running, running_t, 2 * pair + k)
                mixing = (inner * decays).astype(BF)
                y_parts.append(dot(mixing, dt_low))
                dx_parts.append(t_dot(mixing, dy_low))
                own = jnp.where(low_half == (k == 0), dy, 0.0).astype(BF)
                dinner = dinner + dot_t(own, dt_low) * decays
            y_inner = jnp.where(low_half, y_parts[0], y_parts[1])
            dx_inner = jnp.where(low_half, dx_parts[0], dx_parts[1])
            grown_wide, tail_wide = pair_wide(grown, pair), pair_wide(tail, pair)
            held, after_it = carried[state_rows], later[state_rows]
            y_state = dot_t(c_low, held) * grown_wide
            dx_end = dot_t(b_low, after_it) * tail_wide
            dc = dc + dot((dy * grown_wide).astype(BF), held)
            db = db + dot((dt_x * tail_wide).astype(BF), after_it)
            ddt_x = dx_inner + dx_end
            to_tail.append(dt_x * dx_end)
            to_running.append(
                dy_low.astype(F32) * y_inner + dy * y_state
                - dt_low.astype(F32) * dx_inner - to_tail[-1]
            )
            to_steps.append(xs * ddt_x)
            to_skip.append(jnp.sum(dy * xs, axis=0, keepdims=True))
            dxs.append(ddt_x * steps_wide + dy * pair_wide(heads[2:3], pair))
        dinner_low = dinner.astype(BF)
        dc = dc + dot(dinner_low, b_low)
        db = db + t_dot(dinner_low, c_low)

        def by_head(parts):
            return dot(jnp.concatenate(parts, axis=1), head_of, HIGHEST)

        here_on = slice(s * DI, (s + 1) * DI)
        both = t_dot(head_of, carried[here_on].astype(F32) * later[here_on].astype(F32), HIGHEST)
        through = dot_t(jnp.ones((8, N), F32), both, HIGHEST)[0:1]
        last = jnp.sum(by_head(to_tail), axis=0, keepdims=True) + grown[span - 1 : span] * through
        drunning = by_head(to_running)
        drunning = drunning + jnp.where(rows_of(drunning.shape) == span - 1, last, 0.0)
        square = (span, span)
        upper = (lanes(square) >= rows_of(square)).astype(F32)
        dlogs = dot(upper, drunning, HIGHEST)
        dsteps = by_head(to_steps) - jnp.exp(heads[1:2]) * dlogs
        dsteps = dsteps * sigmoid(steps_raw[at])
        dsteps = jnp.where(lanes(dsteps.shape) < HEADS, dsteps, 0.0)
        dsteps_o[at] = dsteps.astype(BF)
        dheads[0] += jnp.sum(dsteps, axis=0, keepdims=True)
        dheads[1] += jnp.sum(logs * dlogs, axis=0, keepdims=True)
        skips = jnp.broadcast_to(jnp.concatenate(to_skip, axis=1), (8, DI))
        dheads[2] += dot(skips, head_of, HIGHEST)[0:1]

        dconv = jnp.concatenate(dxs + [db, dc], axis=1)
        dsum = dconv * (share * (1.0 + summed * (1.0 - share)))
        zeros = jnp.zeros((8, dsum.shape[1]), F32)
        behind = jnp.concatenate([dsum, zeros], axis=0)
        ahead = jnp.concatenate([zeros, dsum[:8]], axis=0)
        draw = jnp.zeros_like(dsum)
        dedge = jnp.zeros_like(zeros)
        first = extended.shape[0] - span - (CONV - 1)
        for k in range(CONV):
            tap = taps[k : k + 1]
            draw = draw + tap * behind[CONV - 1 - k : CONV - 1 - k + span]
            dedge = dedge + tap * ahead[CONV - 1 - k : CONV - 1 - k + 8]
            dtaps[k] += jnp.sum(dsum * extended[first + k : first + k + span], axis=0, keepdims=True)
        dtaps[CONV] += jnp.sum(dsum, axis=0, keepdims=True)
        draw_o[at] = draw
        dedge_o[s] = jnp.concatenate([zeros, dedge], axis=0).astype(BF)
    for k in range(CONV + 1):
        dtaps_o[k : k + 1] = dtaps[k]
    dtaps_o[CONV + 1 :] = jnp.zeros((8 - CONV - 1, taps.shape[1]), F32)
    for k in range(3):
        dheads_o[k : k + 1] = dheads[k]
    dheads_o[3:] = jnp.zeros((5, N), F32)


def enter_back_body(
    draw, edge, dq, dkv, dsteps, dz, cosine, sine, w_a, w_b, drest_o, dxs_o, part_o
):
    span = draw.shape[0] // 2
    bc_at = QW + 2 * HEAD_SIZE
    drest_o[:, :QW] = dq[...]
    drest_o[:, bc_at + 2 * N :] = dsteps[...]
    for s in (0, 1):
        at = slice(s * span, (s + 1) * span)
        added = jnp.concatenate(
            [jnp.zeros((span - edge.shape[1], edge.shape[2]), F32), edge[s].astype(F32)], axis=0
        )
        mine = (draw[at] + added).astype(BF)
        dxs_o[at] = mine[:, :DI]
        drest_o[at, bc_at : bc_at + 2 * N] = mine[:, DI:]
        total = jnp.zeros((span, 2 * HEAD_SIZE), F32)
        for chip in range(dkv.shape[0]):
            total = total + dkv[chip, s].astype(F32)
        drest_o[at, QW:bc_at] = rotate(total, cosine[at, QW:], -sine[at, QW:]).astype(BF)
    z_a = w_a.shape[1] - REST
    grads = dz[...]
    part_o[...] = dot_t(
        jnp.concatenate([drest_o[...], grads[:, :z_a]], axis=1), w_a[...]
    ) + dot_t(jnp.concatenate([grads[:, z_a:], dxs_o[...]], axis=1), w_b[...])


def leave_back_body(dmid, part, other, hidden, gain, grad_o, dgain_o):
    dnorm, dgain = rms_back(part[...] + other[...], hidden[...], gain[...])
    grad_o[...] = dmid[...] + dnorm
    dgain_o[...] = dgain


def weight_grad(operand, grad_rows):
    return lax.dot_general(
        operand, grad_rows, (((0,), (0,)), ((), ())), preferred_element_type=F32
    ).astype(BF)


def layer_forward(hidden, gathers, base, gains, taps, heads, tables):
    here = lax.axis_index("seq").astype(jnp.int32).reshape(1)
    count = lax.axis_size("seq")
    rows = hidden.shape[0]
    span = rows // 2
    cosine, sine = tables
    w_a, w_b = (v.reshape(D, -1) for v in gathers.get(base))
    normed, q, kv, raw, z, steps_raw = kernel(
        enter_body,
        [((rows, D), BF), ((rows, QW), BF), ((count, 2, span + 16, N), BF),
         ((rows, DI + 2 * N), BF), ((rows, DI), BF), ((rows, N), F32)],
        hidden, gains[0], w_a, w_b, cosine, sine, heads,
        flops=2 * rows * D * (w_a.shape[1] + w_b.shape[1]),
    )
    kv = to_all(kv)
    tails = raw.reshape(2, span, -1)[:, span - 16 :]
    edge = lax.ppermute(tails, "seq", [(k, k + 1) for k in range(count - 1)])
    gathers.step(raw)
    y_local, c_low, states, running = kernel(
        local_body,
        [((rows, DI), F32), ((rows, N), BF), ((2 * DI, N), BF), ((rows, N), F32)],
        raw, edge, taps, steps_raw, heads, flops=2 * rows * span * DI * 4,
    )
    blocks = to_all(states.reshape(count, -1, N))
    att, logs = kernel(
        attend_body, [((rows, QW), BF), ((count, 2 * N), F32)], here * span, q, kv,
        flops=4 * rows * QW * 2 * count * span,
    )
    gathers.step(att)
    (carried,) = kernel(
        partial(chain_body, False), [(blocks.shape, BF)], here, blocks, logs, flops=blocks.size
    )
    carried = to_all(carried).reshape(2 * DI, N)
    w_attn, w_out, w_down = held_rows(*gathers.get(base + 1))
    y, gated, part = kernel(
        mix_body, [((rows, DI), F32), ((rows, DI), BF), ((rows, D), F32)],
        y_local, running, c_low, carried, z, att, w_attn, w_out, flops=4 * rows * D * D,
    )
    gathers.step(part)
    w_gate, w_up = (v.reshape(D, -1) for v in gathers.get(base + 2))
    middle, normed_two, gate, up, act, part = kernel(
        feed_body,
        [((rows, D), F32), ((rows, D), BF), ((rows, FFH), F32), ((rows, FFH), F32),
         ((rows, FFH), BF), ((rows, D), F32)],
        hidden, part, swap(part), gains[1], w_gate, w_up, w_down, flops=6 * rows * D * D,
    )
    gathers.step(part)
    result = middle + (part + swap(part))
    kept = (
        hidden, normed, q, kv, logs, raw, edge, steps_raw, c_low, running, carried, y, z, att,
        gated, middle, normed_two, gate, up, act,
    )
    return result, kept, (w_a, w_b, w_attn, w_out, w_gate, w_up, w_down)


def layer_backward(grad_result, kept, weights, gains, taps, heads, tables, reduces):
    (
        hidden, normed, q, kv, logs, raw, edge, steps_raw, c_low, running, carried, y, z, att,
        gated, middle, normed_two, gate, up, act,
    ) = kept
    w_a, w_b, w_attn, w_out, w_gate, w_up, w_down = weights
    here = lax.axis_index("seq").astype(jnp.int32).reshape(1)
    count = lax.axis_size("seq")
    rows = hidden.shape[0]
    span = rows // 2
    cosine, sine = tables
    grads = {}
    low, dgate, dup, part = kernel(
        feed_back_body,
        [((rows, D), BF), ((rows, FFH), BF), ((rows, FFH), BF), ((rows, D), F32)],
        grad_result, gate, up, w_gate, w_up, w_down, flops=6 * rows * D * D,
    )
    grads["gate"], grads["up"] = reduces.pair(
        by_chip(weight_grad(normed_two, dgate)), by_chip(weight_grad(normed_two, dup))
    )
    dw_down = columns_home(weight_grad(act, low))
    dmid, low, datt, dy, dz, states, dgain_two = kernel(
        mix_back_body,
        [((rows, D), F32), ((rows, D), BF), ((rows, QW), BF), ((rows, DI), F32), ((rows, DI), BF),
         ((2 * DI, N), BF), ((1, D), F32)],
        grad_result, part, swap(part), middle, gains[1], w_attn, w_out, z, y, c_low, running,
        flops=4 * rows * D * D,
    )
    blocks = to_all(states.reshape(count, -1, N))
    dw_mix = jnp.concatenate(
        [
            weight_grad(att, low).reshape(count // 2, -1, D),
            weight_grad(gated, low).reshape(count // 2, -1, D),
        ],
        axis=1,
    )
    grads["down"], grads["mix"] = reduces.pair(dw_down, columns_home(dw_mix))
    dq, dkv = kernel(
        attend_back_body, [((rows, QW), BF), ((count, 2, span, N), BF)],
        here * span, q, kv, datt, cosine, sine, flops=10 * rows * QW * 2 * count * span,
    )
    dkv = to_all(dkv)
    (later,) = kernel(
        partial(chain_body, True), [(blocks.shape, BF)], here, blocks, logs, flops=blocks.size
    )
    later = to_all(later).reshape(2 * DI, N)
    z_a = w_a.shape[1] - REST
    grads["z_a"], grads["z_b"] = reduces.pair(
        by_chip(weight_grad(normed, dz[:, :z_a])), by_chip(weight_grad(normed, dz[:, z_a:]))
    )
    draw, dedge, dtaps, dsteps, dheads = kernel(
        scan_back_body,
        [((rows, DI + 2 * N), F32), ((2, 16, DI + 2 * N), BF), ((8, DI + 2 * N), F32),
         ((rows, N), BF), ((8, N), F32)],
        raw, edge, taps, steps_raw, heads, carried, later, dy, flops=20 * rows * span * DI,
    )
    dedge = lax.ppermute(dedge, "seq", [(k + 1, k) for k in range(count - 1)])
    drest, dxs, part = kernel(
        enter_back_body, [((rows, REST), BF), ((rows, DI), BF), ((rows, D), F32)],
        draw, dedge, dq, dkv, dsteps, dz, cosine, sine, w_a, w_b,
        flops=2 * rows * D * (w_a.shape[1] + w_b.shape[1]),
    )
    grads["rest"], grads["xs"] = reduces.pair(
        by_chip(weight_grad(normed, drest)), by_chip(weight_grad(normed, dxs))
    )
    grad, dgain_one = kernel(
        leave_back_body, [((rows, D), F32), ((1, D), F32)],
        dmid, part, swap(part), hidden, gains[0], flops=rows * D,
    )
    small = (
        jnp.concatenate([dgain_one, dgain_two], axis=0), dtaps[: CONV + 1], dheads[:3, :HEADS]
    )
    return grad, grads, small


def halves(array, sizes, at):
    out = []
    for core in (0, 1):
        parts, start = [], at
        for width in sizes:
            half = width // 2
            parts.append(array[:, start + core * half : start + (core + 1) * half])
            start += width
        out.append(parts)
    return out


def rotation_tables(positions):
    half = HEAD_SIZE // 2
    frequency = ROPE_BASE ** (-jnp.arange(half, dtype=F32) / half)
    angles = positions.astype(F32)[:, None] * frequency[None, :]
    cosine, sine = jnp.cos(angles), jnp.sin(angles)
    still = jnp.zeros((positions.shape[0], HEAD_SIZE), F32)
    cosine = jnp.tile(jnp.concatenate([cosine, cosine], axis=1), (1, QH + 1))
    sine = jnp.tile(jnp.concatenate([-sine, sine], axis=1), (1, QH + 1))
    return (
        jnp.tile(jnp.concatenate([cosine, still + 1.0], axis=1), (2, 1)),
        jnp.tile(jnp.concatenate([sine, still], axis=1), (2, 1)),
    )


def held_rows(mix, down):
    core = lax.axis_index("section")
    first = core == 0

    def whole(half):
        blocks = half.reshape((2, half.shape[0] // 2) + half.shape[1:])
        keep = lax.dynamic_index_in_dim(blocks, core, 0, False)
        got = swap(lax.dynamic_index_in_dim(blocks, 1 - core, 0, False))
        return jnp.concatenate([jnp.where(first, keep, got), jnp.where(first, got, keep)], axis=2)

    mix = whole(mix)
    height = QW // mix.shape[0]
    return mix[:, :height].reshape(QW, D), mix[:, height:].reshape(DI, D), whole(down).reshape(FFH, D)


def columns_home(whole):
    first = lax.axis_index("section") == 0
    blocks = whole.reshape(lax.axis_size("seq") // 2, -1, D)
    left, right = blocks[..., :HALF], blocks[..., HALF:]
    keep = jnp.where(first, left, right)
    got = swap(jnp.where(first, right, left))
    return jnp.concatenate([jnp.where(first, keep, got), jnp.where(first, got, keep)], axis=0)


def by_chip(whole):
    return whole.reshape(lax.axis_size("seq"), -1, whole.shape[1])


NAMES = ("first", "second", "mix", "down", "gate", "up")
SHARES = ("rest", "z_a", "z_b", "xs", "mix", "gate", "up", "down")


def per_device(
    boundary, lengths, norm_gains, w_qkv, w_attn, w_in, w_dt, conv_params, head_params, w_out, w_gate_up, w_down,
):
    core = lax.axis_index("section")
    here = lax.axis_index("seq")
    count = lax.axis_size("seq")
    first = core == 0
    span = boundary.shape[2]
    rows = 2 * span

    qkv = halves(w_qkv[0], (QW * 2, 2 * HEAD_SIZE, 2 * HEAD_SIZE), 0)
    into = halves(w_in[0], (2 * DI, 2 * DI), 0)
    both_bc = w_in[0][:, 4 * DI :]
    steps = halves(w_dt[0], (SH,), 0)
    ups = halves(w_gate_up[0], (2 * FFH, 2 * FFH), 0)
    mix = jnp.concatenate([w_attn[0], w_out[0]], axis=0)
    cut = []
    for k in (0, 1):
        step = jnp.pad(steps[k][0], ((0, 0), (0, N - HEADS)))
        z_k = into[k][0]
        z_a = z_k.shape[1] // 2
        cut.append(
            {
                "first": jnp.concatenate(qkv[k] + [both_bc, step, z_k[:, :z_a]], axis=1),
                "second": jnp.concatenate([z_k[:, z_a:], into[k][1]], axis=1),
                "mix": mix[:, k * HALF : (k + 1) * HALF],
                "gate": ups[k][0],
                "up": ups[k][1],
                "down": w_down[0][:, k * HALF : (k + 1) * HALF],
            }
        )
    layers = ({}, {})
    for name in NAMES:
        own = jnp.where(first, cut[0][name], cut[1][name])
        got = swap(jnp.where(first, cut[1][name], cut[0][name]))
        layers[0][name] = jnp.where(first, own, got)
        layers[1][name] = jnp.where(first, got, own)

    small = jnp.concatenate([norm_gains[0].reshape(-1), conv_params[0].reshape(-1)])
    small_other = swap(small)
    small = jnp.stack([jnp.where(first, small, small_other), jnp.where(first, small_other, small)])
    small = to_all(jnp.broadcast_to(small[None], (count,) + small.shape))
    small = small.swapaxes(0, 1).astype(F32)
    width = norm_gains.shape[2]
    gains = small[:, :, : 2 * width].reshape(2, count, 2, width).swapaxes(1, 2).reshape(2, 2, D)
    taps = small[:, :, 2 * width :].reshape(2, count, CONV + 1, -1).swapaxes(1, 2)
    taps = taps.reshape(2, CONV + 1, 4 * DI // 2 + 2 * N)
    taps = jnp.concatenate(
        [jnp.where(first, taps[..., :DI], taps[..., DI : 2 * DI]), taps[..., 2 * DI :]], axis=-1
    )
    heads_other = swap(head_params[0])
    heads = jnp.stack(
        [
            jnp.where(first, head_params[0], heads_other),
            jnp.where(first, heads_other, head_params[0]),
        ]
    )
    heads = jnp.where(first, heads[..., :HEADS], heads[..., HEADS:])
    heads = jnp.pad(heads, ((0, 0), (0, 5), (0, N - HEADS)))
    gains = gains.reshape(2, 2, 1, D)
    taps = jnp.pad(taps, ((0, 0), (0, 8 - CONV - 1), (0, 0)))

    other = swap(boundary[0])
    inputs = jnp.where(first, boundary[0], other).reshape(rows, D).astype(F32)
    positions = here * span + jnp.arange(span, dtype=jnp.int32)
    live = (positions[None, :] < lengths[:, None]).astype(F32)
    cotangent = jnp.where(first, other, boundary[0]).astype(F32) * live[..., None]
    cotangent = cotangent.reshape(rows, D)
    tables = rotation_tables(positions)

    gathers = Gathers(
        [
            (layers[layer][a], layers[layer][b])
            for layer in (0, 1)
            for a, b in (("first", "second"), ("mix", "down"), ("gate", "up"))
        ]
    )
    reduces = Reduces()
    middle, kept_0, weights_0 = layer_forward(
        inputs, gathers, 0, gains[0], taps[0], heads[0], tables
    )
    handed = middle.astype(BF).astype(F32)
    result, kept_1, weights_1 = layer_forward(
        handed, gathers, 3, gains[1], taps[1], heads[1], tables
    )
    grad_handed, grads_1, small_1 = layer_backward(
        cotangent, kept_1, weights_1, gains[1], taps[1], heads[1], tables, reduces
    )
    grad_inputs, grads_0, small_0 = layer_backward(
        grad_handed.astype(BF).astype(F32),
        kept_0, weights_0, gains[0], taps[0], heads[0], tables, reduces,
    )

    shares = {}
    for name in SHARES:
        to_second = lax.ppermute(grads_1[name].astype(BF), "section", [(0, 1)])
        to_first = lax.ppermute(grads_0[name].astype(BF), "section", [(1, 0)])
        own = jnp.where(first, grads_0[name], grads_1[name])
        got = jnp.where(first, to_first, to_second).astype(F32)
        shares[name] = (jnp.where(first, own, got), jnp.where(first, got, own))

    def joined(name, start, width):
        return [half[:, start : start + width] for half in shares[name]]

    rest = shares["rest"]
    bc_at = QW + 2 * HEAD_SIZE
    dt_at = bc_at + 2 * N
    grad_qkv = jnp.concatenate(
        joined("rest", 0, QW) + joined("rest", QW, HEAD_SIZE)
        + joined("rest", QW + HEAD_SIZE, HEAD_SIZE), axis=1,
    )
    grad_in = jnp.concatenate(
        [shares["z_a"][0], shares["z_b"][0], shares["z_a"][1], shares["z_b"][1]]
        + list(shares["xs"])
        + [rest[0][:, bc_at:dt_at] + rest[1][:, bc_at:dt_at]], axis=1,
    )
    grad_dt = jnp.concatenate(joined("rest", dt_at, HEADS), axis=1)
    grad_mix = jnp.concatenate(shares["mix"], axis=1)
    attn_rows = w_attn.shape[1]
    grad_gu = jnp.concatenate(shares["gate"] + shares["up"], axis=1)
    grad_down = jnp.concatenate(shares["down"], axis=1)

    conv_width = conv_params.shape[2]

    def small_sum(parts):
        grad_gains, grad_taps, grad_heads = parts
        zeros = jnp.zeros((CONV + 1, DI), F32)
        xs_part = grad_taps[:, :DI]
        wide = jnp.concatenate(
            [jnp.where(first, xs_part, zeros), jnp.where(first, zeros, xs_part), grad_taps[:, DI:]],
            axis=1,
        )
        none = jnp.zeros((3, HEADS), F32)
        head_wide = jnp.concatenate(
            [jnp.where(first, grad_heads, none), jnp.where(first, none, grad_heads)], axis=1
        )
        gains_once = jnp.where(first, grad_gains, 0.0)
        flat = jnp.concatenate(
            [
                gains_once.reshape(2, count, width).swapaxes(0, 1).reshape(count, -1),
                wide.reshape(CONV + 1, count, conv_width).swapaxes(0, 1).reshape(count, -1),
                jnp.broadcast_to(head_wide.reshape(1, -1), (count, 3 * SH)),
            ],
            axis=1,
        )
        flat = jnp.pad(flat, ((0, 0), (0, -flat.shape[1] % N)))
        return both_cores(jnp.sum(to_all(flat.reshape(count, -1, N)), axis=0)).reshape(-1)

    flat = jnp.where(first, small_sum(small_0), small_sum(small_1))
    taps_at = 2 * width
    heads_at = taps_at + (CONV + 1) * conv_width
    grad_gains = flat[:taps_at].reshape(2, width)
    grad_conv = flat[taps_at:heads_at].reshape(CONV + 1, conv_width)
    total_heads = flat[heads_at : heads_at + 3 * SH].reshape(3, SH)

    ends = jnp.where(first, grad_inputs, result).reshape(2, span, D)
    outs = (
        ends, grad_gains, grad_qkv, grad_mix[:attn_rows], grad_in, grad_dt, grad_conv,
        total_heads, grad_mix[attn_rows:], grad_gu, grad_down,
    )
    return tuple(out[None] for out in outs)


def solution(mesh):
    by_rows = P("section", "seq", None)
    by_columns = P("section", None, "seq")
    whole = P("section", None, None)
    ends = P("section", None, "seq", None)
    in_specs = (
        ends, P(), by_columns, by_rows, by_rows, by_rows, by_rows, by_columns, whole, by_rows,
        by_rows, by_rows,
    )
    out_specs = (
        ends, by_columns, by_rows, by_rows, by_rows, by_rows, by_columns, whole, by_rows, by_rows,
        by_rows,
    )
    return jax.shard_map(
        per_device, mesh=mesh, in_specs=in_specs, out_specs=out_specs, check_vma=False
    )
```

```python
from functools import partial
from math import isqrt

import jax
import jax.numpy as jnp
from jax import lax
from jax.experimental import pallas as pl
from jax.experimental.pallas import tpu as pltpu
from jax.sharding import PartitionSpec as P

D = 1024
HEAD_SIZE = 64
SH = 24
P_SIZE = 64
N = 128
CONV = 4
QH = 4
HEADS = SH // 2
QW = QH * HEAD_SIZE
DI = HEADS * P_SIZE
FFH = 1024
HALF = D // 2
REST = QW + 2 * HEAD_SIZE + 2 * N + N

eps = 1e-05
ROPE_BASE = 100000000000.0
HIGHEST = lax.Precision.HIGHEST
BF = jnp.bfloat16
F32 = jnp.float32
VMEM_BYTES = 56 * 2**20
WEIGHT = 3 * 10**11


def grid_of(count):
    side = isqrt(count // 4)
    return (count // (side * side), side, side)


def place_on(axis):
    dims = grid_of(lax.axis_size("seq"))
    strides = (dims[1] * dims[2], dims[2], 1)
    return lax.axis_index("seq") // strides[axis] % dims[axis], dims[axis], strides[axis]


def hop(value, axis, moves):
    count = lax.axis_size("seq")
    _, length, stride = place_on(axis)
    pairs = []
    for source in range(count):
        at = source // stride % length
        if at in moves and moves[at] < length:
            pairs.append((source, source + (moves[at] - at) * stride))
    return lax.ppermute(value, "seq", pairs)


NEXT = {0: 1, 1: 0, 2: 3, 3: 2}
INNER = {1: 2, 2: 1}
OUTWARD = {1: 0, 2: 3}
INWARD = {0: 1, 3: 2}


def swap(value):
    return lax.ppermute(value, "section", [(0, 1), (1, 0)])


def both_cores(value):
    return value + swap(value)


def line_gather(part, axis, dim):
    at, length, _ = place_on(axis)
    got = hop(part, axis, NEXT)
    even = at % 2 == 0
    pair = jnp.stack([jnp.where(even, part, got), jnp.where(even, got, part)], axis=dim)
    if length == 2:
        return pair
    over = hop(pair, axis, INNER)
    rest = hop(over, axis, OUTWARD)
    far = jnp.where((at == 1) | (at == 2), over, rest)
    return jnp.concatenate(
        [jnp.where(at < 2, pair, far), jnp.where(at < 2, far, pair)], axis=dim
    )


def corner():
    places = [place_on(axis)[0] for axis in (2, 1, 0)]
    return jnp.stack(places + [lax.axis_index("section")]).astype(jnp.int32)


class Gathers:
    def __init__(self, pairs, kernel):
        self.pairs, self.kernel = pairs, kernel
        self.count = lax.axis_size("seq")
        self.depth, self.side, _ = grid_of(self.count)
        self.state = [None] * len(pairs)
        self.steps = [(step, k) for k in range(len(pairs)) for step in (1, 2, 3, 4, 5)]
        self.place = corner()
        self.start(0)

    def start(self, at):
        if at < len(self.pairs):
            stacked = jnp.stack(self.pairs[at])
            self.state[at] = (stacked, hop(stacked, 0, NEXT))

    def until(self, step, at):
        while (step, at) in self.steps:
            now, pair = self.steps.pop(0)
            getattr(self, "step_%d" % now)(pair)

    def step_1(self, at):
        own, got = self.state[at]
        (pair,) = self.kernel(in_order_body, [((2,) + own.shape, BF)], self.place, own, got)
        self.state[at] = (pair, hop(pair, 0, INNER))

    def step_2(self, at):
        pair, over = self.state[at]
        self.kernel.also(over)
        self.state[at] = (pair, over, hop(over, 0, OUTWARD))

    def step_3(self, at):
        pair = self.state[at][0]
        shape = (4,) + pair.shape[2:]
        first, second = self.kernel(line_body, [(shape, BF)] * 2, self.place, *self.state[at])
        if self.side == 2:
            self.state[at] = (first, hop(first, 1, NEXT), second, hop(second, 2, NEXT))
        else:
            self.state[at] = (line_gather(first, 1, 1), line_gather(second, 2, 1))

    def step_4(self, at):
        if self.side == 2:
            first = self.state[at][0]
            shape = (4, 2) + first.shape[1:]
            shape_b = (4, 2) + self.state[at][2].shape[1:]
            first, second = self.kernel(
                first_move_body, [(shape, BF), (shape_b, BF)], self.place, *self.state[at]
            )
            self.state[at] = (first, hop(first, 2, NEXT), second, hop(second, 1, NEXT))
        else:
            first, second = self.state[at]
            self.state[at] = (line_gather(first, 2, 2), line_gather(second, 1, 1))
        self.start(at + 1)

    def step_5(self, at):
        if self.side != 2:
            self.state[at] = [v.reshape(D, -1) for v in self.state[at]]
            return
        shapes = [(self.count,) + self.state[at][k].shape[2:] for k in (0, 2)]
        first, second = self.kernel(
            second_move_body, [(v, BF) for v in shapes], self.place, *self.state[at]
        )
        self.state[at] = [first.reshape(D, -1), second.reshape(D, -1)]

    def get(self, at):
        self.until(5, at)
        return self.state[at]


class Whole:
    def __init__(self, shards, kernel, names):
        height = shards["gate"].shape[0]
        self.kernel, self.at = kernel, {}
        parts, first = [], 0
        for name in names:
            shard = shards[name]
            part = jnp.concatenate(
                [shard[k : k + height] for k in range(0, shard.shape[0], height)], axis=1
            )
            parts.append(part)
            self.at[name] = (first, part.shape[1])
            first += part.shape[1]
        self.flat = jnp.concatenate(parts, axis=1)

    def start(self):
        self.whole = lax.all_gather(self.flat, "seq", axis=0, tiled=True)

    def part(self, name):
        return Part(self.whole, *self.at[name])

    def rows(self):
        part = Part(self.whole, self.at["mix"][0], 2 * D)
        (away,) = self.kernel(cut_body, [((part.shape[0] // 2, 2 * D), BF)], corner(), part)
        return self.kernel(
            partial(rows_body, lax.axis_size("seq") // 2),
            [((QW, D), BF), ((DI, D), BF), ((FFH, D), BF)], corner(), part, swap(away),
        )


def add(a, b, kind):
    return (a.astype(F32) + b.astype(F32)).astype(kind)


def line_reduce(parts, axis, dim):
    at, length, _ = place_on(axis)

    def pick(array, index):
        return lax.dynamic_index_in_dim(array, index, dim, False)

    if length == 4:
        halves = parts.reshape(parts.shape[:dim] + (2, 2) + parts.shape[dim + 1 :])
        far, near = pick(halves, 1 - at // 2), pick(halves, at // 2)
        far = add(far, hop(far, axis, INWARD), BF)
        parts = add(near, hop(far, axis, INNER), BF)
    got = hop(pick(parts, 1 - at % 2), axis, NEXT)
    return pick(parts, at % 2), got


def z_groups():
    count = lax.axis_size("seq")
    depth, side, _ = grid_of(count)
    plane = side * side
    return [[z * plane + k for z in range(depth)] for k in range(plane)]


class Reduces:
    def __init__(self, kernel):
        self.kernel = kernel
        self.paired = grid_of(lax.axis_size("seq"))[2] == 2

    def open_plain(self, rows_a, grad_a, rows_b, grad_b):
        count = lax.axis_size("seq")
        depth = grid_of(count)[0]
        if not self.paired:
            return self.open_whole(
                by_chip(weight_grad(rows_a, grad_a)), by_chip(weight_grad(rows_b, grad_b))
            )
        height = rows_a.shape[1] // count
        shape = (depth, 2, height, grad_a.shape[1])
        parts = self.kernel(
            split_body, [(shape, BF)] * 4, corner(), rows_a, grad_a, rows_b, grad_b,
            flops=4 * rows_a.size * grad_a.shape[1],
        )
        return self.open(parts)

    def columns(self, act, att, gated, grad):
        half = lax.axis_size("seq") // 2
        if not self.paired:
            mix = jnp.concatenate(
                [weight_grad(v, grad[1]).reshape(half, -1, D) for v in (att, gated)], axis=1
            )
            return columns_home(weight_grad(act, grad[0])), columns_home(mix)
        down, mix = (half, FFH // half, HALF), (half, (QW + DI) // half, HALF)
        keep_d, away_d, keep_m, away_m = self.kernel(
            columns_body, [(down, BF), (down, BF), (mix, BF), (mix, BF)],
            corner(), act, att, gated, *grad, flops=4 * act.size * D,
        )
        return keep_d, swap(away_d), keep_m, swap(away_m)

    def open_columns(self, columns):
        if not self.paired:
            return self.open_whole(*columns)
        depth = grid_of(lax.axis_size("seq"))[0]
        shapes = [((depth, 2) + columns[k].shape[1:], BF) for k in range(4)]
        return self.open(self.kernel(regroup_body, shapes, corner(), *columns))

    def open(self, parts):
        send_a, keep_a, send_b, keep_b = parts
        got_a, got_b = hop(send_a, 2, NEXT), hop(send_b, 1, NEXT)
        return keep_a, got_a, keep_b, got_b

    def open_whole(self, first, second):
        dims = grid_of(lax.axis_size("seq"))
        first, second = (v.reshape(dims + v.shape[1:]) for v in (first, second))
        keep_a, got_a = line_reduce(first, 2, 2)
        keep_b, got_b = line_reduce(second, 1, 1)
        return keep_a, got_a, keep_b, got_b

    def fold(self, state):
        keep_a, got_a, keep_b, got_b = state
        if not self.paired:
            first, second = add(keep_a, got_a, BF), add(keep_b, got_b, BF)
            return *line_reduce(first, 1, 1), *line_reduce(second, 2, 1)
        shape = keep_a.shape[:1] + keep_a.shape[2:]
        shape_b = keep_b.shape[:1] + keep_b.shape[2:]
        send_a, keep_a, send_b, keep_b = self.kernel(
            fold_body, [(shape, BF), (shape, BF), (shape_b, BF), (shape_b, BF)],
            corner(), keep_a, got_a, keep_b, got_b,
        )
        return keep_a, hop(send_a, 1, NEXT), keep_b, hop(send_b, 2, NEXT)

    def settle(self, state):
        self.kernel.also(state[1])
        self.kernel.also(state[3])

    def flat(self, state):
        height = D // lax.axis_size("seq")
        return height, sum(v.shape[1] * v.shape[2] // height for v in (state[0], state[2]))

    def z_start(self, *states):
        height = self.flat(states[0])[0]
        shape = (2, height, sum(self.flat(v)[1] for v in states))
        far, near = self.kernel(
            z_start_body, [(shape, BF)] * 2, corner(), *[v for state in states for v in state]
        )
        return far, hop(far, 0, INWARD), near

    def z_across(self, state):
        far, got, near = state
        (far,) = self.kernel(z_across_body, [(far.shape, BF)], far, got)
        return near, hop(far, 0, INNER)

    def z_last(self, state):
        near, got = state
        shape = near.shape[1:]
        send, keep = self.kernel(z_last_body, [(shape, BF)] * 2, corner(), near, got)
        return keep, hop(send, 0, NEXT)

    def own(self, first, second):
        shape = first[0].shape
        mine, away = self.kernel(choose_body, [(shape, F32)] * 2, corner(), *first, *second)
        return mine, swap(away)


def to_all(blocks):
    return lax.all_to_all(blocks, "seq", 0, 0, tiled=True)


class Part:
    def __init__(self, whole, first, width):
        self.whole, self.first = whole, first
        self.shape, self.dtype = (whole.shape[0], width), whole.dtype


class Order:
    def __init__(self):
        self.before = []
        self.weight = 5 * 10**9

    def also(self, value):
        self.before = self.before + [value]

    def __call__(self, body, outs, *args, flops=0):
        out_shape = [jax.ShapeDtypeStruct(shape, kind) for shape, kind in outs]
        count, extra = len(args), len(self.before)
        parts = [k for k, v in enumerate(args) if isinstance(v, Part)]

        def run(*refs):
            given = list(refs[:count])
            results = refs[count + extra : count + extra + len(outs)]
            scratch = refs[count + extra + len(outs) :]
            copies = []
            for slot, k in enumerate(parts):
                source = given[k].at[:, args[k].first : args[k].first + args[k].shape[1]]
                copies.append(pltpu.make_async_copy(source, scratch[slot], scratch[-1].at[slot]))
                copies[-1].start()
                given[k] = scratch[slot]
            for copy in copies:
                copy.wait()
            body(*given, *results)

        def space(v):
            if isinstance(v, Part):
                return pl.ANY
            return pltpu.SMEM if v.dtype == jnp.int32 else pltpu.VMEM

        scratch = [pltpu.VMEM(args[k].shape, args[k].dtype) for k in parts]
        if parts:
            scratch.append(pltpu.SemaphoreType.DMA((len(parts),)))
        results = pl.pallas_call(
            run,
            out_shape=out_shape,
            in_specs=[pl.BlockSpec(memory_space=space(v)) for v in args]
            + [pl.BlockSpec(memory_space=pl.ANY)] * extra,
            out_specs=[pl.BlockSpec(memory_space=pltpu.VMEM) for _ in outs],
            scratch_shapes=scratch,
            compiler_params=pltpu.CompilerParams(vmem_limit_bytes=VMEM_BYTES),
            cost_estimate=pl.CostEstimate(flops=self.weight, bytes_accessed=0, transcendentals=0),
        )(*[v.whole if isinstance(v, Part) else v for v in args], *self.before)
        self.before = [min(results, key=lambda v: v.size)]
        return results


def dot(a, b, precision=None):
    return jnp.dot(a, b, preferred_element_type=F32, precision=precision)


def dot_t(a, b, precision=None):
    return lax.dot_general(
        a, b, (((1,), (1,)), ((), ())), preferred_element_type=F32, precision=precision
    )


def t_dot(a, b, precision=None):
    return lax.dot_general(
        a, b, (((0,), (0,)), ((), ())), preferred_element_type=F32, precision=precision
    )


def sigmoid(v):
    return 1.0 / (1.0 + jnp.exp(-v))


def softplus(v):
    return jnp.maximum(v, 0.0) + jnp.log1p(jnp.exp(-jnp.abs(v)))


def lanes(shape):
    return lax.broadcasted_iota(jnp.int32, shape, len(shape) - 1)


def rows_of(shape):
    return lax.broadcasted_iota(jnp.int32, shape, len(shape) - 2)


def rotate(rows, cosine, sine):
    width = rows.shape[-1]
    half = HEAD_SIZE // 2
    low = (lanes(rows.shape) // half) % 2 == 0
    turned = jnp.where(
        low, pltpu.roll(rows, width - half, 1), pltpu.roll(rows, half, 1)
    )
    return rows * cosine + turned * sine


def inverse_rms(rows):
    return lax.rsqrt(jnp.mean(rows * rows, axis=-1, keepdims=True) + eps)


def rms_back(grad, rows, gain):
    scale = inverse_rms(rows)
    scaled = grad * gain
    inner = jnp.mean(rows * scaled, axis=-1, keepdims=True)
    return (
        scale * scaled - rows * (scale * scale * scale * inner),
        jnp.sum(grad * rows * scale, axis=0, keepdims=True),
    )


def pair_wide(columns, pair):
    shape = (columns.shape[0], 2 * P_SIZE)
    return jnp.where(
        lanes(shape) < P_SIZE,
        jnp.broadcast_to(columns[:, 2 * pair : 2 * pair + 1], shape),
        jnp.broadcast_to(columns[:, 2 * pair + 1 : 2 * pair + 2], shape),
    )


def block(pair):
    return slice(2 * P_SIZE * pair, 2 * P_SIZE * (pair + 1))


def convolved(raw, edge, taps):
    span = raw.shape[0]
    extended = jnp.concatenate([edge.astype(F32), raw.astype(F32)], axis=0)
    at = edge.shape[0] - (CONV - 1)
    summed = jnp.broadcast_to(taps[CONV : CONV + 1], raw.shape)
    for k in range(CONV):
        summed = summed + taps[k : k + 1] * extended[at + k : at + k + span]
    return extended, summed


def decay_of(steps_raw, heads):
    span = steps_raw.shape[0]
    steps = softplus(steps_raw)
    logs = -steps * jnp.exp(heads[1:2])
    square = (span, span)
    lower = (lanes(square) <= rows_of(square)).astype(F32)
    upper = (lanes(square) >= rows_of(square)).astype(F32)
    return steps, logs, dot(lower, logs, HIGHEST), t_dot(logs, upper, HIGHEST)


def decays_between(running, running_t, head):
    span = running.shape[0]
    gap = running[:, head : head + 1] - running_t[head : head + 1, :]
    square = (span, span)
    return jnp.exp(jnp.where(lanes(square) <= rows_of(square), gap, -1e30))


def enter_body(
    hidden, gain, w_a, w_b, cosine, sine, heads, normed_o, q_o, kv_o, raw_o, z_o, steps_o
):
    rows = hidden[...]
    normed = (rows * inverse_rms(rows) * gain[...]).astype(BF)
    normed_o[...] = normed
    a, b = dot(normed, w_a[...]), dot(normed, w_b[...])
    turned = rotate(a[:, : QW + 2 * HEAD_SIZE], cosine[...], sine[...])
    q_o[...] = turned[:, :QW].astype(BF)
    kv = turned[:, QW:].astype(BF)
    bc_at = QW + 2 * HEAD_SIZE
    z_a = w_a.shape[1] - REST
    z_o[:, :z_a] = a[:, REST:].astype(BF)
    z_o[:, z_a:] = b[:, : DI - z_a].astype(BF)
    raw_o[:, :DI] = b[:, DI - z_a :].astype(BF)
    raw_o[:, DI:] = a[:, bc_at : bc_at + 2 * N].astype(BF)
    steps_raw = a[:, bc_at + 2 * N : REST] + heads[0:1]
    steps_o[...] = steps_raw
    logs = -softplus(steps_raw) * jnp.exp(heads[1:2])
    span = rows.shape[0] // 2
    for s in (0, 1):
        total = jnp.sum(logs[s * span : (s + 1) * span], axis=0, keepdims=True)
        high = total.astype(BF).astype(F32)
        middle = (total - high).astype(BF).astype(F32)
        low = total - high - middle
        at = rows_of((16, N))
        packed = jnp.where(
            at == 0, high, jnp.where(at == 1, middle, jnp.where(at == 2, low, 0.0))
        ).astype(BF)
        for chip in range(kv_o.shape[0]):
            kv_o[chip, s, :span] = kv[s * span : (s + 1) * span]
            kv_o[chip, s, span:] = packed


def local_body(raw, edge, taps, steps_raw, heads, y_o, c_o, state_o, running_o):
    span = raw.shape[0] // 2
    for s in (0, 1):
        at = slice(s * span, (s + 1) * span)
        _, summed = convolved(raw[at], edge[s], taps[...])
        conv = summed * sigmoid(summed)
        steps, _, running, running_t = decay_of(steps_raw[at], heads[...])
        running_o[at] = running
        b_low, c_low = conv[:, DI : DI + N].astype(BF), conv[:, DI + N :].astype(BF)
        c_o[at] = c_low
        inner = dot_t(c_low, b_low)
        tail = jnp.exp(running[span - 1 : span] - running)
        low_half = lanes((span, 2 * P_SIZE)) < P_SIZE
        for pair in range(HEADS // 2):
            xs = conv[:, block(pair)]
            dt_x = xs * pair_wide(steps, pair)
            dt_low = dt_x.astype(BF)
            mixed = [
                dot((inner * decays_between(running, running_t, h)).astype(BF), dt_low)
                for h in (2 * pair, 2 * pair + 1)
            ]
            skip = pair_wide(heads[2:3], pair)
            y_o[at, block(pair)] = jnp.where(low_half, mixed[0], mixed[1]) + skip * xs
            end = t_dot((dt_x * pair_wide(tail, pair)).astype(BF), b_low)
            state_o[s * DI + 2 * P_SIZE * pair : s * DI + 2 * P_SIZE * (pair + 1)] = end.astype(BF)


def head_rows(rows, head, upper):
    half = rows[:, block(head // 2)].astype(F32)
    if (head % 2 == 1) != upper:
        half = pltpu.roll(half, P_SIZE, 1)
    keep = lanes(half.shape) >= P_SIZE if upper else lanes(half.shape) < P_SIZE
    return jnp.where(keep, half, 0.0)


def heads_joined(parts, upper):
    out = []
    for even, odd in zip(parts[::2], parts[1::2]):
        low_half = lanes(even.shape) < P_SIZE
        if upper:
            out.append(jnp.where(low_half, pltpu.roll(even, P_SIZE, 1), odd))
        else:
            out.append(jnp.where(low_half, even, pltpu.roll(odd, P_SIZE, 1)))
    return jnp.concatenate(out, axis=1)


def head_groups(chips):
    size = QH if chips <= 16 else 1
    return [list(range(k, k + size)) for k in range(0, QH, size)]


def probabilities(queries, keys, first_row, span):
    scores = dot_t(queries, keys) * HEAD_SIZE ** (-0.5)
    shape = (span, keys.shape[0])
    allowed = lanes(shape) <= rows_of(shape) + first_row
    bias = jnp.where(allowed, 0.0, -1e30)
    scores = scores + jnp.concatenate([bias] * (queries.shape[0] // span), axis=0)
    shifted = jnp.exp(scores - jnp.max(scores, axis=-1, keepdims=True))
    return shifted / jnp.sum(shifted, axis=-1, keepdims=True)


def attend_body(first_row, q, kv, att_o, logs_o):
    chips, _, height, _ = kv.shape
    span = q.shape[0] // 2
    for s in (0, 1):
        keys = kv[:, s, :span].reshape(chips * span, 2 * HEAD_SIZE)
        parts = []
        for group in head_groups(chips):
            rows = [head_rows(q[s * span : (s + 1) * span], h, False) for h in group]
            rows = jnp.concatenate(rows, axis=0).astype(BF)
            prob = probabilities(rows, keys, first_row[0], span)
            out = dot(prob.astype(BF), keys)
            parts += [out[k * span : (k + 1) * span] for k in range(len(group))]
        att_o[s * span : (s + 1) * span] = heads_joined(parts, True).astype(BF)
        for chip in range(chips):
            logs = kv[chip, s, span:height].astype(F32)
            logs_o[chip : chip + 1, s * N : (s + 1) * N] = jnp.sum(logs, axis=0, keepdims=True)


def chain_body(reverse, here, blocks, logs, out):
    chips, rows, _ = blocks.shape
    shape = (rows, 2 * N)
    head = lax.shift_right_logical(rows_of(shape) + here[0] * rows, 6)
    column = jnp.where(head >= HEADS, head + (N - HEADS), head)
    chosen = (lanes(shape) == column).astype(F32)
    decay = jnp.exp(dot_t(chosen, logs[...], HIGHEST))
    carry = jnp.zeros((rows, N), F32)
    for chip in reversed(range(chips)) if reverse else range(chips):
        out[chip] = carry.astype(BF)
        carry = decay[:, chip : chip + 1] * carry + blocks[chip].astype(F32)


def mix_body(y_in, running, c_low, carried, z, att, w_attn, w_out, y_o, g_o, part_o):
    span = y_in.shape[0] // 2
    for s in (0, 1):
        at = slice(s * span, (s + 1) * span)
        from_state = dot_t(c_low[at], carried[s * DI : (s + 1) * DI])
        grown = jnp.exp(running[at])
        for pair in range(HEADS // 2):
            y_o[at, block(pair)] = (
                y_in[at, block(pair)] + from_state[:, block(pair)] * pair_wide(grown, pair)
            )
    gate = z[...].astype(F32)
    gated = (y_o[...] * (gate * sigmoid(gate))).astype(BF)
    g_o[...] = gated
    part_o[...] = dot(att[...], w_attn[...]) + dot(gated, w_out[...])


def feed_body(
    hidden, part, other, gain, w_gate, w_up, w_down, mid_o, normed_o, gate_o, up_o, act_o, part_o
):
    middle = hidden[...] + (part[...] + other[...])
    mid_o[...] = middle
    normed = (middle * inverse_rms(middle) * gain[...]).astype(BF)
    normed_o[...] = normed
    gate, up = dot(normed, w_gate[...]), dot(normed, w_up[...])
    gate_o[...] = gate
    up_o[...] = up
    act = (gate * sigmoid(gate) * up).astype(BF)
    act_o[...] = act
    part_o[...] = dot(act, w_down[...])


def feed_back_body(grad, gate, up, w_gate, w_up, w_down, low_o, dgate_o, dup_o, part_o):
    low = grad[...].astype(BF)
    low_o[...] = low
    dact = dot_t(low, w_down[...])
    gates = gate[...]
    share = sigmoid(gates)
    dgate = (dact * up[...] * (share * (1.0 + gates * (1.0 - share)))).astype(BF)
    dup = (dact * (gates * share)).astype(BF)
    dgate_o[...] = dgate
    dup_o[...] = dup
    part_o[...] = dot_t(dgate, w_gate[...]) + dot_t(dup, w_up[...])


def mix_back_body(
    grad, part, other, middle, gain, w_attn, w_out, z, y, c_low, running,
    dmid_o, low_o, datt_o, dy_o, dz_o, state_o, dgain_o,
):
    dnorm, dgain = rms_back(part[...] + other[...], middle[...], gain[...])
    dgain_o[...] = dgain
    dmid = grad[...] + dnorm
    dmid_o[...] = dmid
    low = dmid.astype(BF)
    low_o[...] = low
    datt_o[...] = dot_t(low, w_attn[...]).astype(BF)
    dgated = dot_t(low, w_out[...])
    gate = z[...].astype(F32)
    share = sigmoid(gate)
    dz_o[...] = (dgated * y[...] * (share * (1.0 + gate * (1.0 - share)))).astype(BF)
    dy_o[...] = dgated * (gate * share)
    span = y.shape[0] // 2
    for s in (0, 1):
        at = slice(s * span, (s + 1) * span)
        grown = jnp.exp(running[at])
        for pair in range(HEADS // 2):
            dy = dy_o[at, block(pair)] * pair_wide(grown, pair)
            into = t_dot(dy.astype(BF), c_low[at])
            state_o[s * DI + 2 * P_SIZE * pair : s * DI + 2 * P_SIZE * (pair + 1)] = into.astype(BF)


def attend_back_body(first_row, q, kv, datt, cosine, sine, dq_o, dkv_o):
    chips = kv.shape[0]
    span = q.shape[0] // 2
    scale = HEAD_SIZE ** (-0.5)
    for s in (0, 1):
        at = slice(s * span, (s + 1) * span)
        keys = kv[:, s, :span].reshape(chips * span, 2 * HEAD_SIZE)
        parts = []
        dkv = jnp.zeros((chips * span, 2 * HEAD_SIZE), F32)
        for group in head_groups(chips):
            rows = [head_rows(q[at], h, False) for h in group]
            rows = jnp.concatenate(rows, axis=0).astype(BF)
            grads = [head_rows(datt[at], h, True) for h in group]
            grads = jnp.concatenate(grads, axis=0).astype(BF)
            prob = probabilities(rows, keys, first_row[0], span)
            dprob = dot_t(grads, keys)
            inner = jnp.sum(prob * dprob, axis=-1, keepdims=True)
            dscores = (prob * (dprob - inner)).astype(BF)
            dq = dot(dscores, keys) * scale
            parts += [dq[k * span : (k + 1) * span] for k in range(len(group))]
            dkv = dkv + t_dot(dscores, rows) * scale + t_dot(prob.astype(BF), grads)
        dq = heads_joined(parts, False)
        dq_o[at] = rotate(dq, cosine[at, :QW], -sine[at, :QW]).astype(BF)
        dkv_o[:, s] = dkv.astype(BF).reshape(chips, span, 2 * HEAD_SIZE)


def scan_back_body(
    raw, edge, taps, steps_raw, heads, carried, later, dy_in,
    draw_o, dedge_o, dtaps_o, dsteps_o, dheads_o,
):
    span = raw.shape[0] // 2
    wide = (DI, N)
    head_of = (lax.shift_right_logical(rows_of(wide), 6) == lanes(wide)).astype(F32)
    dtaps = [jnp.zeros((1, taps.shape[1]), F32) for _ in range(CONV + 1)]
    dheads = [jnp.zeros((1, N), F32) for _ in range(3)]
    for s in (0, 1):
        at = slice(s * span, (s + 1) * span)
        extended, summed = convolved(raw[at], edge[s], taps[...])
        share = sigmoid(summed)
        conv = summed * share
        steps, logs, running, running_t = decay_of(steps_raw[at], heads[...])
        b_low, c_low = conv[:, DI : DI + N].astype(BF), conv[:, DI + N :].astype(BF)
        inner = dot_t(c_low, b_low)
        grown = jnp.exp(running)
        tail = jnp.exp(running[span - 1 : span] - running)
        low_half = lanes((span, 2 * P_SIZE)) < P_SIZE
        dinner = jnp.zeros((span, span), F32)
        db = jnp.zeros((span, N), F32)
        dc = jnp.zeros((span, N), F32)
        to_running, to_steps, to_tail, to_skip, dxs = [], [], [], [], []
        for pair in range(HEADS // 2):
            state_rows = slice(s * DI + 2 * P_SIZE * pair, s * DI + 2 * P_SIZE * (pair + 1))
            xs = conv[:, block(pair)]
            dy = dy_in[at, block(pair)]
            dy_low = dy.astype(BF)
            steps_wide = pair_wide(steps, pair)
            dt_x = xs * steps_wide
            dt_low = dt_x.astype(BF)
            y_parts, dx_parts = [], []
            for k in (0, 1):
                decays = decays_between(running, running_t, 2 * pair + k)
                mixing = (inner * decays).astype(BF)
                y_parts.append(dot(mixing, dt_low))
                dx_parts.append(t_dot(mixing, dy_low))
                own = jnp.where(low_half == (k == 0), dy, 0.0).astype(BF)
                dinner = dinner + dot_t(own, dt_low) * decays
            y_inner = jnp.where(low_half, y_parts[0], y_parts[1])
            dx_inner = jnp.where(low_half, dx_parts[0], dx_parts[1])
            grown_wide, tail_wide = pair_wide(grown, pair), pair_wide(tail, pair)
            held, after_it = carried[state_rows], later[state_rows]
            y_state = dot_t(c_low, held) * grown_wide
            dx_end = dot_t(b_low, after_it) * tail_wide
            dc = dc + dot((dy * grown_wide).astype(BF), held)
            db = db + dot((dt_x * tail_wide).astype(BF), after_it)
            ddt_x = dx_inner + dx_end
            to_tail.append(dt_x * dx_end)
            to_running.append(
                dy_low.astype(F32) * y_inner + dy * y_state
                - dt_low.astype(F32) * dx_inner - to_tail[-1]
            )
            to_steps.append(xs * ddt_x)
            to_skip.append(jnp.sum(dy * xs, axis=0, keepdims=True))
            dxs.append(ddt_x * steps_wide + dy * pair_wide(heads[2:3], pair))
        dinner_low = dinner.astype(BF)
        dc = dc + dot(dinner_low, b_low)
        db = db + t_dot(dinner_low, c_low)

        def by_head(parts):
            return dot(jnp.concatenate(parts, axis=1), head_of, HIGHEST)

        here_on = slice(s * DI, (s + 1) * DI)
        both = t_dot(head_of, carried[here_on].astype(F32) * later[here_on].astype(F32), HIGHEST)
        through = dot_t(jnp.ones((8, N), F32), both, HIGHEST)[0:1]
        last = jnp.sum(by_head(to_tail), axis=0, keepdims=True) + grown[span - 1 : span] * through
        drunning = by_head(to_running)
        drunning = drunning + jnp.where(rows_of(drunning.shape) == span - 1, last, 0.0)
        square = (span, span)
        upper = (lanes(square) >= rows_of(square)).astype(F32)
        dlogs = dot(upper, drunning, HIGHEST)
        dsteps = by_head(to_steps) - jnp.exp(heads[1:2]) * dlogs
        dsteps = dsteps * sigmoid(steps_raw[at])
        dsteps = jnp.where(lanes(dsteps.shape) < HEADS, dsteps, 0.0)
        dsteps_o[at] = dsteps.astype(BF)
        dheads[0] += jnp.sum(dsteps, axis=0, keepdims=True)
        dheads[1] += jnp.sum(logs * dlogs, axis=0, keepdims=True)
        skips = jnp.broadcast_to(jnp.concatenate(to_skip, axis=1), (8, DI))
        dheads[2] += dot(skips, head_of, HIGHEST)[0:1]

        dconv = jnp.concatenate(dxs + [db, dc], axis=1)
        dsum = dconv * (share * (1.0 + summed * (1.0 - share)))
        zeros = jnp.zeros((8, dsum.shape[1]), F32)
        behind = jnp.concatenate([dsum, zeros], axis=0)
        ahead = jnp.concatenate([zeros, dsum[:8]], axis=0)
        draw = jnp.zeros_like(dsum)
        dedge = jnp.zeros_like(zeros)
        first = extended.shape[0] - span - (CONV - 1)
        for k in range(CONV):
            tap = taps[k : k + 1]
            draw = draw + tap * behind[CONV - 1 - k : CONV - 1 - k + span]
            dedge = dedge + tap * ahead[CONV - 1 - k : CONV - 1 - k + 8]
            dtaps[k] += jnp.sum(dsum * extended[first + k : first + k + span], axis=0, keepdims=True)
        dtaps[CONV] += jnp.sum(dsum, axis=0, keepdims=True)
        draw_o[at] = draw
        dedge_o[s] = jnp.concatenate([zeros, dedge], axis=0).astype(BF)
    for k in range(CONV + 1):
        dtaps_o[k : k + 1] = dtaps[k]
    dtaps_o[CONV + 1 :] = jnp.zeros((8 - CONV - 1, taps.shape[1]), F32)
    for k in range(3):
        dheads_o[k : k + 1] = dheads[k]
    dheads_o[3:] = jnp.zeros((5, N), F32)


def enter_back_body(
    draw, edge, dq, dkv, dsteps, dz, cosine, sine, w_a, w_b, drest_o, dxs_o, part_o
):
    span = draw.shape[0] // 2
    bc_at = QW + 2 * HEAD_SIZE
    drest_o[:, :QW] = dq[...]
    drest_o[:, bc_at + 2 * N :] = dsteps[...]
    for s in (0, 1):
        at = slice(s * span, (s + 1) * span)
        added = jnp.concatenate(
            [jnp.zeros((span - edge.shape[1], edge.shape[2]), F32), edge[s].astype(F32)], axis=0
        )
        mine = (draw[at] + added).astype(BF)
        dxs_o[at] = mine[:, :DI]
        drest_o[at, bc_at : bc_at + 2 * N] = mine[:, DI:]
        total = jnp.zeros((span, 2 * HEAD_SIZE), F32)
        for chip in range(dkv.shape[0]):
            total = total + dkv[chip, s].astype(F32)
        drest_o[at, QW:bc_at] = rotate(total, cosine[at, QW:], -sine[at, QW:]).astype(BF)
    z_a = w_a.shape[1] - REST
    grads = dz[...]
    part_o[...] = dot_t(
        jnp.concatenate([drest_o[...], grads[:, :z_a]], axis=1), w_a[...]
    ) + dot_t(jnp.concatenate([grads[:, z_a:], dxs_o[...]], axis=1), w_b[...])


def leave_back_body(dmid, part, other, hidden, gain, grad_o, dgain_o):
    dnorm, dgain = rms_back(part[...] + other[...], hidden[...], gain[...])
    grad_o[...] = dmid[...] + dnorm
    dgain_o[...] = dgain


def in_order_body(at, own, got, out):
    even = at[2] % 2 == 0
    for k in range(own.shape[0]):
        out[0, k] = jnp.where(even, own[k], got[k])
        out[1, k] = jnp.where(even, got[k], own[k])


def line_body(at, pair, over, rest, first, second):
    inner = (at[2] == 1) | (at[2] == 2)
    for k, out in enumerate((first, second)):
        for j in (0, 1):
            far = jnp.where(inner, over[j, k], rest[j, k])
            out[j] = jnp.where(at[2] < 2, pair[j, k], far)
            out[2 + j] = jnp.where(at[2] < 2, far, pair[j, k])


def first_move_body(at, own_a, got_a, own_b, got_b, first, second):
    for index, own, got, out in ((1, own_a, got_a, first), (0, own_b, got_b, second)):
        for z in range(own.shape[0]):
            out[z, 0] = jnp.where(at[index] == 0, own[z], got[z])
            out[z, 1] = jnp.where(at[index] == 0, got[z], own[z])


def second_move_body(at, own_a, got_a, own_b, got_b, first, second):
    for z in range(own_a.shape[0]):
        for k in (0, 1):
            for j in (0, 1):
                own, got = (own_a, got_a) if j == 0 else (got_a, own_a)
                first[4 * z + 2 * k + j] = jnp.where(at[0] == 0, own[z, k], got[z, k])
                own, got = (own_b, got_b) if j == 0 else (got_b, own_b)
                second[4 * z + 2 * j + k] = jnp.where(at[1] == 0, own[z, k], got[z, k])


def cut_body(at, whole, away):
    height = away.shape[0]
    first = pl.multiple_of((1 - at[3]) * height, height)
    away[...] = whole[pl.ds(first, height), :]


def rows_body(chips, at, whole, got, attn, rest, down):
    height = got.shape[0] // chips
    heights = (QW // chips, DI // chips, FFH // chips)
    for j in range(chips):
        block = slice(j * height, (j + 1) * height)
        first = pl.multiple_of(at[3] * got.shape[0] + j * height, height)
        keep = whole[pl.ds(first, height), :]
        for core in (0, 1):
            columns = slice(core * HALF, (core + 1) * HALF)
            both = jnp.where(at[3] == core, keep, got[block])
            mixed, fed = unfolded(both[:, :D]), unfolded(both[:, D:])
            attn[j * heights[0] : (j + 1) * heights[0], columns] = mixed[: heights[0]]
            rest[j * heights[1] : (j + 1) * heights[1], columns] = mixed[heights[0] :]
            down[j * heights[2] : (j + 1) * heights[2], columns] = fed


def sum_body(first, second, third, out):
    out[...] = first[...] + (second[...] + third[...])


def hand_body(first, second, third, out):
    out[...] = (first[...] + (second[...] + third[...])).astype(BF).astype(F32)


def pass_body(value, out):
    out[...] = value[...]


def split_body(at, rows_a, grad_a, rows_b, grad_b, send_a, keep_a, send_b, keep_b):
    depth, _, height, _ = send_a.shape
    for z in range(depth):
        for y in (0, 1):
            first = (2 * z + y) * 2 * height
            out = t_dot(rows_a[:, first : first + 2 * height], grad_a[...])
            low, high = out[:height], out[height:]
            send_a[z, y] = jnp.where(at[0] == 0, high, low).astype(BF)
            keep_a[z, y] = jnp.where(at[0] == 0, low, high).astype(BF)
        first = z * 4 * height
        out = t_dot(rows_b[:, first : first + 4 * height], grad_b[...])
        for x in (0, 1):
            low = out[x * height : (x + 1) * height]
            high = out[(x + 2) * height : (x + 3) * height]
            send_b[z, x] = jnp.where(at[1] == 0, high, low).astype(BF)
            keep_b[z, x] = jnp.where(at[1] == 0, low, high).astype(BF)


def columns_body(at, act, att, gated, grad_d, grad_m, keep_d, away_d, keep_m, away_m):
    chips = keep_d.shape[0]

    def put(keep, away, chip, first, rows):
        left, right = rows[:, :HALF], rows[:, HALF:]
        here = slice(first, first + rows.shape[0])
        keep[chip, here] = jnp.where(at[3] == 0, left, right).astype(BF)
        away[chip, here] = jnp.where(at[3] == 0, right, left).astype(BF)

    def product(rows, grad, chip):
        height = rows.shape[1] // chips
        return t_dot(rows[:, chip * height : (chip + 1) * height], grad[...])

    from_att = t_dot(att[...], grad_m[...])
    height = QW // chips
    for chip in range(chips):
        put(keep_d, away_d, chip, 0, product(act, grad_d, chip))
        put(keep_m, away_m, chip, 0, from_att[chip * height : (chip + 1) * height])
    from_gated = t_dot(gated[...], grad_m[...])
    tall = DI // chips
    for chip in range(chips):
        put(keep_m, away_m, chip, height, from_gated[chip * tall : (chip + 1) * tall])


def regroup_body(at, keep_d, got_d, keep_m, got_m, send_a, rest_a, send_b, rest_b):
    layers = send_a.shape[0] // 2
    for which, (down, mix) in enumerate(((keep_d, keep_m), (got_d, got_m))):
        core = at[3] if which == 0 else 1 - at[3]
        for z in range(layers):
            to = core * layers + z
            for k in (0, 1):
                low, high = down[4 * z + 2 * k], down[4 * z + 2 * k + 1]
                send_a[to, k] = jnp.where(at[0] == 0, high, low)
                rest_a[to, k] = jnp.where(at[0] == 0, low, high)
                low, high = mix[4 * z + k], mix[4 * z + 2 + k]
                send_b[to, k] = jnp.where(at[1] == 0, high, low)
                rest_b[to, k] = jnp.where(at[1] == 0, low, high)


def fold_body(at, keep_a, got_a, keep_b, got_b, send_a, rest_a, send_b, rest_b):
    for index, keep, got, send, rest in (
        (1, keep_a, got_a, send_a, rest_a),
        (0, keep_b, got_b, send_b, rest_b),
    ):
        for z in range(keep.shape[0]):
            low = keep[z, 0].astype(F32) + got[z, 0].astype(F32)
            high = keep[z, 1].astype(F32) + got[z, 1].astype(F32)
            send[z] = jnp.where(at[index] == 0, high, low).astype(BF)
            rest[z] = jnp.where(at[index] == 0, low, high).astype(BF)


def folded(rows, height):
    if rows.shape[0] == height:
        return rows
    return jnp.concatenate([rows[:height], rows[height:]], axis=1)


def unfolded(rows):
    half = rows.shape[1] // 2
    return jnp.concatenate([rows[:, :half], rows[:, half:]], axis=0)


def z_start_body(at, *refs):
    summands, (far, near) = refs[:-2], refs[-2:]
    height = far.shape[1]
    first = 0
    for one, two in zip(summands[::2], summands[1::2]):
        width = one.shape[1] * one.shape[2] // height
        for out, half in ((near, at[2] // 2), (far, 1 - at[2] // 2)):
            for j in (0, 1):
                total = one[2 * half + j].astype(F32) + two[2 * half + j].astype(F32)
                out[j, :, first : first + width] = folded(total, height).astype(BF)
        first += width


def z_across_body(far, got, out):
    for j in (0, 1):
        out[j] = (far[j].astype(F32) + got[j].astype(F32)).astype(BF)


def z_last_body(at, near, got, send, keep):
    low = near[0].astype(F32) + got[0].astype(F32)
    high = near[1].astype(F32) + got[1].astype(F32)
    even = at[2] % 2 == 0
    send[...] = jnp.where(even, high, low).astype(BF)
    keep[...] = jnp.where(even, low, high).astype(BF)


def choose_body(at, keep, got, keep_2, got_2, mine, away):
    one = keep[...].astype(F32) + got[...].astype(F32)
    two = keep_2[...].astype(F32) + got_2[...].astype(F32)
    mine[...] = jnp.where(at[3] == 0, one, two)
    away[...] = jnp.where(at[3] == 0, two, one)


def late_grads_body(at, mine, got, gate_up, down, attn, rest):
    height = attn.shape[0]
    for core in (0, 1):
        for k in (0, 1):
            to = (2 * k + core) * FFH
            from_ = slice(k * FFH, (k + 1) * FFH)
            gate_up[:, to : to + FFH] = jnp.where(at[3] == core, mine[:, from_], got[:, from_])
        here = slice(core * HALF, (core + 1) * HALF)
        from_ = slice(2 * FFH, 2 * FFH + 2 * HALF)
        down[:, here] = unfolded(jnp.where(at[3] == core, mine[:, from_], got[:, from_]))
        from_ = slice(2 * FFH + 2 * HALF, 2 * FFH + 4 * HALF)
        both = unfolded(jnp.where(at[3] == core, mine[:, from_], got[:, from_]))
        attn[:, here] = both[:height]
        rest[:, here] = both[height:]


def early_grads_body(at, mine, got, qkv, into, steps):
    halves_ = [jnp.where(at[3] == core, mine[...], got[...]) for core in (0, 1)]
    rest = [v[:, DI : DI + REST] for v in halves_]
    for core in (0, 1):
        qkv[:, core * QW : (core + 1) * QW] = rest[core][:, :QW]
        into[:, core * DI : (core + 1) * DI] = halves_[core][:, :DI]
        into[:, (2 + core) * DI : (3 + core) * DI] = halves_[core][:, DI + REST :]
    kv = [v[:, QW : QW + 2 * HEAD_SIZE] for v in rest]
    low = lanes(kv[0].shape) < HEAD_SIZE
    turned = [pltpu.roll(v, HEAD_SIZE, 1) for v in kv]
    qkv[:, 2 * QW : 2 * QW + 2 * HEAD_SIZE] = jnp.where(low, kv[0], turned[1])
    qkv[:, 2 * QW + 2 * HEAD_SIZE :] = jnp.where(low, turned[0], kv[1])
    bc_at = QW + 2 * HEAD_SIZE
    into[:, 4 * DI :] = rest[0][:, bc_at : bc_at + 2 * N] + rest[1][:, bc_at : bc_at + 2 * N]
    dt = [v[:, bc_at + 2 * N :] for v in rest]
    dt = [jnp.where(lanes(v.shape) < HEADS, v, 0.0) for v in dt]
    steps[...] = dt[0] + pltpu.roll(dt[1], HEADS, 1)


def weight_grad(operand, grad_rows):
    return lax.dot_general(
        operand, grad_rows, (((0,), (0,)), ((), ())), preferred_element_type=F32
    ).astype(BF)


def layer_forward(kernel, hidden, entering, rows_held, feeding, gains, taps, heads, tables):
    here = lax.axis_index("seq").astype(jnp.int32).reshape(1)
    count = lax.axis_size("seq")
    rows = hidden.shape[0]
    span = rows // 2
    cosine, sine = tables
    w_a, w_b = entering()
    normed, q, kv, raw, z, steps_raw = kernel(
        enter_body,
        [((rows, D), BF), ((rows, QW), BF), ((count, 2, span + 16, N), BF),
         ((rows, DI + 2 * N), BF), ((rows, DI), BF), ((rows, N), F32)],
        hidden, gains[0], w_a, w_b, cosine, sine, heads,
        flops=2 * rows * D * (w_a.shape[1] + w_b.shape[1]),
    )
    kv = to_all(kv)
    tails = raw.reshape(2, span, -1)[:, span - 16 :]
    edge = lax.ppermute(tails, "seq", [(k, k + 1) for k in range(count - 1)])
    w_attn, w_out, w_down = rows_held()
    y_local, c_low, states, running = kernel(
        local_body,
        [((rows, DI), F32), ((rows, N), BF), ((2 * DI, N), BF), ((rows, N), F32)],
        raw, edge, taps, steps_raw, heads, flops=2 * rows * span * DI * 4,
    )
    blocks = to_all(states.reshape(count, -1, N))
    att, logs = kernel(
        attend_body, [((rows, QW), BF), ((count, 2 * N), F32)], here * span, q, kv,
        flops=4 * rows * QW * 2 * count * span,
    )
    (carried,) = kernel(
        partial(chain_body, False), [(blocks.shape, BF)], here, blocks, logs, flops=blocks.size
    )
    carried = to_all(carried).reshape(2 * DI, N)
    y, gated, part = kernel(
        mix_body, [((rows, DI), F32), ((rows, DI), BF), ((rows, D), F32)],
        y_local, running, c_low, carried, z, att, w_attn, w_out, flops=4 * rows * D * D,
    )
    other = swap(part)
    w_gate, w_up = feeding()
    middle, normed_two, gate, up, act, more = kernel(
        feed_body,
        [((rows, D), F32), ((rows, D), BF), ((rows, FFH), F32), ((rows, FFH), F32),
         ((rows, FFH), BF), ((rows, D), F32)],
        hidden, part, other, gains[1], w_gate, w_up, w_down, flops=6 * rows * D * D,
    )
    kept = (
        hidden, normed, q, kv, logs, raw, edge, steps_raw, c_low, running, carried, y, z, att,
        gated, middle, normed_two, gate, up, act,
    )
    return (middle, more, swap(more)), kept, (w_a, w_b, w_attn, w_out, w_gate, w_up, w_down)


def layer_backward(
    kernel, grad_result, kept, weights, gains, taps, heads, tables, reduces, sums=None, owed=None
):
    (
        hidden, normed, q, kv, logs, raw, edge, steps_raw, c_low, running, carried, y, z, att,
        gated, middle, normed_two, gate, up, act,
    ) = kept
    w_a, w_b, w_attn, w_out, w_gate, w_up, w_down = weights
    here = lax.axis_index("seq").astype(jnp.int32).reshape(1)
    count = lax.axis_size("seq")
    rows = hidden.shape[0]
    span = rows // 2
    cosine, sine = tables
    z_a = w_a.shape[1] - REST
    low_down, dgate, dup, part = kernel(
        feed_back_body,
        [((rows, D), BF), ((rows, FFH), BF), ((rows, FFH), BF), ((rows, D), F32)],
        grad_result, gate, up, w_gate, w_up, w_down, flops=6 * rows * D * D,
    )
    other = swap(part)
    result = None
    if owed:
        owed["z"] = reduces.fold(owed["z"])
        late_1 = reduces.z_start(owed["feed"], owed["mixed"])
    else:
        (result,) = kernel(sum_body, [((rows, D), F32)], *sums)
    feed = reduces.open_plain(normed_two, dgate, normed_two, dup)
    if owed:
        reduces.settle(owed["z"])
    dmid, low, datt, dy, dz, into, dgain_two = kernel(
        mix_back_body,
        [((rows, D), F32), ((rows, D), BF), ((rows, QW), BF), ((rows, DI), F32), ((rows, DI), BF),
         ((2 * DI, N), BF), ((1, D), F32)],
        grad_result, part, other, middle, gains[1], w_attn, w_out, z, y, c_low, running,
        flops=4 * rows * D * D,
    )
    blocks = to_all(into.reshape(count, -1, N))
    columns = reduces.columns(act, att, gated, (low_down, low))
    if owed:
        owed["enter"] = reduces.fold(owed["enter"])
        late_1 = reduces.z_across(late_1)
    dq, dkv = kernel(
        attend_back_body, [((rows, QW), BF), ((count, 2, span, N), BF)],
        here * span, q, kv, datt, cosine, sine, flops=10 * rows * QW * 2 * count * span,
    )
    dkv = to_all(dkv)
    mixed = reduces.open_columns(columns)
    if owed:
        reduces.settle(owed["enter"])
    kernel.also(dkv)
    (later,) = kernel(
        partial(chain_body, True), [(blocks.shape, BF)], here, blocks, logs, flops=blocks.size
    )
    later = to_all(later).reshape(2 * DI, N)
    feed = reduces.fold(feed)
    if owed:
        late_1 = reduces.z_last(late_1)
        early_1 = reduces.z_start(owed["z"], owed["enter"])
    draw, dedge, dtaps, dsteps, dheads = kernel(
        scan_back_body,
        [((rows, DI + 2 * N), F32), ((2, 16, DI + 2 * N), BF), ((8, DI + 2 * N), F32),
         ((rows, N), BF), ((8, N), F32)],
        raw, edge, taps, steps_raw, heads, carried, later, dy, flops=20 * rows * span * DI,
    )
    dedge = lax.ppermute(dedge, "seq", [(k + 1, k) for k in range(count - 1)])
    mixed = reduces.fold(mixed)
    reduces.settle(feed)
    drest, dxs, part = kernel(
        enter_back_body, [((rows, REST), BF), ((rows, DI), BF), ((rows, D), F32)],
        draw, dedge, dq, dkv, dsteps, dz, cosine, sine, w_a, w_b,
        flops=2 * rows * D * (w_a.shape[1] + w_b.shape[1]),
    )
    other = swap(part)
    enter = reduces.open_plain(normed, drest, normed, dxs)
    if owed:
        early_1 = reduces.z_across(early_1)
    grad, dgain_one = kernel(
        leave_back_body, [((rows, D), F32), ((1, D), F32)],
        dmid, part, other, hidden, gains[0], flops=rows * D,
    )
    reduces.settle(mixed)
    gate_part = reduces.open_plain(normed, dz[:, :z_a], normed, dz[:, z_a:])
    if owed:
        early_1 = reduces.z_last(early_1)
        late = reduces.z_start(feed, mixed)
        enter = reduces.fold(enter)
        gate_part = reduces.fold(gate_part)
        late = reduces.z_across(late)
        early = reduces.z_start(gate_part, enter)
        late = reduces.z_last(late)
        early = reduces.z_across(early)
        late = reduces.own(late, late_1)
        early = reduces.z_last(early)
        states = {"late": late, "early": reduces.own(early, early_1)}
    else:
        states = {"feed": feed, "mixed": mixed, "z": gate_part, "enter": enter, "result": result}
    small = (
        jnp.concatenate([dgain_one, dgain_two], axis=0), dtaps[: CONV + 1], dheads[:3, :HEADS]
    )
    return grad, states, small


def halves(array, sizes, at):
    out = []
    for core in (0, 1):
        parts, start = [], at
        for width in sizes:
            half = width // 2
            parts.append(array[:, start + core * half : start + (core + 1) * half])
            start += width
        out.append(parts)
    return out


def rotation_tables(positions):
    half = HEAD_SIZE // 2
    frequency = ROPE_BASE ** (-jnp.arange(half, dtype=F32) / half)
    angles = positions.astype(F32)[:, None] * frequency[None, :]
    cosine, sine = jnp.cos(angles), jnp.sin(angles)
    still = jnp.zeros((positions.shape[0], HEAD_SIZE), F32)
    cosine = jnp.tile(jnp.concatenate([cosine, cosine], axis=1), (1, QH + 1))
    sine = jnp.tile(jnp.concatenate([-sine, sine], axis=1), (1, QH + 1))
    return (
        jnp.tile(jnp.concatenate([cosine, still + 1.0], axis=1), (2, 1)),
        jnp.tile(jnp.concatenate([sine, still], axis=1), (2, 1)),
    )


def columns_home(whole):
    first = lax.axis_index("section") == 0
    blocks = whole.reshape(lax.axis_size("seq") // 2, -1, D)
    left, right = blocks[..., :HALF], blocks[..., HALF:]
    keep = jnp.where(first, left, right)
    got = swap(jnp.where(first, right, left))
    return jnp.concatenate([jnp.where(first, keep, got), jnp.where(first, got, keep)], axis=0)


def by_chip(whole):
    return whole.reshape(lax.axis_size("seq"), -1, whole.shape[1])


NAMES = ("first", "second", "mix", "down", "gate", "up")


def per_device(
    boundary, lengths, norm_gains, w_qkv, w_attn, w_in, w_dt, conv_params, head_params, w_out, w_gate_up, w_down,
):
    core = lax.axis_index("section")
    here = lax.axis_index("seq")
    count = lax.axis_size("seq")
    first = core == 0
    span = boundary.shape[2]
    rows = 2 * span

    qkv = halves(w_qkv[0], (QW * 2, 2 * HEAD_SIZE, 2 * HEAD_SIZE), 0)
    into = halves(w_in[0], (2 * DI, 2 * DI), 0)
    both_bc = w_in[0][:, 4 * DI :]
    steps = halves(w_dt[0], (SH,), 0)
    ups = halves(w_gate_up[0], (2 * FFH, 2 * FFH), 0)
    mix = jnp.concatenate([w_attn[0], w_out[0]], axis=0)
    cut = []
    for k in (0, 1):
        step = jnp.pad(steps[k][0], ((0, 0), (0, N - HEADS)))
        z_k = into[k][0]
        z_a = z_k.shape[1] // 2
        cut.append(
            {
                "first": jnp.concatenate(qkv[k] + [both_bc, step, z_k[:, :z_a]], axis=1),
                "second": jnp.concatenate([z_k[:, z_a:], into[k][1]], axis=1),
                "mix": mix[:, k * HALF : (k + 1) * HALF],
                "gate": ups[k][0],
                "up": ups[k][1],
                "down": w_down[0][:, k * HALF : (k + 1) * HALF],
            }
        )
    layers = ({}, {})
    for name in NAMES:
        own = jnp.where(first, cut[0][name], cut[1][name])
        got = swap(jnp.where(first, cut[1][name], cut[0][name]))
        layers[0][name] = jnp.where(first, own, got)
        layers[1][name] = jnp.where(first, got, own)

    kernel = Order()
    gathers = Gathers([(layers[0]["first"], layers[0]["second"])], kernel)
    rest_0 = Whole(layers[0], kernel, NAMES[2:])
    all_1 = Whole(layers[1], kernel, NAMES)
    rest_0.start()
    all_1.start()
    small = jnp.concatenate([norm_gains[0].reshape(-1), conv_params[0].reshape(-1)])
    small_other = swap(small)
    small = jnp.stack([jnp.where(first, small, small_other), jnp.where(first, small_other, small)])
    small = to_all(jnp.broadcast_to(small[None], (count,) + small.shape))
    small = small.swapaxes(0, 1).astype(F32)
    width = norm_gains.shape[2]
    gains = small[:, :, : 2 * width].reshape(2, count, 2, width).swapaxes(1, 2).reshape(2, 2, D)
    taps = small[:, :, 2 * width :].reshape(2, count, CONV + 1, -1).swapaxes(1, 2)
    taps = taps.reshape(2, CONV + 1, 4 * DI // 2 + 2 * N)
    taps = jnp.concatenate(
        [jnp.where(first, taps[..., :DI], taps[..., DI : 2 * DI]), taps[..., 2 * DI :]], axis=-1
    )
    heads_other = swap(head_params[0])
    heads = jnp.stack(
        [
            jnp.where(first, head_params[0], heads_other),
            jnp.where(first, heads_other, head_params[0]),
        ]
    )
    heads = jnp.where(first, heads[..., :HEADS], heads[..., HEADS:])
    heads = jnp.pad(heads, ((0, 0), (0, 5), (0, N - HEADS)))
    gains = gains.reshape(2, 2, 1, D)
    taps = jnp.pad(taps, ((0, 0), (0, 8 - CONV - 1), (0, 0)))

    other = swap(boundary[0])
    inputs = jnp.where(first, boundary[0], other).reshape(rows, D).astype(F32)
    positions = here * span + jnp.arange(span, dtype=jnp.int32)
    live = (positions[None, :] < lengths[:, None]).astype(F32)
    cotangent = jnp.where(first, other, boundary[0]).astype(F32) * live[..., None]
    cotangent = cotangent.reshape(rows, D)
    tables = rotation_tables(positions)

    reduces = Reduces(kernel)
    def pair(whole, one, two):
        return lambda: (whole.part(one), whole.part(two))

    sums, kept_0, weights_0 = layer_forward(
        kernel, inputs, lambda: gathers.get(0), rest_0.rows, pair(rest_0, "gate", "up"),
        gains[0], taps[0], heads[0], tables,
    )
    (handed,) = kernel(hand_body, [((rows, D), F32)], *sums)
    sums, kept_1, weights_1 = layer_forward(
        kernel, handed, pair(all_1, "first", "second"), all_1.rows, pair(all_1, "gate", "up"),
        gains[1], taps[1], heads[1], tables,
    )
    kernel.weight = WEIGHT
    grad_handed, grads_1, small_1 = layer_backward(
        kernel, cotangent, kept_1, weights_1, gains[1], taps[1], heads[1], tables, reduces, sums
    )
    grad_inputs, grads_0, small_0 = layer_backward(
        kernel, grad_handed.astype(BF).astype(F32),
        kept_0, weights_0, gains[0], taps[0], heads[0], tables, reduces, owed=grads_1,
    )

    at = corner()
    height = w_qkv.shape[1]
    grad_gu, grad_down, grad_attn, grad_out = kernel(
        late_grads_body,
        [(v.shape[1:], F32) for v in (w_gate_up, w_down, w_attn, w_out)], at, *grads_0["late"],
    )
    grad_qkv, grad_in, grad_dt = kernel(
        early_grads_body,
        [((height, w_qkv.shape[2]), F32), ((height, w_in.shape[2]), F32), ((height, N), F32)],
        at, *grads_0["early"],
    )

    conv_width = conv_params.shape[2]

    grad_gains, grad_taps, grad_heads = (jnp.stack(v) for v in zip(small_0, small_1))
    xs_part, none = grad_taps[..., :DI], jnp.zeros((2, CONV + 1, DI), F32)
    wide = jnp.concatenate(
        [jnp.where(first, xs_part, none), jnp.where(first, none, xs_part), grad_taps[..., DI:]],
        axis=2,
    )
    none = jnp.zeros((2, 3, HEADS), F32)
    head_wide = jnp.concatenate(
        [jnp.where(first, grad_heads, none), jnp.where(first, none, grad_heads)], axis=2
    )
    gains_once = jnp.where(first, grad_gains, 0.0)
    flat = jnp.concatenate(
        [
            gains_once.reshape(2, 2, count, width).transpose(2, 0, 1, 3).reshape(count, 2, -1),
            wide.reshape(2, CONV + 1, count, conv_width)
            .transpose(2, 0, 1, 3)
            .reshape(count, 2, -1),
            jnp.broadcast_to(head_wide.reshape(1, 2, -1), (count, 2, 3 * SH)),
        ],
        axis=2,
    )
    flat = jnp.pad(flat, ((0, 0), (0, 0), (0, -flat.shape[2] % N)))
    flat = jnp.sum(to_all(flat), axis=0)
    flat = jnp.where(first, flat[0], flat[1]) + swap(jnp.where(first, flat[1], flat[0]))
    taps_at = 2 * width
    heads_at = taps_at + (CONV + 1) * conv_width
    grad_gains = flat[:taps_at].reshape(2, width)
    grad_conv = flat[taps_at:heads_at].reshape(CONV + 1, conv_width)
    total_heads = flat[heads_at : heads_at + 3 * SH].reshape(3, SH)

    ends = jnp.where(first, grad_inputs, grads_1["result"]).reshape(2, span, D)
    outs = (
        ends, grad_gains, grad_qkv, grad_attn, grad_in, grad_dt[:, :SH], grad_conv, total_heads,
        grad_out, grad_gu, grad_down,
    )
    return tuple(out[None] for out in outs)


def solution(mesh):
    by_rows = P("section", "seq", None)
    by_columns = P("section", None, "seq")
    whole = P("section", None, None)
    ends = P("section", None, "seq", None)
    in_specs = (
        ends, P(), by_columns, by_rows, by_rows, by_rows, by_rows, by_columns, whole, by_rows,
        by_rows, by_rows,
    )
    out_specs = (
        ends, by_columns, by_rows, by_rows, by_rows, by_rows, by_columns, whole, by_rows, by_rows,
        by_rows,
    )
    return jax.shard_map(
        per_device, mesh=mesh, in_specs=in_specs, out_specs=out_specs, check_vma=False
    )
```

```python
from functools import partial
from math import isqrt

import jax
import jax.numpy as jnp
from jax import lax
from jax.experimental import pallas as pl
from jax.experimental.pallas import tpu as pltpu
from jax.sharding import PartitionSpec as P

D = 1024
HEAD_SIZE = 64
SH = 24
P_SIZE = 64
N = 128
CONV = 4
QH = 4
HEADS = SH // 2
QW = QH * HEAD_SIZE
DI = HEADS * P_SIZE
FFH = 1024
HALF = D // 2
REST = QW + 2 * HEAD_SIZE + 2 * N + N

eps = 1e-05
ROPE_BASE = 100000000000.0
HIGHEST = lax.Precision.HIGHEST
BF = jnp.bfloat16
F32 = jnp.float32
VMEM_BYTES = 56 * 2**20
WEIGHT = 3 * 10**11


def grid_of(count):
    side = isqrt(count // 4)
    return (count // (side * side), side, side)


def place_on(axis):
    dims = grid_of(lax.axis_size("seq"))
    strides = (dims[1] * dims[2], dims[2], 1)
    return lax.axis_index("seq") // strides[axis] % dims[axis], dims[axis], strides[axis]


def hop(value, axis, moves):
    count = lax.axis_size("seq")
    _, length, stride = place_on(axis)
    pairs = []
    for source in range(count):
        at = source // stride % length
        if at in moves and moves[at] < length:
            pairs.append((source, source + (moves[at] - at) * stride))
    return lax.ppermute(value, "seq", pairs)


NEXT = {0: 1, 1: 0, 2: 3, 3: 2}
INNER = {1: 2, 2: 1}
OUTWARD = {1: 0, 2: 3}
INWARD = {0: 1, 3: 2}


def swap(value):
    return lax.ppermute(value, "section", [(0, 1), (1, 0)])


def both_cores(value):
    return value + swap(value)


def line_gather(part, axis, dim):
    at, length, _ = place_on(axis)
    got = hop(part, axis, NEXT)
    even = at % 2 == 0
    pair = jnp.stack([jnp.where(even, part, got), jnp.where(even, got, part)], axis=dim)
    if length == 2:
        return pair
    over = hop(pair, axis, INNER)
    rest = hop(over, axis, OUTWARD)
    far = jnp.where((at == 1) | (at == 2), over, rest)
    return jnp.concatenate(
        [jnp.where(at < 2, pair, far), jnp.where(at < 2, far, pair)], axis=dim
    )


def corner():
    places = [place_on(axis)[0] for axis in (2, 1, 0)]
    return jnp.stack(places + [lax.axis_index("section")]).astype(jnp.int32)


class Gathers:
    def __init__(self, pairs, kernel):
        self.pairs, self.kernel = pairs, kernel
        self.count = lax.axis_size("seq")
        self.depth, self.side, _ = grid_of(self.count)
        self.state = [None] * len(pairs)
        self.steps = [(step, k) for k in range(len(pairs)) for step in (1, 2, 3, 4, 5)]
        self.place = corner()
        self.start(0)

    def start(self, at):
        if at < len(self.pairs):
            stacked = jnp.stack(self.pairs[at])
            self.state[at] = (stacked, hop(stacked, 0, NEXT))

    def until(self, step, at):
        while (step, at) in self.steps:
            now, pair = self.steps.pop(0)
            getattr(self, "step_%d" % now)(pair)

    def step_1(self, at):
        own, got = self.state[at]
        (pair,) = self.kernel(in_order_body, [((2,) + own.shape, BF)], self.place, own, got)
        self.state[at] = (pair, hop(pair, 0, INNER))

    def step_2(self, at):
        pair, over = self.state[at]
        self.kernel.also(over)
        self.state[at] = (pair, over, hop(over, 0, OUTWARD))

    def step_3(self, at):
        pair = self.state[at][0]
        shape = (4,) + pair.shape[2:]
        first, second = self.kernel(line_body, [(shape, BF)] * 2, self.place, *self.state[at])
        if self.side == 2:
            self.state[at] = (first, hop(first, 1, NEXT), second, hop(second, 2, NEXT))
        else:
            self.state[at] = (line_gather(first, 1, 1), line_gather(second, 2, 1))

    def step_4(self, at):
        if self.side == 2:
            first = self.state[at][0]
            shape = (4, 2) + first.shape[1:]
            shape_b = (4, 2) + self.state[at][2].shape[1:]
            first, second = self.kernel(
                first_move_body, [(shape, BF), (shape_b, BF)], self.place, *self.state[at]
            )
            self.state[at] = (first, hop(first, 2, NEXT), second, hop(second, 1, NEXT))
        else:
            first, second = self.state[at]
            self.state[at] = (line_gather(first, 2, 2), line_gather(second, 1, 1))
        self.start(at + 1)

    def step_5(self, at):
        if self.side != 2:
            self.state[at] = [v.reshape(D, -1) for v in self.state[at]]
            return
        shapes = [(self.count,) + self.state[at][k].shape[2:] for k in (0, 2)]
        first, second = self.kernel(
            second_move_body, [(v, BF) for v in shapes], self.place, *self.state[at]
        )
        self.state[at] = [first.reshape(D, -1), second.reshape(D, -1)]

    def get(self, at):
        self.until(5, at)
        return self.state[at]


class Whole:
    def __init__(self, shards, kernel, names):
        height = shards["gate"].shape[0]
        self.kernel, self.at = kernel, {}
        parts, first = [], 0
        for name in names:
            shard = shards[name]
            part = jnp.concatenate(
                [shard[k : k + height] for k in range(0, shard.shape[0], height)], axis=1
            )
            parts.append(part)
            self.at[name] = (first, part.shape[1])
            first += part.shape[1]
        self.flat = jnp.concatenate(parts, axis=1)

    def start(self):
        self.whole = lax.all_gather(self.flat, "seq", axis=0, tiled=True)

    def part(self, name):
        return Part(self.whole, *self.at[name])

    def rows(self):
        part = Part(self.whole, self.at["mix"][0], 2 * D)
        (away,) = self.kernel(cut_body, [((part.shape[0] // 2, 2 * D), BF)], corner(), part)
        return self.kernel(
            partial(rows_body, lax.axis_size("seq") // 2),
            [((QW, D), BF), ((DI, D), BF), ((FFH, D), BF)], corner(), part, swap(away),
        )


def add(a, b, kind):
    return (a.astype(F32) + b.astype(F32)).astype(kind)


def line_reduce(parts, axis, dim):
    at, length, _ = place_on(axis)

    def pick(array, index):
        return lax.dynamic_index_in_dim(array, index, dim, False)

    if length == 4:
        halves = parts.reshape(parts.shape[:dim] + (2, 2) + parts.shape[dim + 1 :])
        far, near = pick(halves, 1 - at // 2), pick(halves, at // 2)
        far = add(far, hop(far, axis, INWARD), BF)
        parts = add(near, hop(far, axis, INNER), BF)
    got = hop(pick(parts, 1 - at % 2), axis, NEXT)
    return pick(parts, at % 2), got


def z_groups():
    count = lax.axis_size("seq")
    depth, side, _ = grid_of(count)
    plane = side * side
    return [[z * plane + k for z in range(depth)] for k in range(plane)]


class Reduces:
    def __init__(self, kernel):
        self.kernel = kernel
        self.paired = grid_of(lax.axis_size("seq"))[2] == 2

    def open_plain(self, rows_a, grad_a, rows_b, grad_b, *column):
        count = lax.axis_size("seq")
        depth = grid_of(count)[0]
        if not self.paired:
            first = weight_grad(rows_a, grad_a)
            for v in column:
                first = first.at[:, -1].add(v[0])
            return self.open_whole(by_chip(first), by_chip(weight_grad(rows_b, grad_b)))
        height = rows_a.shape[1] // count
        shape = (depth, 2, height, grad_a.shape[1])
        parts = self.kernel(
            split_body, [(shape, BF)] * 4, corner(), rows_a, grad_a, rows_b, grad_b, *column,
            flops=4 * rows_a.size * grad_a.shape[1],
        )
        return self.open(parts)

    def columns(self, act, att, gated, grad):
        half = lax.axis_size("seq") // 2
        if not self.paired:
            mix = jnp.concatenate(
                [weight_grad(v, grad[1]).reshape(half, -1, D) for v in (att, gated)], axis=1
            )
            return columns_home(weight_grad(act, grad[0])), columns_home(mix)
        down, mix = (half, FFH // half, HALF), (half, (QW + DI) // half, HALF)
        keep_d, away_d, keep_m, away_m = self.kernel(
            columns_body, [(down, BF), (down, BF), (mix, BF), (mix, BF)],
            corner(), act, att, gated, *grad, flops=4 * act.size * D,
        )
        return keep_d, swap(away_d), keep_m, swap(away_m)

    def open_columns(self, columns):
        if not self.paired:
            return self.open_whole(*columns)
        depth = grid_of(lax.axis_size("seq"))[0]
        shapes = [((depth, 2) + columns[k].shape[1:], BF) for k in range(4)]
        return self.open(self.kernel(regroup_body, shapes, corner(), *columns))

    def open(self, parts):
        send_a, keep_a, send_b, keep_b = parts
        got_a, got_b = hop(send_a, 2, NEXT), hop(send_b, 1, NEXT)
        return keep_a, got_a, keep_b, got_b

    def open_whole(self, first, second):
        dims = grid_of(lax.axis_size("seq"))
        first, second = (v.reshape(dims + v.shape[1:]) for v in (first, second))
        keep_a, got_a = line_reduce(first, 2, 2)
        keep_b, got_b = line_reduce(second, 1, 1)
        return keep_a, got_a, keep_b, got_b

    def fold(self, state):
        keep_a, got_a, keep_b, got_b = state
        if not self.paired:
            first, second = add(keep_a, got_a, BF), add(keep_b, got_b, BF)
            return *line_reduce(first, 1, 1), *line_reduce(second, 2, 1)
        shape = keep_a.shape[:1] + keep_a.shape[2:]
        shape_b = keep_b.shape[:1] + keep_b.shape[2:]
        send_a, keep_a, send_b, keep_b = self.kernel(
            fold_body, [(shape, BF), (shape, BF), (shape_b, BF), (shape_b, BF)],
            corner(), keep_a, got_a, keep_b, got_b,
        )
        return keep_a, hop(send_a, 1, NEXT), keep_b, hop(send_b, 2, NEXT)

    def settle(self, state):
        self.kernel.also(state[1])
        self.kernel.also(state[3])

    def flat(self, state):
        height = D // lax.axis_size("seq")
        return height, sum(v.shape[1] * v.shape[2] // height for v in (state[0], state[2]))

    def z_start(self, *states):
        height = self.flat(states[0])[0]
        shape = (2, height, sum(self.flat(v)[1] for v in states))
        far, near = self.kernel(
            z_start_body, [(shape, BF)] * 2, corner(), *[v for state in states for v in state]
        )
        return far, hop(far, 0, INWARD), near

    def z_across(self, state):
        far, got, near = state
        (far,) = self.kernel(z_across_body, [(far.shape, BF)], far, got)
        return near, hop(far, 0, INNER)

    def z_last(self, state):
        near, got = state
        shape = near.shape[1:]
        send, keep = self.kernel(z_last_body, [(shape, BF)] * 2, corner(), near, got)
        return keep, hop(send, 0, NEXT)

    def z_once(self, *states):
        height = self.flat(states[0])[0]
        shape = (states[0][0].shape[0], height, sum(self.flat(v)[1] for v in states))
        (whole,) = self.kernel(add_body, [(shape, BF)], *[v for state in states for v in state])
        whole = lax.all_to_all(whole, "seq", 0, 0, tiled=True, axis_index_groups=z_groups())
        return (whole,)

    def own(self, first, second):
        shape = second[0].shape
        mine, away = self.kernel(choose_body, [(shape, F32)] * 2, corner(), *first, *second)
        return mine, swap(away)


def to_all(blocks):
    return lax.all_to_all(blocks, "seq", 0, 0, tiled=True)


class Part:
    def __init__(self, whole, first, width):
        self.whole, self.first = whole, first
        self.shape, self.dtype = (whole.shape[0], width), whole.dtype


class Order:
    def __init__(self):
        self.before = []
        self.weight = 5 * 10**9

    def also(self, value):
        self.before = self.before + [value]

    def __call__(self, body, outs, *args, flops=0):
        out_shape = [jax.ShapeDtypeStruct(shape, kind) for shape, kind in outs]
        count, extra = len(args), len(self.before)
        parts = [k for k, v in enumerate(args) if isinstance(v, Part)]

        def run(*refs):
            given = list(refs[:count])
            results = refs[count + extra : count + extra + len(outs)]
            scratch = refs[count + extra + len(outs) :]
            copies = []
            for slot, k in enumerate(parts):
                source = given[k].at[:, args[k].first : args[k].first + args[k].shape[1]]
                copies.append(pltpu.make_async_copy(source, scratch[slot], scratch[-1].at[slot]))
                copies[-1].start()
                given[k] = scratch[slot]
            for copy in copies:
                copy.wait()
            body(*given, *results)

        def space(v):
            if isinstance(v, Part):
                return pl.ANY
            return pltpu.SMEM if v.dtype == jnp.int32 else pltpu.VMEM

        scratch = [pltpu.VMEM(args[k].shape, args[k].dtype) for k in parts]
        if parts:
            scratch.append(pltpu.SemaphoreType.DMA((len(parts),)))
        results = pl.pallas_call(
            run,
            out_shape=out_shape,
            in_specs=[pl.BlockSpec(memory_space=space(v)) for v in args]
            + [pl.BlockSpec(memory_space=pl.ANY)] * extra,
            out_specs=[pl.BlockSpec(memory_space=pltpu.VMEM) for _ in outs],
            scratch_shapes=scratch,
            compiler_params=pltpu.CompilerParams(vmem_limit_bytes=VMEM_BYTES),
            cost_estimate=pl.CostEstimate(flops=self.weight, bytes_accessed=0, transcendentals=0),
        )(*[v.whole if isinstance(v, Part) else v for v in args], *self.before)
        self.before = [min(results, key=lambda v: v.size)]
        return results


def dot(a, b, precision=None):
    return jnp.dot(a, b, preferred_element_type=F32, precision=precision)


def dot_t(a, b, precision=None):
    return lax.dot_general(
        a, b, (((1,), (1,)), ((), ())), preferred_element_type=F32, precision=precision
    )


def t_dot(a, b, precision=None):
    return lax.dot_general(
        a, b, (((0,), (0,)), ((), ())), preferred_element_type=F32, precision=precision
    )


def sigmoid(v):
    return 1.0 / (1.0 + jnp.exp(-v))


def softplus(v):
    return jnp.maximum(v, 0.0) + jnp.log1p(jnp.exp(-jnp.abs(v)))


def lanes(shape):
    return lax.broadcasted_iota(jnp.int32, shape, len(shape) - 1)


def rows_of(shape):
    return lax.broadcasted_iota(jnp.int32, shape, len(shape) - 2)


def rotate(rows, cosine, sine):
    width = rows.shape[-1]
    half = HEAD_SIZE // 2
    low = (lanes(rows.shape) // half) % 2 == 0
    turned = jnp.where(
        low, pltpu.roll(rows, width - half, 1), pltpu.roll(rows, half, 1)
    )
    return rows * cosine + turned * sine


def inverse_rms(rows):
    return lax.rsqrt(jnp.mean(rows * rows, axis=-1, keepdims=True) + eps)


def rms_back(grad, rows, gain):
    scale = inverse_rms(rows)
    scaled = grad * gain
    inner = jnp.mean(rows * scaled, axis=-1, keepdims=True)
    return (
        scale * scaled - rows * (scale * scale * scale * inner),
        jnp.sum(grad * rows * scale, axis=0, keepdims=True),
    )


def pair_wide(columns, pair):
    shape = (columns.shape[0], 2 * P_SIZE)
    return jnp.where(
        lanes(shape) < P_SIZE,
        jnp.broadcast_to(columns[:, 2 * pair : 2 * pair + 1], shape),
        jnp.broadcast_to(columns[:, 2 * pair + 1 : 2 * pair + 2], shape),
    )


def block(pair):
    return slice(2 * P_SIZE * pair, 2 * P_SIZE * (pair + 1))


def convolved(raw, edge, taps):
    span = raw.shape[0]
    extended = jnp.concatenate([edge.astype(F32), raw.astype(F32)], axis=0)
    at = edge.shape[0] - (CONV - 1)
    summed = jnp.broadcast_to(taps[CONV : CONV + 1], raw.shape)
    for k in range(CONV):
        summed = summed + taps[k : k + 1] * extended[at + k : at + k + span]
    return extended, summed


def decay_of(steps_raw, heads):
    span = steps_raw.shape[0]
    steps = softplus(steps_raw)
    logs = -steps * jnp.exp(heads[1:2])
    square = (span, span)
    lower = (lanes(square) <= rows_of(square)).astype(F32)
    upper = (lanes(square) >= rows_of(square)).astype(F32)
    return steps, logs, dot(lower, logs, HIGHEST), t_dot(logs, upper, HIGHEST)


def decays_between(running, running_t, head):
    span = running.shape[0]
    gap = running[:, head : head + 1] - running_t[head : head + 1, :]
    square = (span, span)
    return jnp.exp(jnp.where(lanes(square) <= rows_of(square), gap, -1e30))


def enter_body(
    hidden, gain, w_a, w_b, cosine, sine, heads, normed_o, q_o, kv_o, raw_o, z_o, steps_o
):
    rows = hidden[...]
    normed = (rows * inverse_rms(rows) * gain[...]).astype(BF)
    normed_o[...] = normed
    a, b = dot(normed, w_a[...]), dot(normed, w_b[...])
    turned = rotate(a[:, : QW + 2 * HEAD_SIZE], cosine[...], sine[...])
    q_o[...] = turned[:, :QW].astype(BF)
    kv = turned[:, QW:].astype(BF)
    bc_at = QW + 2 * HEAD_SIZE
    z_a = w_a.shape[1] - REST
    z_o[:, :z_a] = a[:, REST:].astype(BF)
    z_o[:, z_a:] = b[:, : DI - z_a].astype(BF)
    raw_o[:, :DI] = b[:, DI - z_a :].astype(BF)
    raw_o[:, DI:] = a[:, bc_at : bc_at + 2 * N].astype(BF)
    steps_raw = a[:, bc_at + 2 * N : REST] + heads[0:1]
    steps_o[...] = steps_raw
    logs = -softplus(steps_raw) * jnp.exp(heads[1:2])
    span = rows.shape[0] // 2
    for s in (0, 1):
        total = jnp.sum(logs[s * span : (s + 1) * span], axis=0, keepdims=True)
        high = total.astype(BF).astype(F32)
        middle = (total - high).astype(BF).astype(F32)
        low = total - high - middle
        at = rows_of((16, N))
        packed = jnp.where(
            at == 0, high, jnp.where(at == 1, middle, jnp.where(at == 2, low, 0.0))
        ).astype(BF)
        for chip in range(kv_o.shape[0]):
            kv_o[chip, s, :span] = kv[s * span : (s + 1) * span]
            kv_o[chip, s, span:] = packed


def local_body(raw, edge, taps, steps_raw, heads, y_o, c_o, state_o, running_o):
    span = raw.shape[0] // 2
    for s in (0, 1):
        at = slice(s * span, (s + 1) * span)
        _, summed = convolved(raw[at], edge[s], taps[...])
        conv = summed * sigmoid(summed)
        steps, _, running, running_t = decay_of(steps_raw[at], heads[...])
        running_o[at] = running
        b_low, c_low = conv[:, DI : DI + N].astype(BF), conv[:, DI + N :].astype(BF)
        c_o[at] = c_low
        inner = dot_t(c_low, b_low)
        tail = jnp.exp(running[span - 1 : span] - running)
        low_half = lanes((span, 2 * P_SIZE)) < P_SIZE
        for pair in range(HEADS // 2):
            xs = conv[:, block(pair)]
            dt_x = xs * pair_wide(steps, pair)
            dt_low = dt_x.astype(BF)
            mixed = [
                dot((inner * decays_between(running, running_t, h)).astype(BF), dt_low)
                for h in (2 * pair, 2 * pair + 1)
            ]
            skip = pair_wide(heads[2:3], pair)
            y_o[at, block(pair)] = jnp.where(low_half, mixed[0], mixed[1]) + skip * xs
            end = t_dot((dt_x * pair_wide(tail, pair)).astype(BF), b_low)
            state_o[s * DI + 2 * P_SIZE * pair : s * DI + 2 * P_SIZE * (pair + 1)] = end.astype(BF)


def head_rows(rows, head, upper):
    half = rows[:, block(head // 2)].astype(F32)
    if (head % 2 == 1) != upper:
        half = pltpu.roll(half, P_SIZE, 1)
    keep = lanes(half.shape) >= P_SIZE if upper else lanes(half.shape) < P_SIZE
    return jnp.where(keep, half, 0.0)


def heads_joined(parts, upper):
    out = []
    for even, odd in zip(parts[::2], parts[1::2]):
        low_half = lanes(even.shape) < P_SIZE
        if upper:
            out.append(jnp.where(low_half, pltpu.roll(even, P_SIZE, 1), odd))
        else:
            out.append(jnp.where(low_half, even, pltpu.roll(odd, P_SIZE, 1)))
    return jnp.concatenate(out, axis=1)


def head_groups(chips):
    size = QH if chips <= 16 else 1
    return [list(range(k, k + size)) for k in range(0, QH, size)]


def probabilities(queries, keys, first_row, span):
    scores = dot_t(queries, keys) * HEAD_SIZE ** (-0.5)
    shape = (span, keys.shape[0])
    allowed = lanes(shape) <= rows_of(shape) + first_row
    bias = jnp.where(allowed, 0.0, -1e30)
    scores = scores + jnp.concatenate([bias] * (queries.shape[0] // span), axis=0)
    shifted = jnp.exp(scores - jnp.max(scores, axis=-1, keepdims=True))
    return shifted / jnp.sum(shifted, axis=-1, keepdims=True)


def attend_body(first_row, q, kv, att_o, logs_o):
    chips, _, height, _ = kv.shape
    span = q.shape[0] // 2
    for s in (0, 1):
        keys = kv[:, s, :span].reshape(chips * span, 2 * HEAD_SIZE)
        parts = []
        for group in head_groups(chips):
            rows = [head_rows(q[s * span : (s + 1) * span], h, False) for h in group]
            rows = jnp.concatenate(rows, axis=0).astype(BF)
            prob = probabilities(rows, keys, first_row[0], span)
            out = dot(prob.astype(BF), keys)
            parts += [out[k * span : (k + 1) * span] for k in range(len(group))]
        att_o[s * span : (s + 1) * span] = heads_joined(parts, True).astype(BF)
        for chip in range(chips):
            logs = kv[chip, s, span:height].astype(F32)
            logs_o[chip : chip + 1, s * N : (s + 1) * N] = jnp.sum(logs, axis=0, keepdims=True)


def decay_columns(here, logs, chips, rows):
    shape = (rows, 2 * N)
    head = lax.shift_right_logical(rows_of(shape) + here[0] * rows, 6)
    column = jnp.where(head >= HEADS, head + (N - HEADS), head)
    chosen = (lanes(shape) == column).astype(F32)
    return jnp.exp(dot_t(chosen, logs[...], HIGHEST))


def chain_body(here, blocks, logs, out):
    chips, rows, _ = blocks.shape
    decay = decay_columns(here, logs, chips, rows)
    carry = jnp.zeros((rows, N), F32)
    for chip in range(chips):
        out[chip] = carry.astype(BF)
        carry = decay[:, chip : chip + 1] * carry + blocks[chip].astype(F32)


def chain_back_body(here, blocks, logs, dkv, out):
    chips, rows, _ = blocks.shape
    span = dkv.shape[2]
    decay = decay_columns(here, logs, chips, rows)
    carry = jnp.zeros((rows, N), F32)
    for chip in reversed(range(chips)):
        out[chip, 2 * span :] = carry.astype(BF)
        carry = decay[:, chip : chip + 1] * carry + blocks[chip].astype(F32)
        for s in (0, 1):
            out[chip, s * span : (s + 1) * span] = dkv[chip, s]


def mix_body(y_in, running, c_low, carried, z, att, w_attn, w_out, y_o, g_o, part_o):
    span = y_in.shape[0] // 2
    for s in (0, 1):
        at = slice(s * span, (s + 1) * span)
        from_state = dot_t(c_low[at], carried[s * DI : (s + 1) * DI])
        grown = jnp.exp(running[at])
        for pair in range(HEADS // 2):
            y_o[at, block(pair)] = (
                y_in[at, block(pair)] + from_state[:, block(pair)] * pair_wide(grown, pair)
            )
    gate = z[...].astype(F32)
    gated = (y_o[...] * (gate * sigmoid(gate))).astype(BF)
    g_o[...] = gated
    part_o[...] = dot(att[...], w_attn[...]) + dot(gated, w_out[...])


def feed_body(
    hidden, part, other, gain, w_gate, w_up, w_down, mid_o, normed_o, gate_o, up_o, act_o, part_o
):
    middle = hidden[...] + (part[...] + other[...])
    mid_o[...] = middle
    normed = (middle * inverse_rms(middle) * gain[...]).astype(BF)
    normed_o[...] = normed
    gate, up = dot(normed, w_gate[...]), dot(normed, w_up[...])
    gate_o[...] = gate
    up_o[...] = up
    act = (gate * sigmoid(gate) * up).astype(BF)
    act_o[...] = act
    part_o[...] = dot(act, w_down[...])


def feed_back_body(grad, gate, up, w_gate, w_up, w_down, low_o, dgate_o, dup_o, part_o):
    low = grad[...].astype(BF)
    low_o[...] = low
    dact = dot_t(low, w_down[...])
    gates = gate[...]
    share = sigmoid(gates)
    dgate = (dact * up[...] * (share * (1.0 + gates * (1.0 - share)))).astype(BF)
    dup = (dact * (gates * share)).astype(BF)
    dgate_o[...] = dgate
    dup_o[...] = dup
    part_o[...] = dot_t(dgate, w_gate[...]) + dot_t(dup, w_up[...])


def mix_back_body(
    grad, part, other, middle, gain, w_attn, w_out, z, y, c_low, running,
    dmid_o, low_o, datt_o, dy_o, dz_o, state_o, dgain_o,
):
    dnorm, dgain = rms_back(part[...] + other[...], middle[...], gain[...])
    dgain_o[...] = dgain
    dmid = grad[...] + dnorm
    dmid_o[...] = dmid
    low = dmid.astype(BF)
    low_o[...] = low
    datt_o[...] = dot_t(low, w_attn[...]).astype(BF)
    dgated = dot_t(low, w_out[...])
    gate = z[...].astype(F32)
    share = sigmoid(gate)
    dz_o[...] = (dgated * y[...] * (share * (1.0 + gate * (1.0 - share)))).astype(BF)
    dy_o[...] = dgated * (gate * share)
    span = y.shape[0] // 2
    for s in (0, 1):
        at = slice(s * span, (s + 1) * span)
        grown = jnp.exp(running[at])
        for pair in range(HEADS // 2):
            dy = dy_o[at, block(pair)] * pair_wide(grown, pair)
            into = t_dot(dy.astype(BF), c_low[at])
            state_o[s * DI + 2 * P_SIZE * pair : s * DI + 2 * P_SIZE * (pair + 1)] = into.astype(BF)


def attend_back_body(first_row, q, kv, datt, cosine, sine, dq_o, dkv_o):
    chips = kv.shape[0]
    span = q.shape[0] // 2
    scale = HEAD_SIZE ** (-0.5)
    for s in (0, 1):
        at = slice(s * span, (s + 1) * span)
        keys = kv[:, s, :span].reshape(chips * span, 2 * HEAD_SIZE)
        parts = []
        dkv = jnp.zeros((chips * span, 2 * HEAD_SIZE), F32)
        for group in head_groups(chips):
            rows = [head_rows(q[at], h, False) for h in group]
            rows = jnp.concatenate(rows, axis=0).astype(BF)
            grads = [head_rows(datt[at], h, True) for h in group]
            grads = jnp.concatenate(grads, axis=0).astype(BF)
            prob = probabilities(rows, keys, first_row[0], span)
            dprob = dot_t(grads, keys)
            inner = jnp.sum(prob * dprob, axis=-1, keepdims=True)
            dscores = (prob * (dprob - inner)).astype(BF)
            dq = dot(dscores, keys) * scale
            parts += [dq[k * span : (k + 1) * span] for k in range(len(group))]
            dkv = dkv + t_dot(dscores, rows) * scale + t_dot(prob.astype(BF), grads)
        dq = heads_joined(parts, False)
        dq_o[at] = rotate(dq, cosine[at, :QW], -sine[at, :QW]).astype(BF)
        dkv_o[:, s] = dkv.astype(BF).reshape(chips, span, 2 * HEAD_SIZE)


def scan_back_body(
    raw, edge, taps, steps_raw, heads, carried, later, dy_in,
    draw_o, dedge_o, dtaps_o, dsteps_o, dheads_o,
):
    span = raw.shape[0] // 2
    wide = (DI, N)
    head_of = (lax.shift_right_logical(rows_of(wide), 6) == lanes(wide)).astype(F32)
    dtaps = [jnp.zeros((1, taps.shape[1]), F32) for _ in range(CONV + 1)]
    dheads = [jnp.zeros((1, N), F32) for _ in range(3)]
    for s in (0, 1):
        at = slice(s * span, (s + 1) * span)
        extended, summed = convolved(raw[at], edge[s], taps[...])
        share = sigmoid(summed)
        conv = summed * share
        steps, logs, running, running_t = decay_of(steps_raw[at], heads[...])
        b_low, c_low = conv[:, DI : DI + N].astype(BF), conv[:, DI + N :].astype(BF)
        inner = dot_t(c_low, b_low)
        grown = jnp.exp(running)
        tail = jnp.exp(running[span - 1 : span] - running)
        low_half = lanes((span, 2 * P_SIZE)) < P_SIZE
        dinner = jnp.zeros((span, span), F32)
        db = jnp.zeros((span, N), F32)
        dc = jnp.zeros((span, N), F32)
        to_running, to_steps, to_tail, to_skip, dxs = [], [], [], [], []
        for pair in range(HEADS // 2):
            state_rows = slice(s * DI + 2 * P_SIZE * pair, s * DI + 2 * P_SIZE * (pair + 1))
            xs = conv[:, block(pair)]
            dy = dy_in[at, block(pair)]
            dy_low = dy.astype(BF)
            steps_wide = pair_wide(steps, pair)
            dt_x = xs * steps_wide
            dt_low = dt_x.astype(BF)
            y_parts, dx_parts = [], []
            for k in (0, 1):
                decays = decays_between(running, running_t, 2 * pair + k)
                mixing = (inner * decays).astype(BF)
                y_parts.append(dot(mixing, dt_low))
                dx_parts.append(t_dot(mixing, dy_low))
                own = jnp.where(low_half == (k == 0), dy, 0.0).astype(BF)
                dinner = dinner + dot_t(own, dt_low) * decays
            y_inner = jnp.where(low_half, y_parts[0], y_parts[1])
            dx_inner = jnp.where(low_half, dx_parts[0], dx_parts[1])
            grown_wide, tail_wide = pair_wide(grown, pair), pair_wide(tail, pair)
            held, after_it = carried[state_rows], later[state_rows]
            y_state = dot_t(c_low, held) * grown_wide
            dx_end = dot_t(b_low, after_it) * tail_wide
            dc = dc + dot((dy * grown_wide).astype(BF), held)
            db = db + dot((dt_x * tail_wide).astype(BF), after_it)
            ddt_x = dx_inner + dx_end
            to_tail.append(dt_x * dx_end)
            to_running.append(
                dy_low.astype(F32) * y_inner + dy * y_state
                - dt_low.astype(F32) * dx_inner - to_tail[-1]
            )
            to_steps.append(xs * ddt_x)
            to_skip.append(jnp.sum(dy * xs, axis=0, keepdims=True))
            dxs.append(ddt_x * steps_wide + dy * pair_wide(heads[2:3], pair))
        dinner_low = dinner.astype(BF)
        dc = dc + dot(dinner_low, b_low)
        db = db + t_dot(dinner_low, c_low)

        def by_head(parts):
            return dot(jnp.concatenate(parts, axis=1), head_of, HIGHEST)

        here_on = slice(s * DI, (s + 1) * DI)
        both = t_dot(head_of, carried[here_on].astype(F32) * later[here_on].astype(F32), HIGHEST)
        through = dot_t(jnp.ones((8, N), F32), both, HIGHEST)[0:1]
        last = jnp.sum(by_head(to_tail), axis=0, keepdims=True) + grown[span - 1 : span] * through
        drunning = by_head(to_running)
        drunning = drunning + jnp.where(rows_of(drunning.shape) == span - 1, last, 0.0)
        square = (span, span)
        upper = (lanes(square) >= rows_of(square)).astype(F32)
        dlogs = dot(upper, drunning, HIGHEST)
        dsteps = by_head(to_steps) - jnp.exp(heads[1:2]) * dlogs
        dsteps = dsteps * sigmoid(steps_raw[at])
        dsteps = jnp.where(lanes(dsteps.shape) < HEADS, dsteps, 0.0)
        dsteps_o[at] = dsteps.astype(BF)
        dheads[0] += jnp.sum(dsteps, axis=0, keepdims=True)
        dheads[1] += jnp.sum(logs * dlogs, axis=0, keepdims=True)
        skips = jnp.broadcast_to(jnp.concatenate(to_skip, axis=1), (8, DI))
        dheads[2] += dot(skips, head_of, HIGHEST)[0:1]

        dconv = jnp.concatenate(dxs + [db, dc], axis=1)
        dsum = dconv * (share * (1.0 + summed * (1.0 - share)))
        zeros = jnp.zeros((8, dsum.shape[1]), F32)
        behind = jnp.concatenate([dsum, zeros], axis=0)
        ahead = jnp.concatenate([zeros, dsum[:8]], axis=0)
        draw = jnp.zeros_like(dsum)
        dedge = jnp.zeros_like(zeros)
        first = extended.shape[0] - span - (CONV - 1)
        for k in range(CONV):
            tap = taps[k : k + 1]
            draw = draw + tap * behind[CONV - 1 - k : CONV - 1 - k + span]
            dedge = dedge + tap * ahead[CONV - 1 - k : CONV - 1 - k + 8]
            dtaps[k] += jnp.sum(dsum * extended[first + k : first + k + span], axis=0, keepdims=True)
        dtaps[CONV] += jnp.sum(dsum, axis=0, keepdims=True)
        draw_o[at] = draw
        dedge_o[s] = jnp.concatenate([zeros, dedge], axis=0).astype(BF)
    for k in range(CONV + 1):
        dtaps_o[k : k + 1] = dtaps[k]
    dtaps_o[CONV + 1 :] = jnp.zeros((8 - CONV - 1, taps.shape[1]), F32)
    for k in range(3):
        dheads_o[k : k + 1] = dheads[k]
    dheads_o[3:] = jnp.zeros((5, N), F32)


def enter_back_body(
    draw, edge, dq, dkv, dsteps, dz, cosine, sine, w_a, w_b, hidden,
    drest_o, dxs_o, part_o, dgain_o,
):
    span = draw.shape[0] // 2
    bc_at = QW + 2 * HEAD_SIZE
    drest_o[:, :QW] = dq[...]
    drest_o[:, bc_at + 2 * N :] = dsteps[...]
    for s in (0, 1):
        at = slice(s * span, (s + 1) * span)
        added = jnp.concatenate(
            [jnp.zeros((span - edge.shape[1], edge.shape[2]), F32), edge[s].astype(F32)], axis=0
        )
        mine = (draw[at] + added).astype(BF)
        dxs_o[at] = mine[:, :DI]
        drest_o[at, bc_at : bc_at + 2 * N] = mine[:, DI:]
        total = jnp.zeros((span, 2 * HEAD_SIZE), F32)
        for chip in range(dkv.shape[0]):
            total = total + dkv[chip, s * span : (s + 1) * span].astype(F32)
        drest_o[at, QW:bc_at] = rotate(total, cosine[at, QW:], -sine[at, QW:]).astype(BF)
    z_a = w_a.shape[1] - REST
    grads = dz[...]
    part_o[...] = dot_t(
        jnp.concatenate([drest_o[...], grads[:, :z_a]], axis=1), w_a[...]
    ) + dot_t(jnp.concatenate([grads[:, z_a:], dxs_o[...]], axis=1), w_b[...])
    rows = hidden[...]
    dgain = jnp.sum(part_o[...] * rows * inverse_rms(rows), axis=0, keepdims=True)
    shape = dgain_o.shape
    dgain_o[...] = jnp.where(rows_of(shape) == 0, dgain, 0.0).astype(BF)


def leave_back_body(dmid, part, other, hidden, gain, grad_o):
    dnorm, _ = rms_back(part[...] + other[...], hidden[...], gain[...])
    grad_o[...] = dmid[...] + dnorm


def in_order_body(at, own, got, out):
    even = at[2] % 2 == 0
    for k in range(own.shape[0]):
        out[0, k] = jnp.where(even, own[k], got[k])
        out[1, k] = jnp.where(even, got[k], own[k])


def line_body(at, pair, over, rest, first, second):
    inner = (at[2] == 1) | (at[2] == 2)
    for k, out in enumerate((first, second)):
        for j in (0, 1):
            far = jnp.where(inner, over[j, k], rest[j, k])
            out[j] = jnp.where(at[2] < 2, pair[j, k], far)
            out[2 + j] = jnp.where(at[2] < 2, far, pair[j, k])


def first_move_body(at, own_a, got_a, own_b, got_b, first, second):
    for index, own, got, out in ((1, own_a, got_a, first), (0, own_b, got_b, second)):
        for z in range(own.shape[0]):
            out[z, 0] = jnp.where(at[index] == 0, own[z], got[z])
            out[z, 1] = jnp.where(at[index] == 0, got[z], own[z])


def second_move_body(at, own_a, got_a, own_b, got_b, first, second):
    for z in range(own_a.shape[0]):
        for k in (0, 1):
            for j in (0, 1):
                own, got = (own_a, got_a) if j == 0 else (got_a, own_a)
                first[4 * z + 2 * k + j] = jnp.where(at[0] == 0, own[z, k], got[z, k])
                own, got = (own_b, got_b) if j == 0 else (got_b, own_b)
                second[4 * z + 2 * j + k] = jnp.where(at[1] == 0, own[z, k], got[z, k])


def cut_body(at, whole, away):
    height = away.shape[0]
    first = pl.multiple_of((1 - at[3]) * height, height)
    away[...] = whole[pl.ds(first, height), :]


def rows_body(chips, at, whole, got, attn, rest, down):
    height = got.shape[0] // chips
    heights = (QW // chips, DI // chips, FFH // chips)
    for j in range(chips):
        block = slice(j * height, (j + 1) * height)
        first = pl.multiple_of(at[3] * got.shape[0] + j * height, height)
        keep = whole[pl.ds(first, height), :]
        for core in (0, 1):
            columns = slice(core * HALF, (core + 1) * HALF)
            both = jnp.where(at[3] == core, keep, got[block])
            mixed, fed = unfolded(both[:, :D]), unfolded(both[:, D:])
            attn[j * heights[0] : (j + 1) * heights[0], columns] = mixed[: heights[0]]
            rest[j * heights[1] : (j + 1) * heights[1], columns] = mixed[heights[0] :]
            down[j * heights[2] : (j + 1) * heights[2], columns] = fed


def sum_body(first, second, third, out):
    out[...] = first[...] + (second[...] + third[...])


def hand_body(first, second, third, out):
    out[...] = (first[...] + (second[...] + third[...])).astype(BF).astype(F32)


def pass_body(value, out):
    out[...] = value[...]


def split_body(at, rows_a, grad_a, rows_b, grad_b, *refs):
    column, (send_a, keep_a, send_b, keep_b) = refs[:-4], refs[-4:]
    depth, _, height, width = send_a.shape
    for z in range(depth):
        for y in (0, 1):
            first = (2 * z + y) * 2 * height
            out = t_dot(rows_a[:, first : first + 2 * height], grad_a[...])
            for v in column:
                shape = (v.shape[0], N)
                unit = ((rows_of(shape) == 0) & (lanes(shape) == N - 1)).astype(F32).astype(BF)
                added = t_dot(v[:, first : first + 2 * height], unit)
                out = jnp.concatenate([out[:, : width - N], out[:, width - N :] + added], axis=1)
            low, high = out[:height], out[height:]
            send_a[z, y] = jnp.where(at[0] == 0, high, low).astype(BF)
            keep_a[z, y] = jnp.where(at[0] == 0, low, high).astype(BF)
        first = z * 4 * height
        out = t_dot(rows_b[:, first : first + 4 * height], grad_b[...])
        for x in (0, 1):
            low = out[x * height : (x + 1) * height]
            high = out[(x + 2) * height : (x + 3) * height]
            send_b[z, x] = jnp.where(at[1] == 0, high, low).astype(BF)
            keep_b[z, x] = jnp.where(at[1] == 0, low, high).astype(BF)


def columns_body(at, act, att, gated, grad_d, grad_m, keep_d, away_d, keep_m, away_m):
    chips = keep_d.shape[0]

    def put(keep, away, chip, first, rows):
        left, right = rows[:, :HALF], rows[:, HALF:]
        here = slice(first, first + rows.shape[0])
        keep[chip, here] = jnp.where(at[3] == 0, left, right).astype(BF)
        away[chip, here] = jnp.where(at[3] == 0, right, left).astype(BF)

    def product(rows, grad, chip):
        height = rows.shape[1] // chips
        return t_dot(rows[:, chip * height : (chip + 1) * height], grad[...])

    from_att = t_dot(att[...], grad_m[...])
    height = QW // chips
    for chip in range(chips):
        put(keep_d, away_d, chip, 0, product(act, grad_d, chip))
        put(keep_m, away_m, chip, 0, from_att[chip * height : (chip + 1) * height])
    from_gated = t_dot(gated[...], grad_m[...])
    tall = DI // chips
    for chip in range(chips):
        put(keep_m, away_m, chip, height, from_gated[chip * tall : (chip + 1) * tall])


def regroup_body(at, keep_d, got_d, keep_m, got_m, send_a, rest_a, send_b, rest_b):
    layers = send_a.shape[0] // 2
    for which, (down, mix) in enumerate(((keep_d, keep_m), (got_d, got_m))):
        core = at[3] if which == 0 else 1 - at[3]
        for z in range(layers):
            to = core * layers + z
            for k in (0, 1):
                low, high = down[4 * z + 2 * k], down[4 * z + 2 * k + 1]
                send_a[to, k] = jnp.where(at[0] == 0, high, low)
                rest_a[to, k] = jnp.where(at[0] == 0, low, high)
                low, high = mix[4 * z + k], mix[4 * z + 2 + k]
                send_b[to, k] = jnp.where(at[1] == 0, high, low)
                rest_b[to, k] = jnp.where(at[1] == 0, low, high)


def fold_body(at, keep_a, got_a, keep_b, got_b, send_a, rest_a, send_b, rest_b):
    for index, keep, got, send, rest in (
        (1, keep_a, got_a, send_a, rest_a),
        (0, keep_b, got_b, send_b, rest_b),
    ):
        for z in range(keep.shape[0]):
            low = keep[z, 0].astype(F32) + got[z, 0].astype(F32)
            high = keep[z, 1].astype(F32) + got[z, 1].astype(F32)
            send[z] = jnp.where(at[index] == 0, high, low).astype(BF)
            rest[z] = jnp.where(at[index] == 0, low, high).astype(BF)


def folded(rows, height):
    if rows.shape[0] == height:
        return rows
    return jnp.concatenate([rows[:height], rows[height:]], axis=1)


def unfolded(rows):
    half = rows.shape[1] // 2
    return jnp.concatenate([rows[:, :half], rows[:, half:]], axis=0)


def z_start_body(at, *refs):
    summands, (far, near) = refs[:-2], refs[-2:]
    height = far.shape[1]
    first = 0
    for one, two in zip(summands[::2], summands[1::2]):
        width = one.shape[1] * one.shape[2] // height
        for out, half in ((near, at[2] // 2), (far, 1 - at[2] // 2)):
            for j in (0, 1):
                total = one[2 * half + j].astype(F32) + two[2 * half + j].astype(F32)
                out[j, :, first : first + width] = folded(total, height).astype(BF)
        first += width


def z_across_body(far, got, out):
    for j in (0, 1):
        out[j] = (far[j].astype(F32) + got[j].astype(F32)).astype(BF)


def z_last_body(at, near, got, send, keep):
    low = near[0].astype(F32) + got[0].astype(F32)
    high = near[1].astype(F32) + got[1].astype(F32)
    even = at[2] % 2 == 0
    send[...] = jnp.where(even, high, low).astype(BF)
    keep[...] = jnp.where(even, low, high).astype(BF)


def add_body(*refs):
    summands, out = refs[:-1], refs[-1]
    height = out.shape[1]
    first = 0
    for one, two in zip(summands[::2], summands[1::2]):
        width = one.shape[1] * one.shape[2] // height
        for z in range(out.shape[0]):
            total = one[z].astype(F32) + two[z].astype(F32)
            out[z, :, first : first + width] = folded(total, height).astype(BF)
        first += width


def choose_body(at, blocks, keep, got, mine, away):
    one = sum(blocks[z].astype(F32) for z in range(blocks.shape[0]))
    two = keep[...].astype(F32) + got[...].astype(F32)
    mine[...] = jnp.where(at[3] == 0, one, two)
    away[...] = jnp.where(at[3] == 0, two, one)


def late_grads_body(at, mine, got, gate_up, down, attn, rest):
    height = attn.shape[0]
    for core in (0, 1):
        for k in (0, 1):
            to = (2 * k + core) * FFH
            from_ = slice(k * FFH, (k + 1) * FFH)
            gate_up[:, to : to + FFH] = jnp.where(at[3] == core, mine[:, from_], got[:, from_])
        here = slice(core * HALF, (core + 1) * HALF)
        from_ = slice(2 * FFH, 2 * FFH + 2 * HALF)
        down[:, here] = unfolded(jnp.where(at[3] == core, mine[:, from_], got[:, from_]))
        from_ = slice(2 * FFH + 2 * HALF, 2 * FFH + 4 * HALF)
        both = unfolded(jnp.where(at[3] == core, mine[:, from_], got[:, from_]))
        attn[:, here] = both[:height]
        rest[:, here] = both[height:]


def early_grads_body(at, mine, got, qkv, into, steps, gain):
    halves_ = [jnp.where(at[3] == core, mine[...], got[...]) for core in (0, 1)]
    rest = [v[:, DI : DI + REST] for v in halves_]
    for core in (0, 1):
        qkv[:, core * QW : (core + 1) * QW] = rest[core][:, :QW]
        into[:, core * DI : (core + 1) * DI] = halves_[core][:, :DI]
        into[:, (2 + core) * DI : (3 + core) * DI] = halves_[core][:, DI + REST :]
    kv = [v[:, QW : QW + 2 * HEAD_SIZE] for v in rest]
    low = lanes(kv[0].shape) < HEAD_SIZE
    turned = [pltpu.roll(v, HEAD_SIZE, 1) for v in kv]
    qkv[:, 2 * QW : 2 * QW + 2 * HEAD_SIZE] = jnp.where(low, kv[0], turned[1])
    qkv[:, 2 * QW + 2 * HEAD_SIZE :] = jnp.where(low, turned[0], kv[1])
    bc_at = QW + 2 * HEAD_SIZE
    into[:, 4 * DI :] = rest[0][:, bc_at : bc_at + 2 * N] + rest[1][:, bc_at : bc_at + 2 * N]
    dt = [v[:, bc_at + 2 * N :] for v in rest]
    gain[...] = dt[0] + dt[1]
    dt = [jnp.where(lanes(v.shape) < HEADS, v, 0.0) for v in dt]
    steps[...] = dt[0] + pltpu.roll(dt[1], HEADS, 1)


def weight_grad(operand, grad_rows):
    return lax.dot_general(
        operand, grad_rows, (((0,), (0,)), ((), ())), preferred_element_type=F32
    ).astype(BF)


def layer_forward(kernel, hidden, entering, rows_held, feeding, gains, taps, heads, tables):
    here = lax.axis_index("seq").astype(jnp.int32).reshape(1)
    count = lax.axis_size("seq")
    rows = hidden.shape[0]
    span = rows // 2
    cosine, sine = tables
    w_a, w_b = entering()
    normed, q, kv, raw, z, steps_raw = kernel(
        enter_body,
        [((rows, D), BF), ((rows, QW), BF), ((count, 2, span + 16, N), BF),
         ((rows, DI + 2 * N), BF), ((rows, DI), BF), ((rows, N), F32)],
        hidden, gains[0], w_a, w_b, cosine, sine, heads,
        flops=2 * rows * D * (w_a.shape[1] + w_b.shape[1]),
    )
    kv = to_all(kv)
    tails = raw.reshape(2, span, -1)[:, span - 16 :]
    edge = lax.ppermute(tails, "seq", [(k, k + 1) for k in range(count - 1)])
    w_attn, w_out, w_down = rows_held()
    y_local, c_low, states, running = kernel(
        local_body,
        [((rows, DI), F32), ((rows, N), BF), ((2 * DI, N), BF), ((rows, N), F32)],
        raw, edge, taps, steps_raw, heads, flops=2 * rows * span * DI * 4,
    )
    blocks = to_all(states.reshape(count, -1, N))
    att, logs = kernel(
        attend_body, [((rows, QW), BF), ((count, 2 * N), F32)], here * span, q, kv,
        flops=4 * rows * QW * 2 * count * span,
    )
    (carried,) = kernel(
        chain_body, [(blocks.shape, BF)], here, blocks, logs, flops=blocks.size
    )
    carried = to_all(carried).reshape(2 * DI, N)
    y, gated, part = kernel(
        mix_body, [((rows, DI), F32), ((rows, DI), BF), ((rows, D), F32)],
        y_local, running, c_low, carried, z, att, w_attn, w_out, flops=4 * rows * D * D,
    )
    other = swap(part)
    w_gate, w_up = feeding()
    middle, normed_two, gate, up, act, more = kernel(
        feed_body,
        [((rows, D), F32), ((rows, D), BF), ((rows, FFH), F32), ((rows, FFH), F32),
         ((rows, FFH), BF), ((rows, D), F32)],
        hidden, part, other, gains[1], w_gate, w_up, w_down, flops=6 * rows * D * D,
    )
    kept = (
        hidden, normed, q, kv, logs, raw, edge, steps_raw, c_low, running, carried, y, z, att,
        gated, middle, normed_two, gate, up, act,
    )
    return (middle, more, swap(more)), kept, (w_a, w_b, w_attn, w_out, w_gate, w_up, w_down)


def layer_backward(
    kernel, grad_result, kept, weights, gains, taps, heads, tables, reduces, sums=None, owed=None,
    spread=None,
):
    (
        hidden, normed, q, kv, logs, raw, edge, steps_raw, c_low, running, carried, y, z, att,
        gated, middle, normed_two, gate, up, act,
    ) = kept
    w_a, w_b, w_attn, w_out, w_gate, w_up, w_down = weights
    here = lax.axis_index("seq").astype(jnp.int32).reshape(1)
    count = lax.axis_size("seq")
    rows = hidden.shape[0]
    span = rows // 2
    cosine, sine = tables
    z_a = w_a.shape[1] - REST
    low_down, dgate, dup, part = kernel(
        feed_back_body,
        [((rows, D), BF), ((rows, FFH), BF), ((rows, FFH), BF), ((rows, D), F32)],
        grad_result, gate, up, w_gate, w_up, w_down, flops=6 * rows * D * D,
    )
    other = swap(part)
    result = None
    if owed:
        owed["z"] = reduces.fold(owed["z"])
        late_1 = reduces.z_start(owed["feed"], owed["mixed"])
    else:
        (result,) = kernel(sum_body, [((rows, D), F32)], *sums)
    feed = reduces.open_plain(normed_two, dgate, normed_two, dup)
    if owed:
        reduces.settle(owed["z"])
    dmid, low, datt, dy, dz, into, dgain_two = kernel(
        mix_back_body,
        [((rows, D), F32), ((rows, D), BF), ((rows, QW), BF), ((rows, DI), F32), ((rows, DI), BF),
         ((2 * DI, N), BF), ((1, D), F32)],
        grad_result, part, other, middle, gains[1], w_attn, w_out, z, y, c_low, running,
        flops=4 * rows * D * D,
    )
    blocks = to_all(into.reshape(count, -1, N))
    columns = reduces.columns(act, att, gated, (low_down, low))
    if owed:
        owed["enter"] = reduces.fold(owed["enter"])
        late_1 = reduces.z_across(late_1)
    dq, dkv = kernel(
        attend_back_body, [((rows, QW), BF), ((count, 2, span, N), BF)],
        here * span, q, kv, datt, cosine, sine, flops=10 * rows * QW * 2 * count * span,
    )
    mixed = reduces.open_columns(columns)
    if owed:
        reduces.settle(owed["enter"])
    (back,) = kernel(
        chain_back_body, [((count, 2 * span + blocks.shape[1], N), BF)],
        here, blocks, logs, dkv, flops=blocks.size,
    )
    back = to_all(back)
    later = back[:, 2 * span :].reshape(2 * DI, N)
    feed = reduces.fold(feed)
    if owed:
        late_1 = reduces.z_last(late_1)
    if owed:
        early_1 = reduces.z_start(owed["z"], owed["enter"])
    else:
        gate_part = reduces.open_plain(normed, dz[:, :z_a], normed, dz[:, z_a:])
    reduces.settle(feed)
    draw, dedge, dtaps, dsteps, dheads = kernel(
        scan_back_body,
        [((rows, DI + 2 * N), F32), ((2, 16, DI + 2 * N), BF), ((8, DI + 2 * N), F32),
         ((rows, N), BF), ((8, N), F32)],
        raw, edge, taps, steps_raw, heads, carried, later, dy, flops=20 * rows * span * DI,
    )
    dedge = lax.ppermute(dedge, "seq", [(k + 1, k) for k in range(count - 1)])
    small = (dgain_two, dtaps[: CONV + 1], dheads[:3, :HEADS])
    if owed:
        small = spread(small)
    mixed = reduces.fold(mixed)
    if owed:
        early_1 = reduces.z_across(early_1)
    drest, dxs, part, dgain_one = kernel(
        enter_back_body,
        [((rows, REST), BF), ((rows, DI), BF), ((rows, D), F32), ((16, D), BF)],
        draw, dedge, dq, back, dsteps, dz, cosine, sine, w_a, w_b, hidden,
        flops=2 * rows * D * (w_a.shape[1] + w_b.shape[1]),
    )
    other = swap(part)
    enter = reduces.open_plain(normed, drest, normed, dxs, dgain_one)
    reduces.settle(mixed)
    if owed:
        late = reduces.z_once(feed, mixed)
        gate_part = reduces.open_plain(normed, dz[:, :z_a], normed, dz[:, z_a:])
    (grad,) = kernel(
        leave_back_body, [((rows, D), F32)],
        dmid, part, other, hidden, gains[0], flops=rows * D,
    )
    if not owed:
        states = {"feed": feed, "mixed": mixed, "z": gate_part, "enter": enter, "result": result}
        return grad, states, small
    enter = reduces.fold(enter)
    gate_part = reduces.fold(gate_part)
    early_1 = reduces.z_last(early_1)
    kernel.also(late[0])
    early = reduces.z_once(gate_part, enter)
    late = reduces.own(late, late_1)
    return grad, {"late": late, "early": reduces.own(early, early_1)}, small


def halves(array, sizes, at):
    out = []
    for core in (0, 1):
        parts, start = [], at
        for width in sizes:
            half = width // 2
            parts.append(array[:, start + core * half : start + (core + 1) * half])
            start += width
        out.append(parts)
    return out


def rotation_tables(positions):
    half = HEAD_SIZE // 2
    frequency = ROPE_BASE ** (-jnp.arange(half, dtype=F32) / half)
    angles = positions.astype(F32)[:, None] * frequency[None, :]
    cosine, sine = jnp.cos(angles), jnp.sin(angles)
    still = jnp.zeros((positions.shape[0], HEAD_SIZE), F32)
    cosine = jnp.tile(jnp.concatenate([cosine, cosine], axis=1), (1, QH + 1))
    sine = jnp.tile(jnp.concatenate([-sine, sine], axis=1), (1, QH + 1))
    return (
        jnp.tile(jnp.concatenate([cosine, still + 1.0], axis=1), (2, 1)),
        jnp.tile(jnp.concatenate([sine, still], axis=1), (2, 1)),
    )


def columns_home(whole):
    first = lax.axis_index("section") == 0
    blocks = whole.reshape(lax.axis_size("seq") // 2, -1, D)
    left, right = blocks[..., :HALF], blocks[..., HALF:]
    keep = jnp.where(first, left, right)
    got = swap(jnp.where(first, right, left))
    return jnp.concatenate([jnp.where(first, keep, got), jnp.where(first, got, keep)], axis=0)


def by_chip(whole):
    return whole.reshape(lax.axis_size("seq"), -1, whole.shape[1])


NAMES = ("first", "second", "mix", "down", "gate", "up")


def per_device(
    boundary, lengths, norm_gains, w_qkv, w_attn, w_in, w_dt, conv_params, head_params, w_out, w_gate_up, w_down,
):
    core = lax.axis_index("section")
    here = lax.axis_index("seq")
    count = lax.axis_size("seq")
    first = core == 0
    span = boundary.shape[2]
    rows = 2 * span

    qkv = halves(w_qkv[0], (QW * 2, 2 * HEAD_SIZE, 2 * HEAD_SIZE), 0)
    into = halves(w_in[0], (2 * DI, 2 * DI), 0)
    both_bc = w_in[0][:, 4 * DI :]
    steps = halves(w_dt[0], (SH,), 0)
    ups = halves(w_gate_up[0], (2 * FFH, 2 * FFH), 0)
    mix = jnp.concatenate([w_attn[0], w_out[0]], axis=0)
    cut = []
    for k in (0, 1):
        step = jnp.pad(steps[k][0], ((0, 0), (0, N - HEADS)))
        z_k = into[k][0]
        z_a = z_k.shape[1] // 2
        cut.append(
            {
                "first": jnp.concatenate(qkv[k] + [both_bc, step, z_k[:, :z_a]], axis=1),
                "second": jnp.concatenate([z_k[:, z_a:], into[k][1]], axis=1),
                "mix": mix[:, k * HALF : (k + 1) * HALF],
                "gate": ups[k][0],
                "up": ups[k][1],
                "down": w_down[0][:, k * HALF : (k + 1) * HALF],
            }
        )
    layers = ({}, {})
    for name in NAMES:
        own = jnp.where(first, cut[0][name], cut[1][name])
        got = swap(jnp.where(first, cut[1][name], cut[0][name]))
        layers[0][name] = jnp.where(first, own, got)
        layers[1][name] = jnp.where(first, got, own)

    kernel = Order()
    gathers = Gathers([(layers[0]["first"], layers[0]["second"])], kernel)
    rest_0 = Whole(layers[0], kernel, NAMES[2:])
    all_1 = Whole(layers[1], kernel, NAMES)
    rest_0.start()
    all_1.start()
    small = jnp.concatenate([norm_gains[0].reshape(-1), conv_params[0].reshape(-1)])
    small_other = swap(small)
    small = jnp.stack([jnp.where(first, small, small_other), jnp.where(first, small_other, small)])
    small = to_all(jnp.broadcast_to(small[None], (count,) + small.shape))
    small = small.swapaxes(0, 1).astype(F32)
    width = norm_gains.shape[2]
    gains = small[:, :, : 2 * width].reshape(2, count, 2, width).swapaxes(1, 2).reshape(2, 2, D)
    taps = small[:, :, 2 * width :].reshape(2, count, CONV + 1, -1).swapaxes(1, 2)
    taps = taps.reshape(2, CONV + 1, 4 * DI // 2 + 2 * N)
    taps = jnp.concatenate(
        [jnp.where(first, taps[..., :DI], taps[..., DI : 2 * DI]), taps[..., 2 * DI :]], axis=-1
    )
    heads_other = swap(head_params[0])
    heads = jnp.stack(
        [
            jnp.where(first, head_params[0], heads_other),
            jnp.where(first, heads_other, head_params[0]),
        ]
    )
    heads = jnp.where(first, heads[..., :HEADS], heads[..., HEADS:])
    heads = jnp.pad(heads, ((0, 0), (0, 5), (0, N - HEADS)))
    gains = gains.reshape(2, 2, 1, D)
    taps = jnp.pad(taps, ((0, 0), (0, 8 - CONV - 1), (0, 0)))

    other = swap(boundary[0])
    inputs = jnp.where(first, boundary[0], other).reshape(rows, D).astype(F32)
    positions = here * span + jnp.arange(span, dtype=jnp.int32)
    live = (positions[None, :] < lengths[:, None]).astype(F32)
    cotangent = jnp.where(first, other, boundary[0]).astype(F32) * live[..., None]
    cotangent = cotangent.reshape(rows, D)
    tables = rotation_tables(positions)

    reduces = Reduces(kernel)
    def pair(whole, one, two):
        return lambda: (whole.part(one), whole.part(two))

    sums, kept_0, weights_0 = layer_forward(
        kernel, inputs, lambda: gathers.get(0), rest_0.rows, pair(rest_0, "gate", "up"),
        gains[0], taps[0], heads[0], tables,
    )
    (handed,) = kernel(hand_body, [((rows, D), F32)], *sums)
    sums, kept_1, weights_1 = layer_forward(
        kernel, handed, pair(all_1, "first", "second"), all_1.rows, pair(all_1, "gate", "up"),
        gains[1], taps[1], heads[1], tables,
    )
    conv_width = conv_params.shape[2]

    def spread(small_0, small_1):
        grad_gains, grad_taps, grad_heads = (jnp.stack(v) for v in zip(small_0, small_1))
        xs_part, none = grad_taps[..., :DI], jnp.zeros((2, CONV + 1, DI), F32)
        wide = jnp.concatenate(
            [jnp.where(first, xs_part, none), jnp.where(first, none, xs_part), grad_taps[..., DI:]],
            axis=2,
        )
        none = jnp.zeros((2, 3, HEADS), F32)
        head_wide = jnp.concatenate(
            [jnp.where(first, grad_heads, none), jnp.where(first, none, grad_heads)], axis=2
        )
        gains_once = jnp.where(first, grad_gains, 0.0)
        flat = jnp.concatenate(
            [
                gains_once.reshape(2, count, width).swapaxes(0, 1),
                wide.reshape(2, CONV + 1, count, conv_width)
                .transpose(2, 0, 1, 3)
                .reshape(count, 2, -1),
                jnp.broadcast_to(head_wide.reshape(1, 2, -1), (count, 2, 3 * SH)),
            ],
            axis=2,
        )
        flat = jnp.pad(flat, ((0, 0), (0, 0), (0, -flat.shape[2] % N)))
        return to_all(flat)

    kernel.weight = WEIGHT
    grad_handed, grads_1, small_1 = layer_backward(
        kernel, cotangent, kept_1, weights_1, gains[1], taps[1], heads[1], tables, reduces, sums
    )
    grad_inputs, grads_0, small_0 = layer_backward(
        kernel, grad_handed.astype(BF).astype(F32),
        kept_0, weights_0, gains[0], taps[0], heads[0], tables, reduces, owed=grads_1,
        spread=lambda small_0: spread(small_0, small_1),
    )

    at = corner()
    height = w_qkv.shape[1]
    grad_gu, grad_down, grad_attn, grad_out = kernel(
        late_grads_body,
        [(v.shape[1:], F32) for v in (w_gate_up, w_down, w_attn, w_out)], at, *grads_0["late"],
    )
    grad_qkv, grad_in, grad_dt, gain_one = kernel(
        early_grads_body,
        [((height, w_qkv.shape[2]), F32), ((height, w_in.shape[2]), F32), ((height, N), F32),
         ((height, N), F32)],
        at, *grads_0["early"],
    )

    flat = jnp.sum(small_0, axis=0)
    flat = jnp.where(first, flat[0], flat[1]) + swap(jnp.where(first, flat[1], flat[0]))
    taps_at = width
    heads_at = taps_at + (CONV + 1) * conv_width
    grad_gains = jnp.stack([gain_one[:, N - 1], flat[:taps_at]])
    grad_conv = flat[taps_at:heads_at].reshape(CONV + 1, conv_width)
    total_heads = flat[heads_at : heads_at + 3 * SH].reshape(3, SH)

    ends = jnp.where(first, grad_inputs, grads_1["result"]).reshape(2, span, D)
    outs = (
        ends, grad_gains, grad_qkv, grad_attn, grad_in, grad_dt[:, :SH], grad_conv, total_heads,
        grad_out, grad_gu, grad_down,
    )
    return tuple(out[None] for out in outs)


def solution(mesh):
    by_rows = P("section", "seq", None)
    by_columns = P("section", None, "seq")
    whole = P("section", None, None)
    ends = P("section", None, "seq", None)
    in_specs = (
        ends, P(), by_columns, by_rows, by_rows, by_rows, by_rows, by_columns, whole, by_rows,
        by_rows, by_rows,
    )
    out_specs = (
        ends, by_columns, by_rows, by_rows, by_rows, by_rows, by_columns, whole, by_rows, by_rows,
        by_rows,
    )
    return jax.shard_map(
        per_device, mesh=mesh, in_specs=in_specs, out_specs=out_specs, check_vma=False
    )
```

```python
from functools import partial
from math import isqrt

import jax
import jax.numpy as jnp
from jax import lax
from jax.experimental import pallas as pl
from jax.experimental.pallas import tpu as pltpu
from jax.sharding import PartitionSpec as P

D = 1024
HEAD_SIZE = 64
SH = 24
P_SIZE = 64
N = 128
CONV = 4
QH = 4
HEADS = SH // 2
QW = QH * HEAD_SIZE
DI = HEADS * P_SIZE
FFH = 1024
HALF = D // 2
REST = QW + 2 * HEAD_SIZE + 2 * N + N

eps = 1e-05
ROPE_BASE = 100000000000.0
HIGHEST = lax.Precision.HIGHEST
BF = jnp.bfloat16
F32 = jnp.float32
VMEM_BYTES = 56 * 2**20
WEIGHT = 3 * 10**11


def grid_of(count):
    side = isqrt(count // 4)
    return (count // (side * side), side, side)


def place_on(axis):
    dims = grid_of(lax.axis_size("seq"))
    strides = (dims[1] * dims[2], dims[2], 1)
    return lax.axis_index("seq") // strides[axis] % dims[axis], dims[axis], strides[axis]


def hop(value, axis, moves):
    count = lax.axis_size("seq")
    _, length, stride = place_on(axis)
    pairs = []
    for source in range(count):
        at = source // stride % length
        if at in moves and moves[at] < length:
            pairs.append((source, source + (moves[at] - at) * stride))
    return lax.ppermute(value, "seq", pairs)


NEXT = {0: 1, 1: 0, 2: 3, 3: 2}
INNER = {1: 2, 2: 1}
OUTWARD = {1: 0, 2: 3}
INWARD = {0: 1, 3: 2}


def swap(value):
    return lax.ppermute(value, "section", [(0, 1), (1, 0)])


def both_cores(value):
    return value + swap(value)


def line_gather(part, axis, dim):
    at, length, _ = place_on(axis)
    got = hop(part, axis, NEXT)
    even = at % 2 == 0
    pair = jnp.stack([jnp.where(even, part, got), jnp.where(even, got, part)], axis=dim)
    if length == 2:
        return pair
    over = hop(pair, axis, INNER)
    rest = hop(over, axis, OUTWARD)
    far = jnp.where((at == 1) | (at == 2), over, rest)
    return jnp.concatenate(
        [jnp.where(at < 2, pair, far), jnp.where(at < 2, far, pair)], axis=dim
    )


def corner():
    places = [place_on(axis)[0] for axis in (2, 1, 0)]
    return jnp.stack(places + [lax.axis_index("section")]).astype(jnp.int32)


class Gathers:
    def __init__(self, pairs, kernel):
        self.pairs, self.kernel = pairs, kernel
        self.count = lax.axis_size("seq")
        self.depth, self.side, _ = grid_of(self.count)
        self.state = [None] * len(pairs)
        self.steps = [(step, k) for k in range(len(pairs)) for step in (1, 2, 3, 4, 5)]
        self.place = corner()
        self.start(0)

    def start(self, at):
        if at < len(self.pairs):
            stacked = jnp.stack(self.pairs[at])
            self.state[at] = (stacked, hop(stacked, 0, NEXT))

    def until(self, step, at):
        while (step, at) in self.steps:
            now, pair = self.steps.pop(0)
            getattr(self, "step_%d" % now)(pair)

    def step_1(self, at):
        own, got = self.state[at]
        (pair,) = self.kernel(in_order_body, [((2,) + own.shape, BF)], self.place, own, got)
        self.state[at] = (pair, hop(pair, 0, INNER))

    def step_2(self, at):
        pair, over = self.state[at]
        self.kernel.also(over)
        self.state[at] = (pair, over, hop(over, 0, OUTWARD))

    def step_3(self, at):
        pair = self.state[at][0]
        shape = (4,) + pair.shape[2:]
        first, second = self.kernel(line_body, [(shape, BF)] * 2, self.place, *self.state[at])
        if self.side == 2:
            self.state[at] = (first, hop(first, 1, NEXT), second, hop(second, 2, NEXT))
        else:
            self.state[at] = (line_gather(first, 1, 1), line_gather(second, 2, 1))

    def step_4(self, at):
        if self.side == 2:
            first = self.state[at][0]
            shape = (4, 2) + first.shape[1:]
            shape_b = (4, 2) + self.state[at][2].shape[1:]
            first, second = self.kernel(
                first_move_body, [(shape, BF), (shape_b, BF)], self.place, *self.state[at]
            )
            self.state[at] = (first, hop(first, 2, NEXT), second, hop(second, 1, NEXT))
        else:
            first, second = self.state[at]
            self.state[at] = (line_gather(first, 2, 2), line_gather(second, 1, 1))
        self.start(at + 1)

    def step_5(self, at):
        if self.side != 2:
            self.state[at] = [v.reshape(D, -1) for v in self.state[at]]
            return
        shapes = [(self.count,) + self.state[at][k].shape[2:] for k in (0, 2)]
        first, second = self.kernel(
            second_move_body, [(v, BF) for v in shapes], self.place, *self.state[at]
        )
        self.state[at] = [first.reshape(D, -1), second.reshape(D, -1)]

    def get(self, at):
        self.until(5, at)
        return self.state[at]


class Whole:
    def __init__(self, shards, kernel, names):
        height = shards["gate"].shape[0]
        self.kernel, self.at = kernel, {}
        parts, first = [], 0
        for name in names:
            shard = shards[name]
            part = jnp.concatenate(
                [shard[k : k + height] for k in range(0, shard.shape[0], height)], axis=1
            )
            parts.append(part)
            self.at[name] = (first, part.shape[1])
            first += part.shape[1]
        self.flat = jnp.concatenate(parts, axis=1)

    def start(self):
        self.whole = lax.all_gather(self.flat, "seq", axis=0, tiled=True)

    def part(self, name):
        return Part(self.whole, *self.at[name])

    def rows(self):
        part = Part(self.whole, self.at["mix"][0], 2 * D)
        (away,) = self.kernel(cut_body, [((part.shape[0] // 2, 2 * D), BF)], corner(), part)
        return self.kernel(
            partial(rows_body, lax.axis_size("seq") // 2),
            [((QW, D), BF), ((DI, D), BF), ((FFH, D), BF)], corner(), part, swap(away),
        )


def add(a, b, kind):
    return (a.astype(F32) + b.astype(F32)).astype(kind)


def line_reduce(parts, axis, dim):
    at, length, _ = place_on(axis)

    def pick(array, index):
        return lax.dynamic_index_in_dim(array, index, dim, False)

    if length == 4:
        halves = parts.reshape(parts.shape[:dim] + (2, 2) + parts.shape[dim + 1 :])
        far, near = pick(halves, 1 - at // 2), pick(halves, at // 2)
        far = add(far, hop(far, axis, INWARD), BF)
        parts = add(near, hop(far, axis, INNER), BF)
    got = hop(pick(parts, 1 - at % 2), axis, NEXT)
    return pick(parts, at % 2), got


def z_groups():
    count = lax.axis_size("seq")
    depth, side, _ = grid_of(count)
    plane = side * side
    return [[z * plane + k for z in range(depth)] for k in range(plane)]


class Reduces:
    def __init__(self, kernel):
        self.kernel = kernel
        self.paired = grid_of(lax.axis_size("seq"))[2] == 2

    def open_plain(self, rows_a, grad_a, rows_b, grad_b, *column):
        count = lax.axis_size("seq")
        depth = grid_of(count)[0]
        if not self.paired:
            first = weight_grad(rows_a, grad_a)
            for v in column:
                first = first.at[:, -1].add(v[0])
            return self.open_whole(by_chip(first), by_chip(weight_grad(rows_b, grad_b)))
        height = rows_a.shape[1] // count
        shape = (depth, 2, height, grad_a.shape[1])
        parts = self.kernel(
            split_body, [(shape, BF)] * 4, corner(), rows_a, grad_a, rows_b, grad_b, *column,
            flops=4 * rows_a.size * grad_a.shape[1],
        )
        return self.open(parts)

    def columns(self, act, att, gated, grad):
        half = lax.axis_size("seq") // 2
        if not self.paired:
            mix = jnp.concatenate(
                [weight_grad(v, grad[1]).reshape(half, -1, D) for v in (att, gated)], axis=1
            )
            return columns_home(weight_grad(act, grad[0])), columns_home(mix)
        down, mix = (half, FFH // half, HALF), (half, (QW + DI) // half, HALF)
        keep_d, away_d, keep_m, away_m = self.kernel(
            columns_body, [(down, BF), (down, BF), (mix, BF), (mix, BF)],
            corner(), act, att, gated, *grad, flops=4 * act.size * D,
        )
        return keep_d, swap(away_d), keep_m, swap(away_m)

    def open_columns(self, columns):
        if not self.paired:
            return self.open_whole(*columns)
        depth = grid_of(lax.axis_size("seq"))[0]
        shapes = [((depth, 2) + columns[k].shape[1:], BF) for k in range(4)]
        return self.open(self.kernel(regroup_body, shapes, corner(), *columns))

    def open(self, parts):
        send_a, keep_a, send_b, keep_b = parts
        got_a, got_b = hop(send_a, 2, NEXT), hop(send_b, 1, NEXT)
        return keep_a, got_a, keep_b, got_b

    def open_whole(self, first, second):
        dims = grid_of(lax.axis_size("seq"))
        first, second = (v.reshape(dims + v.shape[1:]) for v in (first, second))
        keep_a, got_a = line_reduce(first, 2, 2)
        keep_b, got_b = line_reduce(second, 1, 1)
        return keep_a, got_a, keep_b, got_b

    def fold(self, state):
        keep_a, got_a, keep_b, got_b = state
        if not self.paired:
            first, second = add(keep_a, got_a, BF), add(keep_b, got_b, BF)
            return *line_reduce(first, 1, 1), *line_reduce(second, 2, 1)
        shape = keep_a.shape[:1] + keep_a.shape[2:]
        shape_b = keep_b.shape[:1] + keep_b.shape[2:]
        send_a, keep_a, send_b, keep_b = self.kernel(
            fold_body, [(shape, BF), (shape, BF), (shape_b, BF), (shape_b, BF)],
            corner(), keep_a, got_a, keep_b, got_b,
        )
        return keep_a, hop(send_a, 1, NEXT), keep_b, hop(send_b, 2, NEXT)

    def settle(self, state):
        self.kernel.also(state[1])
        self.kernel.also(state[3])

    def flat(self, state):
        height = D // lax.axis_size("seq")
        return height, sum(v.shape[1] * v.shape[2] // height for v in (state[0], state[2]))

    def z_start(self, *states):
        height = self.flat(states[0])[0]
        shape = (2, height, sum(self.flat(v)[1] for v in states))
        far, near = self.kernel(
            z_start_body, [(shape, BF)] * 2, corner(), *[v for state in states for v in state]
        )
        return far, hop(far, 0, INWARD), near

    def z_across(self, state):
        far, got, near = state
        (far,) = self.kernel(z_across_body, [(far.shape, BF)], far, got)
        return near, hop(far, 0, INNER)

    def z_last(self, state):
        near, got = state
        shape = near.shape[1:]
        send, keep = self.kernel(z_last_body, [(shape, BF)] * 2, corner(), near, got)
        return keep, hop(send, 0, NEXT)

    def z_once(self, *states):
        height = self.flat(states[0])[0]
        shape = (states[0][0].shape[0], height, sum(self.flat(v)[1] for v in states))
        (whole,) = self.kernel(add_body, [(shape, BF)], *[v for state in states for v in state])
        whole = lax.all_to_all(whole, "seq", 0, 0, tiled=True, axis_index_groups=z_groups())
        return (whole,)

    def own(self, first, second):
        shape = second[0].shape
        mine, away = self.kernel(choose_body, [(shape, F32)] * 2, corner(), *first, *second)
        return mine, swap(away)


def to_all(blocks):
    return lax.all_to_all(blocks, "seq", 0, 0, tiled=True)


class Part:
    def __init__(self, whole, first, width):
        self.whole, self.first = whole, first
        self.shape, self.dtype = (whole.shape[0], width), whole.dtype


class Order:
    def __init__(self):
        self.before = []
        self.weight = 15 * 10**9

    def also(self, value):
        self.before = self.before + [value]

    def __call__(self, body, outs, *args, flops=0):
        out_shape = [jax.ShapeDtypeStruct(shape, kind) for shape, kind in outs]
        count, extra = len(args), len(self.before)
        parts = [k for k, v in enumerate(args) if isinstance(v, Part)]

        def run(*refs):
            given = list(refs[:count])
            results = refs[count + extra : count + extra + len(outs)]
            scratch = refs[count + extra + len(outs) :]
            copies = []
            for slot, k in enumerate(parts):
                source = given[k].at[:, args[k].first : args[k].first + args[k].shape[1]]
                copies.append(pltpu.make_async_copy(source, scratch[slot], scratch[-1].at[slot]))
                copies[-1].start()
                given[k] = scratch[slot]
            for copy in copies:
                copy.wait()
            body(*given, *results)

        def space(v):
            if isinstance(v, Part):
                return pl.ANY
            return pltpu.SMEM if v.dtype == jnp.int32 else pltpu.VMEM

        scratch = [pltpu.VMEM(args[k].shape, args[k].dtype) for k in parts]
        if parts:
            scratch.append(pltpu.SemaphoreType.DMA((len(parts),)))
        results = pl.pallas_call(
            run,
            out_shape=out_shape,
            in_specs=[pl.BlockSpec(memory_space=space(v)) for v in args]
            + [pl.BlockSpec(memory_space=pl.ANY)] * extra,
            out_specs=[pl.BlockSpec(memory_space=pltpu.VMEM) for _ in outs],
            scratch_shapes=scratch,
            compiler_params=pltpu.CompilerParams(vmem_limit_bytes=VMEM_BYTES),
            cost_estimate=pl.CostEstimate(flops=self.weight, bytes_accessed=0, transcendentals=0),
        )(*[v.whole if isinstance(v, Part) else v for v in args], *self.before)
        self.before = [min(results, key=lambda v: v.size)]
        return results


def dot(a, b, precision=None):
    return jnp.dot(a, b, preferred_element_type=F32, precision=precision)


def dot_t(a, b, precision=None):
    return lax.dot_general(
        a, b, (((1,), (1,)), ((), ())), preferred_element_type=F32, precision=precision
    )


def t_dot(a, b, precision=None):
    return lax.dot_general(
        a, b, (((0,), (0,)), ((), ())), preferred_element_type=F32, precision=precision
    )


def sigmoid(v):
    return 1.0 / (1.0 + jnp.exp(-v))


def softplus(v):
    return jnp.maximum(v, 0.0) + jnp.log1p(jnp.exp(-jnp.abs(v)))


def lanes(shape):
    return lax.broadcasted_iota(jnp.int32, shape, len(shape) - 1)


def rows_of(shape):
    return lax.broadcasted_iota(jnp.int32, shape, len(shape) - 2)


def rotate(rows, cosine, sine):
    width = rows.shape[-1]
    half = HEAD_SIZE // 2
    low = (lanes(rows.shape) // half) % 2 == 0
    turned = jnp.where(
        low, pltpu.roll(rows, width - half, 1), pltpu.roll(rows, half, 1)
    )
    return rows * cosine + turned * sine


def inverse_rms(rows):
    return lax.rsqrt(jnp.mean(rows * rows, axis=-1, keepdims=True) + eps)


def rms_back(grad, rows, gain):
    scale = inverse_rms(rows)
    scaled = grad * gain
    inner = jnp.mean(rows * scaled, axis=-1, keepdims=True)
    return (
        scale * scaled - rows * (scale * scale * scale * inner),
        jnp.sum(grad * rows * scale, axis=0, keepdims=True),
    )


def pair_wide(columns, pair):
    shape = (columns.shape[0], 2 * P_SIZE)
    return jnp.where(
        lanes(shape) < P_SIZE,
        jnp.broadcast_to(columns[:, 2 * pair : 2 * pair + 1], shape),
        jnp.broadcast_to(columns[:, 2 * pair + 1 : 2 * pair + 2], shape),
    )


def block(pair):
    return slice(2 * P_SIZE * pair, 2 * P_SIZE * (pair + 1))


def convolved(raw, edge, taps):
    span = raw.shape[0]
    extended = jnp.concatenate([edge.astype(F32), raw.astype(F32)], axis=0)
    at = edge.shape[0] - (CONV - 1)
    summed = jnp.broadcast_to(taps[CONV : CONV + 1], raw.shape)
    for k in range(CONV):
        summed = summed + taps[k : k + 1] * extended[at + k : at + k + span]
    return extended, summed


def decay_of(steps_raw, heads):
    span = steps_raw.shape[0]
    steps = softplus(steps_raw)
    logs = -steps * jnp.exp(heads[1:2])
    square = (span, span)
    lower = (lanes(square) <= rows_of(square)).astype(F32)
    upper = (lanes(square) >= rows_of(square)).astype(F32)
    return steps, logs, dot(lower, logs, HIGHEST), t_dot(logs, upper, HIGHEST)


def decays_between(running, running_t, head):
    span = running.shape[0]
    gap = running[:, head : head + 1] - running_t[head : head + 1, :]
    square = (span, span)
    return jnp.exp(jnp.where(lanes(square) <= rows_of(square), gap, -1e30))


def enter_body(
    hidden, gain, w_a, w_b, cosine, sine, heads, normed_o, q_o, kv_o, raw_o, z_o, steps_o
):
    rows = hidden[...]
    normed = (rows * inverse_rms(rows) * gain[...]).astype(BF)
    normed_o[...] = normed
    a, b = dot(normed, w_a[...]), dot(normed, w_b[...])
    turned = rotate(a[:, : QW + 2 * HEAD_SIZE], cosine[...], sine[...])
    q_o[...] = turned[:, :QW].astype(BF)
    kv = turned[:, QW:].astype(BF)
    bc_at = QW + 2 * HEAD_SIZE
    z_a = w_a.shape[1] - REST
    z_o[:, :z_a] = a[:, REST:].astype(BF)
    z_o[:, z_a:] = b[:, : DI - z_a].astype(BF)
    raw_o[:, :DI] = b[:, DI - z_a :].astype(BF)
    raw_o[:, DI:] = a[:, bc_at : bc_at + 2 * N].astype(BF)
    steps_raw = a[:, bc_at + 2 * N : REST] + heads[0:1]
    steps_o[...] = steps_raw
    logs = -softplus(steps_raw) * jnp.exp(heads[1:2])
    span = rows.shape[0] // 2
    for s in (0, 1):
        total = jnp.sum(logs[s * span : (s + 1) * span], axis=0, keepdims=True)
        high = total.astype(BF).astype(F32)
        middle = (total - high).astype(BF).astype(F32)
        low = total - high - middle
        at = rows_of((16, N))
        packed = jnp.where(
            at == 0, high, jnp.where(at == 1, middle, jnp.where(at == 2, low, 0.0))
        ).astype(BF)
        for chip in range(kv_o.shape[0]):
            kv_o[chip, s, :span] = kv[s * span : (s + 1) * span]
            kv_o[chip, s, span:] = packed


def local_body(raw, edge, taps, steps_raw, heads, y_o, c_o, state_o, running_o):
    span = raw.shape[0] // 2
    for s in (0, 1):
        at = slice(s * span, (s + 1) * span)
        _, summed = convolved(raw[at], edge[s], taps[...])
        conv = summed * sigmoid(summed)
        steps, _, running, running_t = decay_of(steps_raw[at], heads[...])
        running_o[at] = running
        b_low, c_low = conv[:, DI : DI + N].astype(BF), conv[:, DI + N :].astype(BF)
        c_o[at] = c_low
        inner = dot_t(c_low, b_low)
        tail = jnp.exp(running[span - 1 : span] - running)
        low_half = lanes((span, 2 * P_SIZE)) < P_SIZE
        for pair in range(HEADS // 2):
            xs = conv[:, block(pair)]
            dt_x = xs * pair_wide(steps, pair)
            dt_low = dt_x.astype(BF)
            mixed = [
                dot((inner * decays_between(running, running_t, h)).astype(BF), dt_low)
                for h in (2 * pair, 2 * pair + 1)
            ]
            skip = pair_wide(heads[2:3], pair)
            y_o[at, block(pair)] = jnp.where(low_half, mixed[0], mixed[1]) + skip * xs
            end = t_dot((dt_x * pair_wide(tail, pair)).astype(BF), b_low)
            state_o[s * DI + 2 * P_SIZE * pair : s * DI + 2 * P_SIZE * (pair + 1)] = end.astype(BF)


def head_rows(rows, head, upper):
    half = rows[:, block(head // 2)].astype(F32)
    if (head % 2 == 1) != upper:
        half = pltpu.roll(half, P_SIZE, 1)
    keep = lanes(half.shape) >= P_SIZE if upper else lanes(half.shape) < P_SIZE
    return jnp.where(keep, half, 0.0)


def heads_joined(parts, upper):
    out = []
    for even, odd in zip(parts[::2], parts[1::2]):
        low_half = lanes(even.shape) < P_SIZE
        if upper:
            out.append(jnp.where(low_half, pltpu.roll(even, P_SIZE, 1), odd))
        else:
            out.append(jnp.where(low_half, even, pltpu.roll(odd, P_SIZE, 1)))
    return jnp.concatenate(out, axis=1)


def head_groups(chips):
    size = QH if chips <= 16 else 1
    return [list(range(k, k + size)) for k in range(0, QH, size)]


def probabilities(queries, keys, first_row, span):
    scores = dot_t(queries, keys) * HEAD_SIZE ** (-0.5)
    shape = (span, keys.shape[0])
    allowed = lanes(shape) <= rows_of(shape) + first_row
    bias = jnp.where(allowed, 0.0, -1e30)
    scores = scores + jnp.concatenate([bias] * (queries.shape[0] // span), axis=0)
    shifted = jnp.exp(scores - jnp.max(scores, axis=-1, keepdims=True))
    return shifted / jnp.sum(shifted, axis=-1, keepdims=True)


def attend_body(first_row, q, kv, att_o, logs_o):
    chips, _, height, _ = kv.shape
    span = q.shape[0] // 2
    for s in (0, 1):
        keys = kv[:, s, :span].reshape(chips * span, 2 * HEAD_SIZE)
        parts = []
        for group in head_groups(chips):
            rows = [head_rows(q[s * span : (s + 1) * span], h, False) for h in group]
            rows = jnp.concatenate(rows, axis=0).astype(BF)
            prob = probabilities(rows, keys, first_row[0], span)
            out = dot(prob.astype(BF), keys)
            parts += [out[k * span : (k + 1) * span] for k in range(len(group))]
        att_o[s * span : (s + 1) * span] = heads_joined(parts, True).astype(BF)
        for chip in range(chips):
            logs = kv[chip, s, span:height].astype(F32)
            logs_o[chip : chip + 1, s * N : (s + 1) * N] = jnp.sum(logs, axis=0, keepdims=True)


def decay_columns(here, logs, chips, rows):
    shape = (rows, 2 * N)
    head = lax.shift_right_logical(rows_of(shape) + here[0] * rows, 6)
    column = jnp.where(head >= HEADS, head + (N - HEADS), head)
    chosen = (lanes(shape) == column).astype(F32)
    return jnp.exp(dot_t(chosen, logs[...], HIGHEST))


def chain_body(here, blocks, logs, out):
    chips, rows, _ = blocks.shape
    decay = decay_columns(here, logs, chips, rows)
    carry = jnp.zeros((rows, N), F32)
    for chip in range(chips):
        out[chip] = carry.astype(BF)
        carry = decay[:, chip : chip + 1] * carry + blocks[chip].astype(F32)


def chain_back_body(here, blocks, logs, dkv, out):
    chips, rows, _ = blocks.shape
    span = dkv.shape[2]
    decay = decay_columns(here, logs, chips, rows)
    carry = jnp.zeros((rows, N), F32)
    for chip in reversed(range(chips)):
        out[chip, 2 * span :] = carry.astype(BF)
        carry = decay[:, chip : chip + 1] * carry + blocks[chip].astype(F32)
        for s in (0, 1):
            out[chip, s * span : (s + 1) * span] = dkv[chip, s]


def mix_body(y_in, running, c_low, carried, z, att, w_attn, w_out, y_o, g_o, part_o):
    span = y_in.shape[0] // 2
    for s in (0, 1):
        at = slice(s * span, (s + 1) * span)
        from_state = dot_t(c_low[at], carried[s * DI : (s + 1) * DI])
        grown = jnp.exp(running[at])
        for pair in range(HEADS // 2):
            y_o[at, block(pair)] = (
                y_in[at, block(pair)] + from_state[:, block(pair)] * pair_wide(grown, pair)
            )
    gate = z[...].astype(F32)
    gated = (y_o[...] * (gate * sigmoid(gate))).astype(BF)
    g_o[...] = gated
    part_o[...] = dot(att[...], w_attn[...]) + dot(gated, w_out[...])


def feed_body(
    hidden, part, other, gain, w_gate, w_up, w_down, mid_o, normed_o, gate_o, up_o, act_o, part_o
):
    middle = hidden[...] + (part[...] + other[...])
    mid_o[...] = middle
    normed = (middle * inverse_rms(middle) * gain[...]).astype(BF)
    normed_o[...] = normed
    gate, up = dot(normed, w_gate[...]), dot(normed, w_up[...])
    gate_o[...] = gate
    up_o[...] = up
    act = (gate * sigmoid(gate) * up).astype(BF)
    act_o[...] = act
    part_o[...] = dot(act, w_down[...])


def feed_back(low, gates, ups, w_gate, w_up, w_down, dgate_o, dup_o, part_o):
    dact = dot_t(low, w_down[...])
    share = sigmoid(gates)
    dgate = (dact * ups * (share * (1.0 + gates * (1.0 - share)))).astype(BF)
    dup = (dact * (gates * share)).astype(BF)
    dgate_o[...] = dgate
    dup_o[...] = dup
    part_o[...] = dot_t(dgate, w_gate[...]) + dot_t(dup, w_up[...])


def turn_body(
    hidden, part, other, gain, w_gate, w_up, w_down, grad,
    mid_o, normed_o, act_o, more_o, low_o, dgate_o, dup_o, part_o,
):
    middle = hidden[...] + (part[...] + other[...])
    mid_o[...] = middle
    normed = (middle * inverse_rms(middle) * gain[...]).astype(BF)
    normed_o[...] = normed
    gate, up = dot(normed, w_gate[...]), dot(normed, w_up[...])
    act = (gate * sigmoid(gate) * up).astype(BF)
    act_o[...] = act
    more_o[...] = dot(act, w_down[...])
    low = grad[...].astype(BF)
    low_o[...] = low
    feed_back(low, gate, up, w_gate, w_up, w_down, dgate_o, dup_o, part_o)


def pass_back_body(
    dmid, more, other, hidden, gain, gate, up, w_gate, w_up, w_down,
    grad_o, low_o, dgate_o, dup_o, part_o,
):
    dnorm, _ = rms_back(more[...] + other[...], hidden[...], gain[...])
    low = (dmid[...] + dnorm).astype(BF)
    grad_o[...] = low.astype(F32)
    low_o[...] = low
    feed_back(low, gate[...], up[...], w_gate, w_up, w_down, dgate_o, dup_o, part_o)


def mix_back_body(
    grad, part, other, middle, gain, w_attn, w_out, z, y, c_low, running,
    dmid_o, low_o, datt_o, dy_o, dz_o, state_o, dgain_o,
):
    dnorm, dgain = rms_back(part[...] + other[...], middle[...], gain[...])
    dgain_o[...] = dgain
    dmid = grad[...] + dnorm
    dmid_o[...] = dmid
    low = dmid.astype(BF)
    low_o[...] = low
    datt_o[...] = dot_t(low, w_attn[...]).astype(BF)
    dgated = dot_t(low, w_out[...])
    gate = z[...].astype(F32)
    share = sigmoid(gate)
    dz_o[...] = (dgated * y[...] * (share * (1.0 + gate * (1.0 - share)))).astype(BF)
    dy_o[...] = dgated * (gate * share)
    span = y.shape[0] // 2
    for s in (0, 1):
        at = slice(s * span, (s + 1) * span)
        grown = jnp.exp(running[at])
        for pair in range(HEADS // 2):
            dy = dy_o[at, block(pair)] * pair_wide(grown, pair)
            into = t_dot(dy.astype(BF), c_low[at])
            state_o[s * DI + 2 * P_SIZE * pair : s * DI + 2 * P_SIZE * (pair + 1)] = into.astype(BF)


def attend_back_body(first_row, q, kv, datt, cosine, sine, dq_o, dkv_o):
    chips = kv.shape[0]
    span = q.shape[0] // 2
    scale = HEAD_SIZE ** (-0.5)
    for s in (0, 1):
        at = slice(s * span, (s + 1) * span)
        keys = kv[:, s, :span].reshape(chips * span, 2 * HEAD_SIZE)
        parts = []
        dkv = jnp.zeros((chips * span, 2 * HEAD_SIZE), F32)
        for group in head_groups(chips):
            rows = [head_rows(q[at], h, False) for h in group]
            rows = jnp.concatenate(rows, axis=0).astype(BF)
            grads = [head_rows(datt[at], h, True) for h in group]
            grads = jnp.concatenate(grads, axis=0).astype(BF)
            prob = probabilities(rows, keys, first_row[0], span)
            dprob = dot_t(grads, keys)
            inner = jnp.sum(prob * dprob, axis=-1, keepdims=True)
            dscores = (prob * (dprob - inner)).astype(BF)
            dq = dot(dscores, keys) * scale
            parts += [dq[k * span : (k + 1) * span] for k in range(len(group))]
            dkv = dkv + t_dot(dscores, rows) * scale + t_dot(prob.astype(BF), grads)
        dq = heads_joined(parts, False)
        dq_o[at] = rotate(dq, cosine[at, :QW], -sine[at, :QW]).astype(BF)
        dkv_o[:, s] = dkv.astype(BF).reshape(chips, span, 2 * HEAD_SIZE)


def scan_back_body(
    raw, edge, taps, steps_raw, heads, carried, later, dy_in,
    draw_o, dedge_o, dtaps_o, dsteps_o, dheads_o,
):
    span = raw.shape[0] // 2
    wide = (DI, N)
    head_of = (lax.shift_right_logical(rows_of(wide), 6) == lanes(wide)).astype(F32)
    dtaps = [jnp.zeros((1, taps.shape[1]), F32) for _ in range(CONV + 1)]
    dheads = [jnp.zeros((1, N), F32) for _ in range(3)]
    for s in (0, 1):
        at = slice(s * span, (s + 1) * span)
        extended, summed = convolved(raw[at], edge[s], taps[...])
        share = sigmoid(summed)
        conv = summed * share
        steps, logs, running, running_t = decay_of(steps_raw[at], heads[...])
        b_low, c_low = conv[:, DI : DI + N].astype(BF), conv[:, DI + N :].astype(BF)
        inner = dot_t(c_low, b_low)
        grown = jnp.exp(running)
        tail = jnp.exp(running[span - 1 : span] - running)
        low_half = lanes((span, 2 * P_SIZE)) < P_SIZE
        dinner = jnp.zeros((span, span), F32)
        db = jnp.zeros((span, N), F32)
        dc = jnp.zeros((span, N), F32)
        to_running, to_steps, to_tail, to_skip, dxs = [], [], [], [], []
        for pair in range(HEADS // 2):
            state_rows = slice(s * DI + 2 * P_SIZE * pair, s * DI + 2 * P_SIZE * (pair + 1))
            xs = conv[:, block(pair)]
            dy = dy_in[at, block(pair)]
            dy_low = dy.astype(BF)
            steps_wide = pair_wide(steps, pair)
            dt_x = xs * steps_wide
            dt_low = dt_x.astype(BF)
            y_parts, dx_parts = [], []
            for k in (0, 1):
                decays = decays_between(running, running_t, 2 * pair + k)
                mixing = (inner * decays).astype(BF)
                y_parts.append(dot(mixing, dt_low))
                dx_parts.append(t_dot(mixing, dy_low))
                own = jnp.where(low_half == (k == 0), dy, 0.0).astype(BF)
                dinner = dinner + dot_t(own, dt_low) * decays
            y_inner = jnp.where(low_half, y_parts[0], y_parts[1])
            dx_inner = jnp.where(low_half, dx_parts[0], dx_parts[1])
            grown_wide, tail_wide = pair_wide(grown, pair), pair_wide(tail, pair)
            held, after_it = carried[state_rows], later[state_rows]
            y_state = dot_t(c_low, held) * grown_wide
            dx_end = dot_t(b_low, after_it) * tail_wide
            dc = dc + dot((dy * grown_wide).astype(BF), held)
            db = db + dot((dt_x * tail_wide).astype(BF), after_it)
            ddt_x = dx_inner + dx_end
            to_tail.append(dt_x * dx_end)
            to_running.append(
                dy_low.astype(F32) * y_inner + dy * y_state
                - dt_low.astype(F32) * dx_inner - to_tail[-1]
            )
            to_steps.append(xs * ddt_x)
            to_skip.append(jnp.sum(dy * xs, axis=0, keepdims=True))
            dxs.append(ddt_x * steps_wide + dy * pair_wide(heads[2:3], pair))
        dinner_low = dinner.astype(BF)
        dc = dc + dot(dinner_low, b_low)
        db = db + t_dot(dinner_low, c_low)

        def by_head(parts):
            return dot(jnp.concatenate(parts, axis=1), head_of, HIGHEST)

        here_on = slice(s * DI, (s + 1) * DI)
        both = t_dot(head_of, carried[here_on].astype(F32) * later[here_on].astype(F32), HIGHEST)
        through = dot_t(jnp.ones((8, N), F32), both, HIGHEST)[0:1]
        last = jnp.sum(by_head(to_tail), axis=0, keepdims=True) + grown[span - 1 : span] * through
        drunning = by_head(to_running)
        drunning = drunning + jnp.where(rows_of(drunning.shape) == span - 1, last, 0.0)
        square = (span, span)
        upper = (lanes(square) >= rows_of(square)).astype(F32)
        dlogs = dot(upper, drunning, HIGHEST)
        dsteps = by_head(to_steps) - jnp.exp(heads[1:2]) * dlogs
        dsteps = dsteps * sigmoid(steps_raw[at])
        dsteps = jnp.where(lanes(dsteps.shape) < HEADS, dsteps, 0.0)
        dsteps_o[at] = dsteps.astype(BF)
        dheads[0] += jnp.sum(dsteps, axis=0, keepdims=True)
        dheads[1] += jnp.sum(logs * dlogs, axis=0, keepdims=True)
        skips = jnp.broadcast_to(jnp.concatenate(to_skip, axis=1), (8, DI))
        dheads[2] += dot(skips, head_of, HIGHEST)[0:1]

        dconv = jnp.concatenate(dxs + [db, dc], axis=1)
        dsum = dconv * (share * (1.0 + summed * (1.0 - share)))
        zeros = jnp.zeros((8, dsum.shape[1]), F32)
        behind = jnp.concatenate([dsum, zeros], axis=0)
        ahead = jnp.concatenate([zeros, dsum[:8]], axis=0)
        draw = jnp.zeros_like(dsum)
        dedge = jnp.zeros_like(zeros)
        first = extended.shape[0] - span - (CONV - 1)
        for k in range(CONV):
            tap = taps[k : k + 1]
            draw = draw + tap * behind[CONV - 1 - k : CONV - 1 - k + span]
            dedge = dedge + tap * ahead[CONV - 1 - k : CONV - 1 - k + 8]
            dtaps[k] += jnp.sum(dsum * extended[first + k : first + k + span], axis=0, keepdims=True)
        dtaps[CONV] += jnp.sum(dsum, axis=0, keepdims=True)
        draw_o[at] = draw
        dedge_o[s] = jnp.concatenate([zeros, dedge], axis=0).astype(BF)
    for k in range(CONV + 1):
        dtaps_o[k : k + 1] = dtaps[k]
    dtaps_o[CONV + 1 :] = jnp.zeros((8 - CONV - 1, taps.shape[1]), F32)
    for k in range(3):
        dheads_o[k : k + 1] = dheads[k]
    dheads_o[3:] = jnp.zeros((5, N), F32)


def enter_back_body(
    draw, edge, dq, dkv, dsteps, dz, cosine, sine, w_a, w_b, hidden,
    drest_o, dxs_o, part_o, dgain_o,
):
    span = draw.shape[0] // 2
    bc_at = QW + 2 * HEAD_SIZE
    drest_o[:, :QW] = dq[...]
    drest_o[:, bc_at + 2 * N :] = dsteps[...]
    for s in (0, 1):
        at = slice(s * span, (s + 1) * span)
        added = jnp.concatenate(
            [jnp.zeros((span - edge.shape[1], edge.shape[2]), F32), edge[s].astype(F32)], axis=0
        )
        mine = (draw[at] + added).astype(BF)
        dxs_o[at] = mine[:, :DI]
        drest_o[at, bc_at : bc_at + 2 * N] = mine[:, DI:]
        total = jnp.zeros((span, 2 * HEAD_SIZE), F32)
        for chip in range(dkv.shape[0]):
            total = total + dkv[chip, s * span : (s + 1) * span].astype(F32)
        drest_o[at, QW:bc_at] = rotate(total, cosine[at, QW:], -sine[at, QW:]).astype(BF)
    z_a = w_a.shape[1] - REST
    grads = dz[...]
    part_o[...] = dot_t(
        jnp.concatenate([drest_o[...], grads[:, :z_a]], axis=1), w_a[...]
    ) + dot_t(jnp.concatenate([grads[:, z_a:], dxs_o[...]], axis=1), w_b[...])
    rows = hidden[...]
    dgain = jnp.sum(part_o[...] * rows * inverse_rms(rows), axis=0, keepdims=True)
    shape = dgain_o.shape
    dgain_o[...] = jnp.where(rows_of(shape) == 0, dgain, 0.0).astype(BF)


def leave_back_body(dmid, part, other, hidden, gain, grad_o):
    dnorm, _ = rms_back(part[...] + other[...], hidden[...], gain[...])
    grad_o[...] = dmid[...] + dnorm


def in_order_body(at, own, got, out):
    even = at[2] % 2 == 0
    for k in range(own.shape[0]):
        out[0, k] = jnp.where(even, own[k], got[k])
        out[1, k] = jnp.where(even, got[k], own[k])


def line_body(at, pair, over, rest, first, second):
    inner = (at[2] == 1) | (at[2] == 2)
    for k, out in enumerate((first, second)):
        for j in (0, 1):
            far = jnp.where(inner, over[j, k], rest[j, k])
            out[j] = jnp.where(at[2] < 2, pair[j, k], far)
            out[2 + j] = jnp.where(at[2] < 2, far, pair[j, k])


def first_move_body(at, own_a, got_a, own_b, got_b, first, second):
    for index, own, got, out in ((1, own_a, got_a, first), (0, own_b, got_b, second)):
        for z in range(own.shape[0]):
            out[z, 0] = jnp.where(at[index] == 0, own[z], got[z])
            out[z, 1] = jnp.where(at[index] == 0, got[z], own[z])


def second_move_body(at, own_a, got_a, own_b, got_b, first, second):
    for z in range(own_a.shape[0]):
        for k in (0, 1):
            for j in (0, 1):
                own, got = (own_a, got_a) if j == 0 else (got_a, own_a)
                first[4 * z + 2 * k + j] = jnp.where(at[0] == 0, own[z, k], got[z, k])
                own, got = (own_b, got_b) if j == 0 else (got_b, own_b)
                second[4 * z + 2 * j + k] = jnp.where(at[1] == 0, own[z, k], got[z, k])


def cut_body(at, whole, away):
    height = away.shape[0]
    first = pl.multiple_of((1 - at[3]) * height, height)
    away[...] = whole[pl.ds(first, height), :]


def rows_body(chips, at, whole, got, attn, rest, down):
    height = got.shape[0] // chips
    heights = (QW // chips, DI // chips, FFH // chips)
    for j in range(chips):
        block = slice(j * height, (j + 1) * height)
        first = pl.multiple_of(at[3] * got.shape[0] + j * height, height)
        keep = whole[pl.ds(first, height), :]
        for core in (0, 1):
            columns = slice(core * HALF, (core + 1) * HALF)
            both = jnp.where(at[3] == core, keep, got[block])
            mixed, fed = unfolded(both[:, :D]), unfolded(both[:, D:])
            attn[j * heights[0] : (j + 1) * heights[0], columns] = mixed[: heights[0]]
            rest[j * heights[1] : (j + 1) * heights[1], columns] = mixed[heights[0] :]
            down[j * heights[2] : (j + 1) * heights[2], columns] = fed


def sum_body(first, second, third, out):
    out[...] = first[...] + (second[...] + third[...])


def hand_body(first, second, third, out):
    out[...] = (first[...] + (second[...] + third[...])).astype(BF).astype(F32)


def pass_body(value, out):
    out[...] = value[...]


def split_body(at, rows_a, grad_a, rows_b, grad_b, *refs):
    column, (send_a, keep_a, send_b, keep_b) = refs[:-4], refs[-4:]
    depth, _, height, width = send_a.shape
    for z in range(depth):
        for y in (0, 1):
            first = (2 * z + y) * 2 * height
            out = t_dot(rows_a[:, first : first + 2 * height], grad_a[...])
            for v in column:
                shape = (v.shape[0], N)
                unit = ((rows_of(shape) == 0) & (lanes(shape) == N - 1)).astype(F32).astype(BF)
                added = t_dot(v[:, first : first + 2 * height], unit)
                out = jnp.concatenate([out[:, : width - N], out[:, width - N :] + added], axis=1)
            low, high = out[:height], out[height:]
            send_a[z, y] = jnp.where(at[0] == 0, high, low).astype(BF)
            keep_a[z, y] = jnp.where(at[0] == 0, low, high).astype(BF)
        first = z * 4 * height
        out = t_dot(rows_b[:, first : first + 4 * height], grad_b[...])
        for x in (0, 1):
            low = out[x * height : (x + 1) * height]
            high = out[(x + 2) * height : (x + 3) * height]
            send_b[z, x] = jnp.where(at[1] == 0, high, low).astype(BF)
            keep_b[z, x] = jnp.where(at[1] == 0, low, high).astype(BF)


def columns_body(at, act, att, gated, grad_d, grad_m, keep_d, away_d, keep_m, away_m):
    chips = keep_d.shape[0]

    def put(keep, away, chip, first, rows):
        left, right = rows[:, :HALF], rows[:, HALF:]
        here = slice(first, first + rows.shape[0])
        keep[chip, here] = jnp.where(at[3] == 0, left, right).astype(BF)
        away[chip, here] = jnp.where(at[3] == 0, right, left).astype(BF)

    def product(rows, grad, chip):
        height = rows.shape[1] // chips
        return t_dot(rows[:, chip * height : (chip + 1) * height], grad[...])

    from_att = t_dot(att[...], grad_m[...])
    height = QW // chips
    for chip in range(chips):
        put(keep_d, away_d, chip, 0, product(act, grad_d, chip))
        put(keep_m, away_m, chip, 0, from_att[chip * height : (chip + 1) * height])
    from_gated = t_dot(gated[...], grad_m[...])
    tall = DI // chips
    for chip in range(chips):
        put(keep_m, away_m, chip, height, from_gated[chip * tall : (chip + 1) * tall])


def regroup_body(at, keep_d, got_d, keep_m, got_m, send_a, rest_a, send_b, rest_b):
    layers = send_a.shape[0] // 2
    for which, (down, mix) in enumerate(((keep_d, keep_m), (got_d, got_m))):
        core = at[3] if which == 0 else 1 - at[3]
        for z in range(layers):
            to = core * layers + z
            for k in (0, 1):
                low, high = down[4 * z + 2 * k], down[4 * z + 2 * k + 1]
                send_a[to, k] = jnp.where(at[0] == 0, high, low)
                rest_a[to, k] = jnp.where(at[0] == 0, low, high)
                low, high = mix[4 * z + k], mix[4 * z + 2 + k]
                send_b[to, k] = jnp.where(at[1] == 0, high, low)
                rest_b[to, k] = jnp.where(at[1] == 0, low, high)


def fold_body(at, keep_a, got_a, keep_b, got_b, send_a, rest_a, send_b, rest_b):
    for index, keep, got, send, rest in (
        (1, keep_a, got_a, send_a, rest_a),
        (0, keep_b, got_b, send_b, rest_b),
    ):
        for z in range(keep.shape[0]):
            low = keep[z, 0].astype(F32) + got[z, 0].astype(F32)
            high = keep[z, 1].astype(F32) + got[z, 1].astype(F32)
            send[z] = jnp.where(at[index] == 0, high, low).astype(BF)
            rest[z] = jnp.where(at[index] == 0, low, high).astype(BF)


def folded(rows, height):
    if rows.shape[0] == height:
        return rows
    return jnp.concatenate([rows[:height], rows[height:]], axis=1)


def unfolded(rows):
    half = rows.shape[1] // 2
    return jnp.concatenate([rows[:, :half], rows[:, half:]], axis=0)


def z_start_body(at, *refs):
    summands, (far, near) = refs[:-2], refs[-2:]
    height = far.shape[1]
    first = 0
    for one, two in zip(summands[::2], summands[1::2]):
        width = one.shape[1] * one.shape[2] // height
        for out, half in ((near, at[2] // 2), (far, 1 - at[2] // 2)):
            for j in (0, 1):
                total = one[2 * half + j].astype(F32) + two[2 * half + j].astype(F32)
                out[j, :, first : first + width] = folded(total, height).astype(BF)
        first += width


def z_across_body(far, got, out):
    for j in (0, 1):
        out[j] = (far[j].astype(F32) + got[j].astype(F32)).astype(BF)


def z_last_body(at, near, got, send, keep):
    low = near[0].astype(F32) + got[0].astype(F32)
    high = near[1].astype(F32) + got[1].astype(F32)
    even = at[2] % 2 == 0
    send[...] = jnp.where(even, high, low).astype(BF)
    keep[...] = jnp.where(even, low, high).astype(BF)


def add_body(*refs):
    summands, out = refs[:-1], refs[-1]
    height = out.shape[1]
    first = 0
    for one, two in zip(summands[::2], summands[1::2]):
        width = one.shape[1] * one.shape[2] // height
        for z in range(out.shape[0]):
            total = one[z].astype(F32) + two[z].astype(F32)
            out[z, :, first : first + width] = folded(total, height).astype(BF)
        first += width


def choose_body(at, blocks, keep, got, mine, away):
    one = sum(blocks[z].astype(F32) for z in range(blocks.shape[0]))
    two = keep[...].astype(F32) + got[...].astype(F32)
    mine[...] = jnp.where(at[3] == 0, one, two)
    away[...] = jnp.where(at[3] == 0, two, one)


def late_grads_body(at, mine, got, gate_up, down, attn, rest):
    height = attn.shape[0]
    for core in (0, 1):
        for k in (0, 1):
            to = (2 * k + core) * FFH
            from_ = slice(k * FFH, (k + 1) * FFH)
            gate_up[:, to : to + FFH] = jnp.where(at[3] == core, mine[:, from_], got[:, from_])
        here = slice(core * HALF, (core + 1) * HALF)
        from_ = slice(2 * FFH, 2 * FFH + 2 * HALF)
        down[:, here] = unfolded(jnp.where(at[3] == core, mine[:, from_], got[:, from_]))
        from_ = slice(2 * FFH + 2 * HALF, 2 * FFH + 4 * HALF)
        both = unfolded(jnp.where(at[3] == core, mine[:, from_], got[:, from_]))
        attn[:, here] = both[:height]
        rest[:, here] = both[height:]


def early_grads_body(at, mine, got, qkv, into, steps, gain):
    halves_ = [jnp.where(at[3] == core, mine[...], got[...]) for core in (0, 1)]
    rest = [v[:, DI : DI + REST] for v in halves_]
    for core in (0, 1):
        qkv[:, core * QW : (core + 1) * QW] = rest[core][:, :QW]
        into[:, core * DI : (core + 1) * DI] = halves_[core][:, :DI]
        into[:, (2 + core) * DI : (3 + core) * DI] = halves_[core][:, DI + REST :]
    kv = [v[:, QW : QW + 2 * HEAD_SIZE] for v in rest]
    low = lanes(kv[0].shape) < HEAD_SIZE
    turned = [pltpu.roll(v, HEAD_SIZE, 1) for v in kv]
    qkv[:, 2 * QW : 2 * QW + 2 * HEAD_SIZE] = jnp.where(low, kv[0], turned[1])
    qkv[:, 2 * QW + 2 * HEAD_SIZE :] = jnp.where(low, turned[0], kv[1])
    bc_at = QW + 2 * HEAD_SIZE
    into[:, 4 * DI :] = rest[0][:, bc_at : bc_at + 2 * N] + rest[1][:, bc_at : bc_at + 2 * N]
    dt = [v[:, bc_at + 2 * N :] for v in rest]
    gain[...] = dt[0] + dt[1]
    dt = [jnp.where(lanes(v.shape) < HEADS, v, 0.0) for v in dt]
    steps[...] = dt[0] + pltpu.roll(dt[1], HEADS, 1)


def weight_grad(operand, grad_rows):
    return lax.dot_general(
        operand, grad_rows, (((0,), (0,)), ((), ())), preferred_element_type=F32
    ).astype(BF)


def layer_forward(
    kernel, hidden, entering, rows_held, feeding, gains, taps, heads, tables, grad=None
):
    here = lax.axis_index("seq").astype(jnp.int32).reshape(1)
    count = lax.axis_size("seq")
    rows = hidden.shape[0]
    span = rows // 2
    cosine, sine = tables
    w_a, w_b = entering()
    normed, q, kv, raw, z, steps_raw = kernel(
        enter_body,
        [((rows, D), BF), ((rows, QW), BF), ((count, 2, span + 16, N), BF),
         ((rows, DI + 2 * N), BF), ((rows, DI), BF), ((rows, N), F32)],
        hidden, gains[0], w_a, w_b, cosine, sine, heads,
        flops=2 * rows * D * (w_a.shape[1] + w_b.shape[1]),
    )
    kv = to_all(kv)
    tails = raw.reshape(2, span, -1)[:, span - 16 :]
    edge = lax.ppermute(tails, "seq", [(k, k + 1) for k in range(count - 1)])
    w_attn, w_out, w_down = rows_held()
    y_local, c_low, states, running = kernel(
        local_body,
        [((rows, DI), F32), ((rows, N), BF), ((2 * DI, N), BF), ((rows, N), F32)],
        raw, edge, taps, steps_raw, heads, flops=2 * rows * span * DI * 4,
    )
    blocks = to_all(states.reshape(count, -1, N))
    att, logs = kernel(
        attend_body, [((rows, QW), BF), ((count, 2 * N), F32)], here * span, q, kv,
        flops=4 * rows * QW * 2 * count * span,
    )
    (carried,) = kernel(
        chain_body, [(blocks.shape, BF)], here, blocks, logs, flops=blocks.size
    )
    carried = to_all(carried).reshape(2 * DI, N)
    y, gated, part = kernel(
        mix_body, [((rows, DI), F32), ((rows, DI), BF), ((rows, D), F32)],
        y_local, running, c_low, carried, z, att, w_attn, w_out, flops=4 * rows * D * D,
    )
    other = swap(part)
    w_gate, w_up = feeding()
    given = (hidden, part, other, gains[1], w_gate, w_up, w_down)
    wide, low, half = ((rows, D), F32), ((rows, D), BF), ((rows, FFH), BF)
    if grad is None:
        halves_up = ((rows, FFH), F32)
        middle, normed_two, gate, up, act, more = kernel(
            feed_body, [wide, low, halves_up, halves_up, half, wide], *given
        )
        turned = None
    else:
        gate = up = None
        middle, normed_two, act, more, *turned = kernel(
            turn_body, [wide, low, half, wide, low, half, half, wide], *given, grad
        )
    kept = (
        hidden, normed, q, kv, logs, raw, edge, steps_raw, c_low, running, carried, y, z, att,
        gated, middle, normed_two, gate, up, act,
    )
    weights = (w_a, w_b, w_attn, w_out, w_gate, w_up, w_down)
    return (middle, more, swap(more)), kept, weights, turned


def layer_backward(
    kernel, grad_result, turned, kept, weights, gains, taps, heads, tables, reduces, sums=None, before=None,
    owed=None, spread=None,
):
    (
        hidden, normed, q, kv, logs, raw, edge, steps_raw, c_low, running, carried, y, z, att,
        gated, middle, normed_two, gate, up, act,
    ) = kept
    w_a, w_b, w_attn, w_out, w_gate, w_up, w_down = weights
    here = lax.axis_index("seq").astype(jnp.int32).reshape(1)
    count = lax.axis_size("seq")
    rows = hidden.shape[0]
    span = rows // 2
    cosine, sine = tables
    z_a = w_a.shape[1] - REST
    low_down, dgate, dup, part = turned
    other = swap(part)
    result = None
    if owed:
        owed["z"] = reduces.fold(owed["z"])
        late_1 = reduces.z_start(owed["feed"], owed["mixed"])
    else:
        (result,) = kernel(sum_body, [((rows, D), F32)], *sums)
    feed = reduces.open_plain(normed_two, dgate, normed_two, dup)
    if owed:
        reduces.settle(owed["z"])
    dmid, low, datt, dy, dz, into, dgain_two = kernel(
        mix_back_body,
        [((rows, D), F32), ((rows, D), BF), ((rows, QW), BF), ((rows, DI), F32), ((rows, DI), BF),
         ((2 * DI, N), BF), ((1, D), F32)],
        grad_result, part, other, middle, gains[1], w_attn, w_out, z, y, c_low, running,
        flops=4 * rows * D * D,
    )
    blocks = to_all(into.reshape(count, -1, N))
    columns = reduces.columns(act, att, gated, (low_down, low))
    if owed:
        owed["enter"] = reduces.fold(owed["enter"])
        late_1 = reduces.z_across(late_1)
    dq, dkv = kernel(
        attend_back_body, [((rows, QW), BF), ((count, 2, span, N), BF)],
        here * span, q, kv, datt, cosine, sine, flops=10 * rows * QW * 2 * count * span,
    )
    mixed = reduces.open_columns(columns)
    if owed:
        reduces.settle(owed["enter"])
    (back,) = kernel(
        chain_back_body, [((count, 2 * span + blocks.shape[1], N), BF)],
        here, blocks, logs, dkv, flops=blocks.size,
    )
    back = to_all(back)
    later = back[:, 2 * span :].reshape(2 * DI, N)
    feed = reduces.fold(feed)
    if owed:
        late_1 = reduces.z_last(late_1)
    if owed:
        early_1 = reduces.z_start(owed["z"], owed["enter"])
    draw, dedge, dtaps, dsteps, dheads = kernel(
        scan_back_body,
        [((rows, DI + 2 * N), F32), ((2, 16, DI + 2 * N), BF), ((8, DI + 2 * N), F32),
         ((rows, N), BF), ((8, N), F32)],
        raw, edge, taps, steps_raw, heads, carried, later, dy, flops=20 * rows * span * DI,
    )
    dedge = lax.ppermute(dedge, "seq", [(k + 1, k) for k in range(count - 1)])
    small = (dgain_two, dtaps[: CONV + 1], dheads[:3, :HEADS])
    if owed:
        small = spread(small)
    mixed = reduces.fold(mixed)
    reduces.settle(feed)
    if not owed:
        gate_part = reduces.open_plain(normed, dz[:, :z_a], normed, dz[:, z_a:])
    if owed:
        early_1 = reduces.z_across(early_1)
    drest, dxs, part, dgain_one = kernel(
        enter_back_body,
        [((rows, REST), BF), ((rows, DI), BF), ((rows, D), F32), ((16, D), BF)],
        draw, dedge, dq, back, dsteps, dz, cosine, sine, w_a, w_b, hidden,
        flops=2 * rows * D * (w_a.shape[1] + w_b.shape[1]),
    )
    other = swap(part)
    enter = reduces.open_plain(normed, drest, normed, dxs, dgain_one)
    reduces.settle(mixed)
    if owed:
        late = reduces.z_once(feed, mixed)
        gate_part = reduces.open_plain(normed, dz[:, :z_a], normed, dz[:, z_a:])
    given = (dmid, part, other, hidden, gains[0])
    if owed:
        (grad,) = kernel(leave_back_body, [((rows, D), F32)], *given)
    else:
        low, half = ((rows, D), BF), ((rows, FFH), BF)
        grad, *turned = kernel(
            pass_back_body, [((rows, D), F32), low, half, half, ((rows, D), F32)], *given, *before
        )
    if not owed:
        states = {"feed": feed, "mixed": mixed, "z": gate_part, "enter": enter, "result": result}
        return (grad, turned), states, small
    enter = reduces.fold(enter)
    gate_part = reduces.fold(gate_part)
    early_1 = reduces.z_last(early_1)
    kernel.also(late[0])
    early = reduces.z_once(gate_part, enter)
    late = reduces.own(late, late_1)
    return grad, {"late": late, "early": reduces.own(early, early_1)}, small


def halves(array, sizes, at):
    out = []
    for core in (0, 1):
        parts, start = [], at
        for width in sizes:
            half = width // 2
            parts.append(array[:, start + core * half : start + (core + 1) * half])
            start += width
        out.append(parts)
    return out


def rotation_tables(positions):
    half = HEAD_SIZE // 2
    frequency = ROPE_BASE ** (-jnp.arange(half, dtype=F32) / half)
    angles = positions.astype(F32)[:, None] * frequency[None, :]
    cosine, sine = jnp.cos(angles), jnp.sin(angles)
    still = jnp.zeros((positions.shape[0], HEAD_SIZE), F32)
    cosine = jnp.tile(jnp.concatenate([cosine, cosine], axis=1), (1, QH + 1))
    sine = jnp.tile(jnp.concatenate([-sine, sine], axis=1), (1, QH + 1))
    return (
        jnp.tile(jnp.concatenate([cosine, still + 1.0], axis=1), (2, 1)),
        jnp.tile(jnp.concatenate([sine, still], axis=1), (2, 1)),
    )


def columns_home(whole):
    first = lax.axis_index("section") == 0
    blocks = whole.reshape(lax.axis_size("seq") // 2, -1, D)
    left, right = blocks[..., :HALF], blocks[..., HALF:]
    keep = jnp.where(first, left, right)
    got = swap(jnp.where(first, right, left))
    return jnp.concatenate([jnp.where(first, keep, got), jnp.where(first, got, keep)], axis=0)


def by_chip(whole):
    return whole.reshape(lax.axis_size("seq"), -1, whole.shape[1])


NAMES = ("first", "second", "mix", "down", "gate", "up")


def per_device(
    boundary, lengths, norm_gains, w_qkv, w_attn, w_in, w_dt, conv_params, head_params, w_out, w_gate_up, w_down,
):
    core = lax.axis_index("section")
    here = lax.axis_index("seq")
    count = lax.axis_size("seq")
    first = core == 0
    span = boundary.shape[2]
    rows = 2 * span

    qkv = halves(w_qkv[0], (QW * 2, 2 * HEAD_SIZE, 2 * HEAD_SIZE), 0)
    into = halves(w_in[0], (2 * DI, 2 * DI), 0)
    both_bc = w_in[0][:, 4 * DI :]
    steps = halves(w_dt[0], (SH,), 0)
    ups = halves(w_gate_up[0], (2 * FFH, 2 * FFH), 0)
    mix = jnp.concatenate([w_attn[0], w_out[0]], axis=0)
    cut = []
    for k in (0, 1):
        step = jnp.pad(steps[k][0], ((0, 0), (0, N - HEADS)))
        z_k = into[k][0]
        z_a = z_k.shape[1] // 2
        cut.append(
            {
                "first": jnp.concatenate(qkv[k] + [both_bc, step, z_k[:, :z_a]], axis=1),
                "second": jnp.concatenate([z_k[:, z_a:], into[k][1]], axis=1),
                "mix": mix[:, k * HALF : (k + 1) * HALF],
                "gate": ups[k][0],
                "up": ups[k][1],
                "down": w_down[0][:, k * HALF : (k + 1) * HALF],
            }
        )
    layers = ({}, {})
    for name in NAMES:
        own = jnp.where(first, cut[0][name], cut[1][name])
        got = swap(jnp.where(first, cut[1][name], cut[0][name]))
        layers[0][name] = jnp.where(first, own, got)
        layers[1][name] = jnp.where(first, got, own)

    kernel = Order()
    gathers = Gathers([(layers[0]["first"], layers[0]["second"])], kernel)
    rest_0 = Whole(layers[0], kernel, NAMES[2:])
    all_1 = Whole(layers[1], kernel, NAMES)
    rest_0.start()
    all_1.start()
    small = jnp.concatenate([norm_gains[0].reshape(-1), conv_params[0].reshape(-1)])
    small_other = swap(small)
    small = jnp.stack([jnp.where(first, small, small_other), jnp.where(first, small_other, small)])
    small = to_all(jnp.broadcast_to(small[None], (count,) + small.shape))
    small = small.swapaxes(0, 1).astype(F32)
    width = norm_gains.shape[2]
    gains = small[:, :, : 2 * width].reshape(2, count, 2, width).swapaxes(1, 2).reshape(2, 2, D)
    taps = small[:, :, 2 * width :].reshape(2, count, CONV + 1, -1).swapaxes(1, 2)
    taps = taps.reshape(2, CONV + 1, 4 * DI // 2 + 2 * N)
    taps = jnp.concatenate(
        [jnp.where(first, taps[..., :DI], taps[..., DI : 2 * DI]), taps[..., 2 * DI :]], axis=-1
    )
    heads_other = swap(head_params[0])
    heads = jnp.stack(
        [
            jnp.where(first, head_params[0], heads_other),
            jnp.where(first, heads_other, head_params[0]),
        ]
    )
    heads = jnp.where(first, heads[..., :HEADS], heads[..., HEADS:])
    heads = jnp.pad(heads, ((0, 0), (0, 5), (0, N - HEADS)))
    gains = gains.reshape(2, 2, 1, D)
    taps = jnp.pad(taps, ((0, 0), (0, 8 - CONV - 1), (0, 0)))

    other = swap(boundary[0])
    inputs = jnp.where(first, boundary[0], other).reshape(rows, D).astype(F32)
    positions = here * span + jnp.arange(span, dtype=jnp.int32)
    live = (positions[None, :] < lengths[:, None]).astype(F32)
    cotangent = jnp.where(first, other, boundary[0]).astype(F32) * live[..., None]
    cotangent = cotangent.reshape(rows, D)
    tables = rotation_tables(positions)

    reduces = Reduces(kernel)
    def pair(whole, one, two):
        return lambda: (whole.part(one), whole.part(two))

    sums, kept_0, weights_0, _ = layer_forward(
        kernel, inputs, lambda: gathers.get(0), rest_0.rows, pair(rest_0, "gate", "up"),
        gains[0], taps[0], heads[0], tables,
    )
    (handed,) = kernel(hand_body, [((rows, D), F32)], *sums)
    sums, kept_1, weights_1, turned = layer_forward(
        kernel, handed, pair(all_1, "first", "second"), all_1.rows, pair(all_1, "gate", "up"),
        gains[1], taps[1], heads[1], tables, cotangent,
    )
    conv_width = conv_params.shape[2]

    def spread(small_0, small_1):
        grad_gains, grad_taps, grad_heads = (jnp.stack(v) for v in zip(small_0, small_1))
        xs_part, none = grad_taps[..., :DI], jnp.zeros((2, CONV + 1, DI), F32)
        wide = jnp.concatenate(
            [jnp.where(first, xs_part, none), jnp.where(first, none, xs_part), grad_taps[..., DI:]],
            axis=2,
        )
        none = jnp.zeros((2, 3, HEADS), F32)
        head_wide = jnp.concatenate(
            [jnp.where(first, grad_heads, none), jnp.where(first, none, grad_heads)], axis=2
        )
        gains_once = jnp.where(first, grad_gains, 0.0)
        flat = jnp.concatenate(
            [
                gains_once.reshape(2, count, width).swapaxes(0, 1),
                wide.reshape(2, CONV + 1, count, conv_width)
                .transpose(2, 0, 1, 3)
                .reshape(count, 2, -1),
                jnp.broadcast_to(head_wide.reshape(1, 2, -1), (count, 2, 3 * SH)),
            ],
            axis=2,
        )
        flat = jnp.pad(flat, ((0, 0), (0, 0), (0, -flat.shape[2] % N)))
        return to_all(flat)

    kernel.weight = WEIGHT
    (grad_handed, turned), grads_1, small_1 = layer_backward(
        kernel, cotangent, turned, kept_1, weights_1, gains[1], taps[1], heads[1], tables, reduces,
        sums, kept_0[-3:-1] + weights_0[-3:],
    )
    grad_inputs, grads_0, small_0 = layer_backward(
        kernel, grad_handed, turned, kept_0, weights_0, gains[0], taps[0], heads[0], tables, reduces, owed=grads_1,
        spread=lambda small_0: spread(small_0, small_1),
    )

    at = corner()
    height = w_qkv.shape[1]
    grad_gu, grad_down, grad_attn, grad_out = kernel(
        late_grads_body,
        [(v.shape[1:], F32) for v in (w_gate_up, w_down, w_attn, w_out)], at, *grads_0["late"],
    )
    grad_qkv, grad_in, grad_dt, gain_one = kernel(
        early_grads_body,
        [((height, w_qkv.shape[2]), F32), ((height, w_in.shape[2]), F32), ((height, N), F32),
         ((height, N), F32)],
        at, *grads_0["early"],
    )

    flat = jnp.sum(small_0, axis=0)
    flat = jnp.where(first, flat[0], flat[1]) + swap(jnp.where(first, flat[1], flat[0]))
    taps_at = width
    heads_at = taps_at + (CONV + 1) * conv_width
    grad_gains = jnp.stack([gain_one[:, N - 1], flat[:taps_at]])
    grad_conv = flat[taps_at:heads_at].reshape(CONV + 1, conv_width)
    total_heads = flat[heads_at : heads_at + 3 * SH].reshape(3, SH)

    ends = jnp.where(first, grad_inputs, grads_1["result"]).reshape(2, span, D)
    outs = (
        ends, grad_gains, grad_qkv, grad_attn, grad_in, grad_dt[:, :SH], grad_conv, total_heads,
        grad_out, grad_gu, grad_down,
    )
    return tuple(out[None] for out in outs)


def solution(mesh):
    by_rows = P("section", "seq", None)
    by_columns = P("section", None, "seq")
    whole = P("section", None, None)
    ends = P("section", None, "seq", None)
    in_specs = (
        ends, P(), by_columns, by_rows, by_rows, by_rows, by_rows, by_columns, whole, by_rows,
        by_rows, by_rows,
    )
    out_specs = (
        ends, by_columns, by_rows, by_rows, by_rows, by_rows, by_columns, whole, by_rows, by_rows,
        by_rows,
    )
    return jax.shard_map(
        per_device, mesh=mesh, in_specs=in_specs, out_specs=out_specs, check_vma=False
    )
```

```python
from functools import partial
from math import isqrt

import jax
import jax.numpy as jnp
from jax import lax
from jax.experimental import pallas as pl
from jax.experimental.pallas import tpu as pltpu
from jax.sharding import PartitionSpec as P

D = 1024
HEAD_SIZE = 64
SH = 24
P_SIZE = 64
N = 128
CONV = 4
QH = 4
HEADS = SH // 2
QW = QH * HEAD_SIZE
DI = HEADS * P_SIZE
FFH = 1024
HALF = D // 2
REST = QW + 2 * HEAD_SIZE + 2 * N + N

eps = 1e-05
ROPE_BASE = 100000000000.0
HIGHEST = lax.Precision.HIGHEST
BF = jnp.bfloat16
F32 = jnp.float32
VMEM_BYTES = 56 * 2**20
WEIGHT = 3 * 10**11


def grid_of(count):
    side = isqrt(count // 4)
    return (count // (side * side), side, side)


def place_on(axis):
    dims = grid_of(lax.axis_size("seq"))
    strides = (dims[1] * dims[2], dims[2], 1)
    return lax.axis_index("seq") // strides[axis] % dims[axis], dims[axis], strides[axis]


def hop(value, axis, moves):
    count = lax.axis_size("seq")
    _, length, stride = place_on(axis)
    pairs = []
    for source in range(count):
        at = source // stride % length
        if at in moves and moves[at] < length:
            pairs.append((source, source + (moves[at] - at) * stride))
    return lax.ppermute(value, "seq", pairs)


NEXT = {0: 1, 1: 0, 2: 3, 3: 2}
INNER = {1: 2, 2: 1}
OUTWARD = {1: 0, 2: 3}
INWARD = {0: 1, 3: 2}


def swap(value):
    return lax.ppermute(value, "section", [(0, 1), (1, 0)])


def both_cores(value):
    return value + swap(value)


def line_gather(part, axis, dim):
    at, length, _ = place_on(axis)
    got = hop(part, axis, NEXT)
    even = at % 2 == 0
    pair = jnp.stack([jnp.where(even, part, got), jnp.where(even, got, part)], axis=dim)
    if length == 2:
        return pair
    over = hop(pair, axis, INNER)
    rest = hop(over, axis, OUTWARD)
    far = jnp.where((at == 1) | (at == 2), over, rest)
    return jnp.concatenate(
        [jnp.where(at < 2, pair, far), jnp.where(at < 2, far, pair)], axis=dim
    )


def corner():
    places = [place_on(axis)[0] for axis in (2, 1, 0)]
    return jnp.stack(places + [lax.axis_index("section")]).astype(jnp.int32)


class Gathers:
    def __init__(self, pairs, kernel):
        self.pairs, self.kernel = pairs, kernel
        self.count = lax.axis_size("seq")
        self.depth, self.side, _ = grid_of(self.count)
        self.state = [None] * len(pairs)
        self.steps = [(step, k) for k in range(len(pairs)) for step in (1, 2, 3, 4, 5)]
        self.place = corner()
        self.start(0)

    def start(self, at):
        if at < len(self.pairs):
            stacked = jnp.stack(self.pairs[at])
            self.state[at] = (stacked, hop(stacked, 0, NEXT))

    def until(self, step, at):
        while (step, at) in self.steps:
            now, pair = self.steps.pop(0)
            getattr(self, "step_%d" % now)(pair)

    def step_1(self, at):
        own, got = self.state[at]
        (pair,) = self.kernel(in_order_body, [((2,) + own.shape, BF)], self.place, own, got)
        self.state[at] = (pair, hop(pair, 0, INNER))

    def step_2(self, at):
        pair, over = self.state[at]
        self.kernel.also(over)
        self.state[at] = (pair, over, hop(over, 0, OUTWARD))

    def step_3(self, at):
        pair = self.state[at][0]
        shape = (4,) + pair.shape[2:]
        first, second = self.kernel(line_body, [(shape, BF)] * 2, self.place, *self.state[at])
        if self.side == 2:
            self.state[at] = (first, hop(first, 1, NEXT), second, hop(second, 2, NEXT))
        else:
            self.state[at] = (line_gather(first, 1, 1), line_gather(second, 2, 1))

    def step_4(self, at):
        if self.side == 2:
            first = self.state[at][0]
            shape = (4, 2) + first.shape[1:]
            shape_b = (4, 2) + self.state[at][2].shape[1:]
            first, second = self.kernel(
                first_move_body, [(shape, BF), (shape_b, BF)], self.place, *self.state[at]
            )
            self.state[at] = (first, hop(first, 2, NEXT), second, hop(second, 1, NEXT))
        else:
            first, second = self.state[at]
            self.state[at] = (line_gather(first, 2, 2), line_gather(second, 1, 1))
        self.start(at + 1)

    def step_5(self, at):
        if self.side != 2:
            self.state[at] = [v.reshape(D, -1) for v in self.state[at]]
            return
        shapes = [(self.count,) + self.state[at][k].shape[2:] for k in (0, 2)]
        first, second = self.kernel(
            second_move_body, [(v, BF) for v in shapes], self.place, *self.state[at]
        )
        self.state[at] = [first.reshape(D, -1), second.reshape(D, -1)]

    def get(self, at):
        self.until(5, at)
        return self.state[at]


class Whole:
    def __init__(self, shards, kernel, names):
        height = shards["gate"].shape[0]
        self.kernel, self.at = kernel, {}
        parts, first = [], 0
        for name in names:
            shard = shards[name]
            part = jnp.concatenate(
                [shard[k : k + height] for k in range(0, shard.shape[0], height)], axis=1
            )
            parts.append(part)
            self.at[name] = (first, part.shape[1])
            first += part.shape[1]
        self.flat = jnp.concatenate(parts, axis=1)

    def start(self):
        self.whole = lax.all_gather(self.flat, "seq", axis=0, tiled=True)

    def part(self, name):
        return Part(self.whole, *self.at[name])

    def rows(self):
        part = Part(self.whole, self.at["mix"][0], 2 * D)
        (away,) = self.kernel(cut_body, [((part.shape[0] // 2, 2 * D), BF)], corner(), part)
        return self.kernel(
            partial(rows_body, lax.axis_size("seq") // 2),
            [((QW, D), BF), ((DI, D), BF), ((FFH, D), BF)], corner(), part, swap(away),
        )


def add(a, b, kind):
    return (a.astype(F32) + b.astype(F32)).astype(kind)


def line_reduce(parts, axis, dim):
    at, length, _ = place_on(axis)

    def pick(array, index):
        return lax.dynamic_index_in_dim(array, index, dim, False)

    if length == 4:
        halves = parts.reshape(parts.shape[:dim] + (2, 2) + parts.shape[dim + 1 :])
        far, near = pick(halves, 1 - at // 2), pick(halves, at // 2)
        far = add(far, hop(far, axis, INWARD), BF)
        parts = add(near, hop(far, axis, INNER), BF)
    got = hop(pick(parts, 1 - at % 2), axis, NEXT)
    return pick(parts, at % 2), got


def z_groups():
    count = lax.axis_size("seq")
    depth, side, _ = grid_of(count)
    plane = side * side
    return [[z * plane + k for z in range(depth)] for k in range(plane)]


class Reduces:
    def __init__(self, kernel):
        self.kernel = kernel
        self.paired = grid_of(lax.axis_size("seq"))[2] == 2

    def open_plain(self, rows_a, grad_a, rows_b, grad_b, *column):
        count = lax.axis_size("seq")
        depth = grid_of(count)[0]
        if not self.paired:
            first = weight_grad(rows_a, grad_a)
            for v in column:
                first = first.at[:, -1].add(v[0])
            return self.open_whole(by_chip(first), by_chip(weight_grad(rows_b, grad_b)))
        height = rows_a.shape[1] // count
        shape = (depth, 2, height, grad_a.shape[1])
        parts = self.kernel(
            split_body, [(shape, BF)] * 4, corner(), rows_a, grad_a, rows_b, grad_b, *column,
            flops=4 * rows_a.size * grad_a.shape[1],
        )
        return self.open(parts)

    def columns(self, act, att, gated, grad):
        half = lax.axis_size("seq") // 2
        if not self.paired:
            mix = jnp.concatenate(
                [weight_grad(v, grad[1]).reshape(half, -1, D) for v in (att, gated)], axis=1
            )
            return columns_home(weight_grad(act, grad[0])), columns_home(mix)
        down, mix = (half, FFH // half, HALF), (half, (QW + DI) // half, HALF)
        keep_d, away_d, keep_m, away_m = self.kernel(
            columns_body, [(down, BF), (down, BF), (mix, BF), (mix, BF)],
            corner(), act, att, gated, *grad, flops=4 * act.size * D,
        )
        return keep_d, swap(away_d), keep_m, swap(away_m)

    def open_columns(self, columns):
        if not self.paired:
            return self.open_whole(*columns)
        depth = grid_of(lax.axis_size("seq"))[0]
        shapes = [((depth, 2) + columns[k].shape[1:], BF) for k in range(4)]
        return self.open(self.kernel(regroup_body, shapes, corner(), *columns))

    def open(self, parts):
        send_a, keep_a, send_b, keep_b = parts
        got_a, got_b = hop(send_a, 2, NEXT), hop(send_b, 1, NEXT)
        return keep_a, got_a, keep_b, got_b

    def open_whole(self, first, second):
        dims = grid_of(lax.axis_size("seq"))
        first, second = (v.reshape(dims + v.shape[1:]) for v in (first, second))
        keep_a, got_a = line_reduce(first, 2, 2)
        keep_b, got_b = line_reduce(second, 1, 1)
        return keep_a, got_a, keep_b, got_b

    def fold(self, state):
        keep_a, got_a, keep_b, got_b = state
        if not self.paired:
            first, second = add(keep_a, got_a, BF), add(keep_b, got_b, BF)
            return *line_reduce(first, 1, 1), *line_reduce(second, 2, 1)
        shape = keep_a.shape[:1] + keep_a.shape[2:]
        shape_b = keep_b.shape[:1] + keep_b.shape[2:]
        send_a, keep_a, send_b, keep_b = self.kernel(
            fold_body, [(shape, BF), (shape, BF), (shape_b, BF), (shape_b, BF)],
            corner(), keep_a, got_a, keep_b, got_b,
        )
        return keep_a, hop(send_a, 1, NEXT), keep_b, hop(send_b, 2, NEXT)

    def settle(self, state):
        self.kernel.also(state[1])
        self.kernel.also(state[3])

    def flat(self, state):
        height = D // lax.axis_size("seq")
        return height, sum(v.shape[1] * v.shape[2] // height for v in (state[0], state[2]))

    def z_start(self, *states):
        height = self.flat(states[0])[0]
        shape = (2, height, sum(self.flat(v)[1] for v in states))
        far, near = self.kernel(
            z_start_body, [(shape, BF)] * 2, corner(), *[v for state in states for v in state]
        )
        return far, hop(far, 0, INWARD), near

    def z_across(self, state):
        far, got, near = state
        (far,) = self.kernel(z_across_body, [(far.shape, BF)], far, got)
        return near, hop(far, 0, INNER)

    def z_last(self, state):
        near, got = state
        shape = near.shape[1:]
        send, keep = self.kernel(z_last_body, [(shape, BF)] * 2, corner(), near, got)
        return keep, hop(send, 0, NEXT)

    def z_once(self, *states):
        height = self.flat(states[0])[0]
        shape = (states[0][0].shape[0], height, sum(self.flat(v)[1] for v in states))
        (whole,) = self.kernel(add_body, [(shape, BF)], *[v for state in states for v in state])
        whole = lax.all_to_all(whole, "seq", 0, 0, tiled=True, axis_index_groups=z_groups())
        return (whole,)

    def own(self, first, second):
        shape = second[0].shape
        mine, away = self.kernel(choose_body, [(shape, F32)] * 2, corner(), *first, *second)
        return mine, swap(away)


def to_all(blocks):
    return lax.all_to_all(blocks, "seq", 0, 0, tiled=True)


class Part:
    def __init__(self, whole, first, width):
        self.whole, self.first = whole, first
        self.shape, self.dtype = (whole.shape[0], width), whole.dtype


class Order:
    def __init__(self):
        self.before = []
        self.weight = 15 * 10**9

    def also(self, value):
        self.before = self.before + [value]

    def __call__(self, body, outs, *args, flops=0):
        out_shape = [jax.ShapeDtypeStruct(shape, kind) for shape, kind in outs]
        count, extra = len(args), len(self.before)
        parts = [k for k, v in enumerate(args) if isinstance(v, Part)]

        def run(*refs):
            given = list(refs[:count])
            results = refs[count + extra : count + extra + len(outs)]
            scratch = refs[count + extra + len(outs) :]
            copies = []
            for slot, k in enumerate(parts):
                source = given[k].at[:, args[k].first : args[k].first + args[k].shape[1]]
                copies.append(pltpu.make_async_copy(source, scratch[slot], scratch[-1].at[slot]))
                copies[-1].start()
                given[k] = scratch[slot]
            for copy in copies:
                copy.wait()
            body(*given, *results)

        def space(v):
            if isinstance(v, Part):
                return pl.ANY
            return pltpu.SMEM if v.dtype == jnp.int32 else pltpu.VMEM

        scratch = [pltpu.VMEM(args[k].shape, args[k].dtype) for k in parts]
        if parts:
            scratch.append(pltpu.SemaphoreType.DMA((len(parts),)))
        results = pl.pallas_call(
            run,
            out_shape=out_shape,
            in_specs=[pl.BlockSpec(memory_space=space(v)) for v in args]
            + [pl.BlockSpec(memory_space=pl.ANY)] * extra,
            out_specs=[pl.BlockSpec(memory_space=pltpu.VMEM) for _ in outs],
            scratch_shapes=scratch,
            compiler_params=pltpu.CompilerParams(vmem_limit_bytes=VMEM_BYTES),
            cost_estimate=pl.CostEstimate(flops=self.weight, bytes_accessed=0, transcendentals=0),
        )(*[v.whole if isinstance(v, Part) else v for v in args], *self.before)
        self.before = [min(results, key=lambda v: v.size)]
        return results


def dot(a, b, precision=None):
    return jnp.dot(a, b, preferred_element_type=F32, precision=precision)


def dot_t(a, b, precision=None):
    return lax.dot_general(
        a, b, (((1,), (1,)), ((), ())), preferred_element_type=F32, precision=precision
    )


def t_dot(a, b, precision=None):
    return lax.dot_general(
        a, b, (((0,), (0,)), ((), ())), preferred_element_type=F32, precision=precision
    )


def sigmoid(v):
    return 1.0 / (1.0 + jnp.exp(-v))


def softplus(v):
    return jnp.maximum(v, 0.0) + jnp.log1p(jnp.exp(-jnp.abs(v)))


def lanes(shape):
    return lax.broadcasted_iota(jnp.int32, shape, len(shape) - 1)


def rows_of(shape):
    return lax.broadcasted_iota(jnp.int32, shape, len(shape) - 2)


def rotate(rows, cosine, sine):
    width = rows.shape[-1]
    half = HEAD_SIZE // 2
    low = (lanes(rows.shape) // half) % 2 == 0
    turned = jnp.where(
        low, pltpu.roll(rows, width - half, 1), pltpu.roll(rows, half, 1)
    )
    return rows * cosine + turned * sine


def inverse_rms(rows):
    return lax.rsqrt(jnp.mean(rows * rows, axis=-1, keepdims=True) + eps)


def rms_back(grad, rows, gain):
    scale = inverse_rms(rows)
    scaled = grad * gain
    inner = jnp.mean(rows * scaled, axis=-1, keepdims=True)
    return (
        scale * scaled - rows * (scale * scale * scale * inner),
        jnp.sum(grad * rows * scale, axis=0, keepdims=True),
    )


def pair_wide(columns, pair):
    shape = (columns.shape[0], 2 * P_SIZE)
    return jnp.where(
        lanes(shape) < P_SIZE,
        jnp.broadcast_to(columns[:, 2 * pair : 2 * pair + 1], shape),
        jnp.broadcast_to(columns[:, 2 * pair + 1 : 2 * pair + 2], shape),
    )


def block(pair):
    return slice(2 * P_SIZE * pair, 2 * P_SIZE * (pair + 1))


def convolved(raw, edge, taps):
    span = raw.shape[0]
    extended = jnp.concatenate([edge.astype(F32), raw.astype(F32)], axis=0)
    at = edge.shape[0] - (CONV - 1)
    summed = jnp.broadcast_to(taps[CONV : CONV + 1], raw.shape)
    for k in range(CONV):
        summed = summed + taps[k : k + 1] * extended[at + k : at + k + span]
    return extended, summed


def decay_of(steps_raw, heads):
    span = steps_raw.shape[0]
    steps = softplus(steps_raw)
    logs = -steps * jnp.exp(heads[1:2])
    square = (span, span)
    lower = (lanes(square) <= rows_of(square)).astype(F32)
    upper = (lanes(square) >= rows_of(square)).astype(F32)
    return steps, logs, dot(lower, logs, HIGHEST), t_dot(logs, upper, HIGHEST)


def decays_between(running, running_t, head):
    span = running.shape[0]
    gap = running[:, head : head + 1] - running_t[head : head + 1, :]
    square = (span, span)
    return jnp.exp(jnp.where(lanes(square) <= rows_of(square), gap, -1e30))


def enter_body(
    hidden, gain, w_a, w_b, cosine, sine, heads, normed_o, q_o, kv_o, raw_o, z_o, steps_o
):
    rows = hidden[...]
    normed = (rows * inverse_rms(rows) * gain[...]).astype(BF)
    normed_o[...] = normed
    a, b = dot(normed, w_a[...]), dot(normed, w_b[...])
    turned = rotate(a[:, : QW + 2 * HEAD_SIZE], cosine[...], sine[...])
    q_o[...] = turned[:, :QW].astype(BF)
    kv = turned[:, QW:].astype(BF)
    bc_at = QW + 2 * HEAD_SIZE
    z_a = w_a.shape[1] - REST
    z_o[:, :z_a] = a[:, REST:].astype(BF)
    z_o[:, z_a:] = b[:, : DI - z_a].astype(BF)
    raw_o[:, :DI] = b[:, DI - z_a :].astype(BF)
    raw_o[:, DI:] = a[:, bc_at : bc_at + 2 * N].astype(BF)
    steps_raw = a[:, bc_at + 2 * N : REST] + heads[0:1]
    steps_o[...] = steps_raw
    logs = -softplus(steps_raw) * jnp.exp(heads[1:2])
    span = rows.shape[0] // 2
    for s in (0, 1):
        total = jnp.sum(logs[s * span : (s + 1) * span], axis=0, keepdims=True)
        high = total.astype(BF).astype(F32)
        middle = (total - high).astype(BF).astype(F32)
        low = total - high - middle
        at = rows_of((16, N))
        packed = jnp.where(
            at == 0, high, jnp.where(at == 1, middle, jnp.where(at == 2, low, 0.0))
        ).astype(BF)
        for chip in range(kv_o.shape[0]):
            kv_o[chip, s, :span] = kv[s * span : (s + 1) * span]
            kv_o[chip, s, span:] = packed


def local_body(raw, edge, taps, steps_raw, heads, y_o, c_o, state_o, running_o):
    span = raw.shape[0] // 2
    for s in (0, 1):
        at = slice(s * span, (s + 1) * span)
        _, summed = convolved(raw[at], edge[s], taps[...])
        conv = summed * sigmoid(summed)
        steps, _, running, running_t = decay_of(steps_raw[at], heads[...])
        running_o[at] = running
        b_low, c_low = conv[:, DI : DI + N].astype(BF), conv[:, DI + N :].astype(BF)
        c_o[at] = c_low
        inner = dot_t(c_low, b_low)
        tail = jnp.exp(running[span - 1 : span] - running)
        low_half = lanes((span, 2 * P_SIZE)) < P_SIZE
        for pair in range(HEADS // 2):
            xs = conv[:, block(pair)]
            dt_x = xs * pair_wide(steps, pair)
            dt_low = dt_x.astype(BF)
            mixed = [
                dot((inner * decays_between(running, running_t, h)).astype(BF), dt_low)
                for h in (2 * pair, 2 * pair + 1)
            ]
            skip = pair_wide(heads[2:3], pair)
            y_o[at, block(pair)] = jnp.where(low_half, mixed[0], mixed[1]) + skip * xs
            end = t_dot((dt_x * pair_wide(tail, pair)).astype(BF), b_low)
            state_o[s * DI + 2 * P_SIZE * pair : s * DI + 2 * P_SIZE * (pair + 1)] = end.astype(BF)


def head_rows(rows, head, upper):
    half = rows[:, block(head // 2)].astype(F32)
    if (head % 2 == 1) != upper:
        half = pltpu.roll(half, P_SIZE, 1)
    keep = lanes(half.shape) >= P_SIZE if upper else lanes(half.shape) < P_SIZE
    return jnp.where(keep, half, 0.0)


def heads_joined(parts, upper):
    out = []
    for even, odd in zip(parts[::2], parts[1::2]):
        low_half = lanes(even.shape) < P_SIZE
        if upper:
            out.append(jnp.where(low_half, pltpu.roll(even, P_SIZE, 1), odd))
        else:
            out.append(jnp.where(low_half, even, pltpu.roll(odd, P_SIZE, 1)))
    return jnp.concatenate(out, axis=1)


def head_groups(chips):
    size = QH if chips <= 16 else 1
    return [list(range(k, k + size)) for k in range(0, QH, size)]


def probabilities(queries, keys, first_row, span):
    scores = dot_t(queries, keys) * HEAD_SIZE ** (-0.5)
    shape = (span, keys.shape[0])
    allowed = lanes(shape) <= rows_of(shape) + first_row
    bias = jnp.where(allowed, 0.0, -1e30)
    scores = scores + jnp.concatenate([bias] * (queries.shape[0] // span), axis=0)
    shifted = jnp.exp(scores - jnp.max(scores, axis=-1, keepdims=True))
    return shifted / jnp.sum(shifted, axis=-1, keepdims=True)


def attend_body(first_row, q, kv, att_o, logs_o):
    chips, _, height, _ = kv.shape
    span = q.shape[0] // 2
    for s in (0, 1):
        keys = kv[:, s, :span].reshape(chips * span, 2 * HEAD_SIZE)
        parts = []
        for group in head_groups(chips):
            rows = [head_rows(q[s * span : (s + 1) * span], h, False) for h in group]
            rows = jnp.concatenate(rows, axis=0).astype(BF)
            prob = probabilities(rows, keys, first_row[0], span)
            out = dot(prob.astype(BF), keys)
            parts += [out[k * span : (k + 1) * span] for k in range(len(group))]
        att_o[s * span : (s + 1) * span] = heads_joined(parts, True).astype(BF)
        for chip in range(chips):
            logs = kv[chip, s, span:height].astype(F32)
            logs_o[chip : chip + 1, s * N : (s + 1) * N] = jnp.sum(logs, axis=0, keepdims=True)


def decay_columns(here, logs, chips, rows):
    shape = (rows, 2 * N)
    head = lax.shift_right_logical(rows_of(shape) + here[0] * rows, 6)
    column = jnp.where(head >= HEADS, head + (N - HEADS), head)
    chosen = (lanes(shape) == column).astype(F32)
    return jnp.exp(dot_t(chosen, logs[...], HIGHEST))


def chain_body(here, blocks, logs, out):
    chips, rows, _ = blocks.shape
    decay = decay_columns(here, logs, chips, rows)
    carry = jnp.zeros((rows, N), F32)
    for chip in range(chips):
        out[chip] = carry.astype(BF)
        carry = decay[:, chip : chip + 1] * carry + blocks[chip].astype(F32)


def chain_back_body(here, blocks, logs, dkv, out):
    chips, rows, _ = blocks.shape
    span = dkv.shape[2]
    decay = decay_columns(here, logs, chips, rows)
    carry = jnp.zeros((rows, N), F32)
    for chip in reversed(range(chips)):
        out[chip, 2 * span :] = carry.astype(BF)
        carry = decay[:, chip : chip + 1] * carry + blocks[chip].astype(F32)
        for s in (0, 1):
            out[chip, s * span : (s + 1) * span] = dkv[chip, s]


def mix_body(y_in, running, c_low, carried, z, att, w_attn, w_out, y_o, g_o, part_o):
    span = y_in.shape[0] // 2
    for s in (0, 1):
        at = slice(s * span, (s + 1) * span)
        from_state = dot_t(c_low[at], carried[s * DI : (s + 1) * DI])
        grown = jnp.exp(running[at])
        for pair in range(HEADS // 2):
            y_o[at, block(pair)] = (
                y_in[at, block(pair)] + from_state[:, block(pair)] * pair_wide(grown, pair)
            )
    gate = z[...].astype(F32)
    gated = (y_o[...] * (gate * sigmoid(gate))).astype(BF)
    g_o[...] = gated
    part_o[...] = dot(att[...], w_attn[...]) + dot(gated, w_out[...])


def feed_body(
    hidden, part, other, gain, w_gate, w_up, w_down, mid_o, normed_o, gate_o, up_o, act_o, part_o
):
    middle = hidden[...] + (part[...] + other[...])
    mid_o[...] = middle
    normed = (middle * inverse_rms(middle) * gain[...]).astype(BF)
    normed_o[...] = normed
    gate, up = dot(normed, w_gate[...]), dot(normed, w_up[...])
    gate_o[...] = gate
    up_o[...] = up
    act = (gate * sigmoid(gate) * up).astype(BF)
    act_o[...] = act
    part_o[...] = dot(act, w_down[...])


def feed_back(low, gates, ups, w_gate, w_up, w_down, dgate_o, dup_o, part_o):
    dact = dot_t(low, w_down[...])
    share = sigmoid(gates)
    dgate = (dact * ups * (share * (1.0 + gates * (1.0 - share)))).astype(BF)
    dup = (dact * (gates * share)).astype(BF)
    dgate_o[...] = dgate
    dup_o[...] = dup
    part_o[...] = dot_t(dgate, w_gate[...]) + dot_t(dup, w_up[...])


def turn_body(
    hidden, part, other, gain, w_gate, w_up, w_down, grad,
    mid_o, normed_o, act_o, more_o, low_o, dgate_o, dup_o, part_o,
):
    middle = hidden[...] + (part[...] + other[...])
    mid_o[...] = middle
    normed = (middle * inverse_rms(middle) * gain[...]).astype(BF)
    normed_o[...] = normed
    gate, up = dot(normed, w_gate[...]), dot(normed, w_up[...])
    act = (gate * sigmoid(gate) * up).astype(BF)
    act_o[...] = act
    more_o[...] = dot(act, w_down[...])
    low = grad[...].astype(BF)
    low_o[...] = low
    feed_back(low, gate, up, w_gate, w_up, w_down, dgate_o, dup_o, part_o)


def pass_back_body(
    dmid, more, other, hidden, gain, gate, up, w_gate, w_up, w_down,
    grad_o, low_o, dgate_o, dup_o, part_o,
):
    dnorm, _ = rms_back(more[...] + other[...], hidden[...], gain[...])
    low = (dmid[...] + dnorm).astype(BF)
    grad_o[...] = low.astype(F32)
    low_o[...] = low
    feed_back(low, gate[...], up[...], w_gate, w_up, w_down, dgate_o, dup_o, part_o)


def mix_back_body(
    grad, part, other, middle, gain, w_attn, w_out, z, y, c_low, running,
    dmid_o, low_o, datt_o, dy_o, dz_o, state_o, dgain_o,
):
    dnorm, dgain = rms_back(part[...] + other[...], middle[...], gain[...])
    dgain_o[...] = dgain
    dmid = grad[...] + dnorm
    dmid_o[...] = dmid
    low = dmid.astype(BF)
    low_o[...] = low
    datt_o[...] = dot_t(low, w_attn[...]).astype(BF)
    dgated = dot_t(low, w_out[...])
    gate = z[...].astype(F32)
    share = sigmoid(gate)
    dz_o[...] = (dgated * y[...] * (share * (1.0 + gate * (1.0 - share)))).astype(BF)
    dy_o[...] = dgated * (gate * share)
    span = y.shape[0] // 2
    for s in (0, 1):
        at = slice(s * span, (s + 1) * span)
        grown = jnp.exp(running[at])
        for pair in range(HEADS // 2):
            dy = dy_o[at, block(pair)] * pair_wide(grown, pair)
            into = t_dot(dy.astype(BF), c_low[at])
            state_o[s * DI + 2 * P_SIZE * pair : s * DI + 2 * P_SIZE * (pair + 1)] = into.astype(BF)


def attend_back_body(first_row, q, kv, datt, cosine, sine, dq_o, dkv_o):
    chips = kv.shape[0]
    span = q.shape[0] // 2
    scale = HEAD_SIZE ** (-0.5)
    for s in (0, 1):
        at = slice(s * span, (s + 1) * span)
        keys = kv[:, s, :span].reshape(chips * span, 2 * HEAD_SIZE)
        parts = []
        dkv = jnp.zeros((chips * span, 2 * HEAD_SIZE), F32)
        for group in head_groups(chips):
            rows = [head_rows(q[at], h, False) for h in group]
            rows = jnp.concatenate(rows, axis=0).astype(BF)
            grads = [head_rows(datt[at], h, True) for h in group]
            grads = jnp.concatenate(grads, axis=0).astype(BF)
            prob = probabilities(rows, keys, first_row[0], span)
            dprob = dot_t(grads, keys)
            inner = jnp.sum(prob * dprob, axis=-1, keepdims=True)
            dscores = (prob * (dprob - inner)).astype(BF)
            dq = dot(dscores, keys) * scale
            parts += [dq[k * span : (k + 1) * span] for k in range(len(group))]
            dkv = dkv + t_dot(dscores, rows) * scale + t_dot(prob.astype(BF), grads)
        dq = heads_joined(parts, False)
        dq_o[at] = rotate(dq, cosine[at, :QW], -sine[at, :QW]).astype(BF)
        dkv_o[:, s] = dkv.astype(BF).reshape(chips, span, 2 * HEAD_SIZE)


def scan_back_body(
    raw, edge, taps, steps_raw, heads, carried, later, dy_in,
    draw_o, dedge_o, dtaps_o, dsteps_o, dheads_o,
):
    span = raw.shape[0] // 2
    wide = (DI, N)
    head_of = (lax.shift_right_logical(rows_of(wide), 6) == lanes(wide)).astype(F32)
    dtaps = [jnp.zeros((1, taps.shape[1]), F32) for _ in range(CONV + 1)]
    dheads = [jnp.zeros((1, N), F32) for _ in range(3)]
    for s in (0, 1):
        at = slice(s * span, (s + 1) * span)
        extended, summed = convolved(raw[at], edge[s], taps[...])
        share = sigmoid(summed)
        conv = summed * share
        steps, logs, running, running_t = decay_of(steps_raw[at], heads[...])
        b_low, c_low = conv[:, DI : DI + N].astype(BF), conv[:, DI + N :].astype(BF)
        inner = dot_t(c_low, b_low)
        grown = jnp.exp(running)
        tail = jnp.exp(running[span - 1 : span] - running)
        low_half = lanes((span, 2 * P_SIZE)) < P_SIZE
        dinner = jnp.zeros((span, span), F32)
        db = jnp.zeros((span, N), F32)
        dc = jnp.zeros((span, N), F32)
        to_running, to_steps, to_tail, to_skip, dxs = [], [], [], [], []
        for pair in range(HEADS // 2):
            state_rows = slice(s * DI + 2 * P_SIZE * pair, s * DI + 2 * P_SIZE * (pair + 1))
            xs = conv[:, block(pair)]
            dy = dy_in[at, block(pair)]
            dy_low = dy.astype(BF)
            steps_wide = pair_wide(steps, pair)
            dt_x = xs * steps_wide
            dt_low = dt_x.astype(BF)
            y_parts, dx_parts = [], []
            for k in (0, 1):
                decays = decays_between(running, running_t, 2 * pair + k)
                mixing = (inner * decays).astype(BF)
                y_parts.append(dot(mixing, dt_low))
                dx_parts.append(t_dot(mixing, dy_low))
                own = jnp.where(low_half == (k == 0), dy, 0.0).astype(BF)
                dinner = dinner + dot_t(own, dt_low) * decays
            y_inner = jnp.where(low_half, y_parts[0], y_parts[1])
            dx_inner = jnp.where(low_half, dx_parts[0], dx_parts[1])
            grown_wide, tail_wide = pair_wide(grown, pair), pair_wide(tail, pair)
            held, after_it = carried[state_rows], later[state_rows]
            y_state = dot_t(c_low, held) * grown_wide
            dx_end = dot_t(b_low, after_it) * tail_wide
            dc = dc + dot((dy * grown_wide).astype(BF), held)
            db = db + dot((dt_x * tail_wide).astype(BF), after_it)
            ddt_x = dx_inner + dx_end
            to_tail.append(dt_x * dx_end)
            to_running.append(
                dy_low.astype(F32) * y_inner + dy * y_state
                - dt_low.astype(F32) * dx_inner - to_tail[-1]
            )
            to_steps.append(xs * ddt_x)
            to_skip.append(jnp.sum(dy * xs, axis=0, keepdims=True))
            dxs.append(ddt_x * steps_wide + dy * pair_wide(heads[2:3], pair))
        dinner_low = dinner.astype(BF)
        dc = dc + dot(dinner_low, b_low)
        db = db + t_dot(dinner_low, c_low)

        def by_head(parts):
            return dot(jnp.concatenate(parts, axis=1), head_of, HIGHEST)

        here_on = slice(s * DI, (s + 1) * DI)
        both = t_dot(head_of, carried[here_on].astype(F32) * later[here_on].astype(F32), HIGHEST)
        through = dot_t(jnp.ones((8, N), F32), both, HIGHEST)[0:1]
        last = jnp.sum(by_head(to_tail), axis=0, keepdims=True) + grown[span - 1 : span] * through
        drunning = by_head(to_running)
        drunning = drunning + jnp.where(rows_of(drunning.shape) == span - 1, last, 0.0)
        square = (span, span)
        upper = (lanes(square) >= rows_of(square)).astype(F32)
        dlogs = dot(upper, drunning, HIGHEST)
        dsteps = by_head(to_steps) - jnp.exp(heads[1:2]) * dlogs
        dsteps = dsteps * sigmoid(steps_raw[at])
        dsteps = jnp.where(lanes(dsteps.shape) < HEADS, dsteps, 0.0)
        dsteps_o[at] = dsteps.astype(BF)
        dheads[0] += jnp.sum(dsteps, axis=0, keepdims=True)
        dheads[1] += jnp.sum(logs * dlogs, axis=0, keepdims=True)
        skips = jnp.broadcast_to(jnp.concatenate(to_skip, axis=1), (8, DI))
        dheads[2] += dot(skips, head_of, HIGHEST)[0:1]

        dconv = jnp.concatenate(dxs + [db, dc], axis=1)
        dsum = dconv * (share * (1.0 + summed * (1.0 - share)))
        zeros = jnp.zeros((8, dsum.shape[1]), F32)
        behind = jnp.concatenate([dsum, zeros], axis=0)
        ahead = jnp.concatenate([zeros, dsum[:8]], axis=0)
        draw = jnp.zeros_like(dsum)
        dedge = jnp.zeros_like(zeros)
        first = extended.shape[0] - span - (CONV - 1)
        for k in range(CONV):
            tap = taps[k : k + 1]
            draw = draw + tap * behind[CONV - 1 - k : CONV - 1 - k + span]
            dedge = dedge + tap * ahead[CONV - 1 - k : CONV - 1 - k + 8]
            dtaps[k] += jnp.sum(dsum * extended[first + k : first + k + span], axis=0, keepdims=True)
        dtaps[CONV] += jnp.sum(dsum, axis=0, keepdims=True)
        draw_o[at] = draw
        dedge_o[s] = jnp.concatenate([zeros, dedge], axis=0).astype(BF)
    for k in range(CONV + 1):
        dtaps_o[k : k + 1] = dtaps[k]
    dtaps_o[CONV + 1 :] = jnp.zeros((8 - CONV - 1, taps.shape[1]), F32)
    for k in range(3):
        dheads_o[k : k + 1] = dheads[k]
    dheads_o[3:] = jnp.zeros((5, N), F32)


def enter_back_body(
    draw, edge, dq, dkv, dsteps, dz, cosine, sine, w_a, w_b, hidden,
    drest_o, dxs_o, part_o, dgain_o,
):
    span = draw.shape[0] // 2
    bc_at = QW + 2 * HEAD_SIZE
    drest_o[:, :QW] = dq[...]
    drest_o[:, bc_at + 2 * N :] = dsteps[...]
    for s in (0, 1):
        at = slice(s * span, (s + 1) * span)
        added = jnp.concatenate(
            [jnp.zeros((span - edge.shape[1], edge.shape[2]), F32), edge[s].astype(F32)], axis=0
        )
        mine = (draw[at] + added).astype(BF)
        dxs_o[at] = mine[:, :DI]
        drest_o[at, bc_at : bc_at + 2 * N] = mine[:, DI:]
        total = jnp.zeros((span, 2 * HEAD_SIZE), F32)
        for chip in range(dkv.shape[0]):
            total = total + dkv[chip, s * span : (s + 1) * span].astype(F32)
        drest_o[at, QW:bc_at] = rotate(total, cosine[at, QW:], -sine[at, QW:]).astype(BF)
    z_a = w_a.shape[1] - REST
    grads = dz[...]
    part_o[...] = dot_t(
        jnp.concatenate([drest_o[...], grads[:, :z_a]], axis=1), w_a[...]
    ) + dot_t(jnp.concatenate([grads[:, z_a:], dxs_o[...]], axis=1), w_b[...])
    rows = hidden[...]
    dgain = jnp.sum(part_o[...] * rows * inverse_rms(rows), axis=0, keepdims=True)
    shape = dgain_o.shape
    dgain_o[...] = jnp.where(rows_of(shape) == 0, dgain, 0.0).astype(BF)


def leave_back_body(dmid, part, other, hidden, gain, grad_o):
    dnorm, _ = rms_back(part[...] + other[...], hidden[...], gain[...])
    grad_o[...] = dmid[...] + dnorm


def in_order_body(at, own, got, out):
    even = at[2] % 2 == 0
    for k in range(own.shape[0]):
        out[0, k] = jnp.where(even, own[k], got[k])
        out[1, k] = jnp.where(even, got[k], own[k])


def line_body(at, pair, over, rest, first, second):
    inner = (at[2] == 1) | (at[2] == 2)
    for k, out in enumerate((first, second)):
        for j in (0, 1):
            far = jnp.where(inner, over[j, k], rest[j, k])
            out[j] = jnp.where(at[2] < 2, pair[j, k], far)
            out[2 + j] = jnp.where(at[2] < 2, far, pair[j, k])


def first_move_body(at, own_a, got_a, own_b, got_b, first, second):
    for index, own, got, out in ((1, own_a, got_a, first), (0, own_b, got_b, second)):
        for z in range(own.shape[0]):
            out[z, 0] = jnp.where(at[index] == 0, own[z], got[z])
            out[z, 1] = jnp.where(at[index] == 0, got[z], own[z])


def second_move_body(at, own_a, got_a, own_b, got_b, first, second):
    for z in range(own_a.shape[0]):
        for k in (0, 1):
            for j in (0, 1):
                own, got = (own_a, got_a) if j == 0 else (got_a, own_a)
                first[4 * z + 2 * k + j] = jnp.where(at[0] == 0, own[z, k], got[z, k])
                own, got = (own_b, got_b) if j == 0 else (got_b, own_b)
                second[4 * z + 2 * j + k] = jnp.where(at[1] == 0, own[z, k], got[z, k])


def cut_body(at, whole, away):
    height = away.shape[0]
    first = pl.multiple_of((1 - at[3]) * height, height)
    away[...] = whole[pl.ds(first, height), :]


def rows_body(chips, at, whole, got, attn, rest, down):
    height = got.shape[0] // chips
    heights = (QW // chips, DI // chips, FFH // chips)
    for j in range(chips):
        block = slice(j * height, (j + 1) * height)
        first = pl.multiple_of(at[3] * got.shape[0] + j * height, height)
        keep = whole[pl.ds(first, height), :]
        for core in (0, 1):
            columns = slice(core * HALF, (core + 1) * HALF)
            both = jnp.where(at[3] == core, keep, got[block])
            mixed, fed = unfolded(both[:, :D]), unfolded(both[:, D:])
            attn[j * heights[0] : (j + 1) * heights[0], columns] = mixed[: heights[0]]
            rest[j * heights[1] : (j + 1) * heights[1], columns] = mixed[heights[0] :]
            down[j * heights[2] : (j + 1) * heights[2], columns] = fed


def sum_body(first, second, third, out):
    out[...] = first[...] + (second[...] + third[...])


def hand_body(first, second, third, out):
    out[...] = (first[...] + (second[...] + third[...])).astype(BF).astype(F32)


def pass_body(value, out):
    out[...] = value[...]


def split_body(at, rows_a, grad_a, rows_b, grad_b, *refs):
    column, (send_a, keep_a, send_b, keep_b) = refs[:-4], refs[-4:]
    depth, _, height, width = send_a.shape
    for z in range(depth):
        for y in (0, 1):
            first = (2 * z + y) * 2 * height
            out = t_dot(rows_a[:, first : first + 2 * height], grad_a[...])
            for v in column:
                shape = (v.shape[0], N)
                unit = ((rows_of(shape) == 0) & (lanes(shape) == N - 1)).astype(F32).astype(BF)
                added = t_dot(v[:, first : first + 2 * height], unit)
                out = jnp.concatenate([out[:, : width - N], out[:, width - N :] + added], axis=1)
            low, high = out[:height], out[height:]
            send_a[z, y] = jnp.where(at[0] == 0, high, low).astype(BF)
            keep_a[z, y] = jnp.where(at[0] == 0, low, high).astype(BF)
        first = z * 4 * height
        out = t_dot(rows_b[:, first : first + 4 * height], grad_b[...])
        for x in (0, 1):
            low = out[x * height : (x + 1) * height]
            high = out[(x + 2) * height : (x + 3) * height]
            send_b[z, x] = jnp.where(at[1] == 0, high, low).astype(BF)
            keep_b[z, x] = jnp.where(at[1] == 0, low, high).astype(BF)


def columns_body(at, act, att, gated, grad_d, grad_m, keep_d, away_d, keep_m, away_m):
    chips = keep_d.shape[0]

    def put(keep, away, chip, first, rows):
        left, right = rows[:, :HALF], rows[:, HALF:]
        here = slice(first, first + rows.shape[0])
        keep[chip, here] = jnp.where(at[3] == 0, left, right).astype(BF)
        away[chip, here] = jnp.where(at[3] == 0, right, left).astype(BF)

    def product(rows, grad, chip):
        height = rows.shape[1] // chips
        return t_dot(rows[:, chip * height : (chip + 1) * height], grad[...])

    from_att = t_dot(att[...], grad_m[...])
    height = QW // chips
    for chip in range(chips):
        put(keep_d, away_d, chip, 0, product(act, grad_d, chip))
        put(keep_m, away_m, chip, 0, from_att[chip * height : (chip + 1) * height])
    from_gated = t_dot(gated[...], grad_m[...])
    tall = DI // chips
    for chip in range(chips):
        put(keep_m, away_m, chip, height, from_gated[chip * tall : (chip + 1) * tall])


def regroup_body(at, keep_d, got_d, keep_m, got_m, send_a, rest_a, send_b, rest_b):
    layers = send_a.shape[0] // 2
    for which, (down, mix) in enumerate(((keep_d, keep_m), (got_d, got_m))):
        core = at[3] if which == 0 else 1 - at[3]
        for z in range(layers):
            to = core * layers + z
            for k in (0, 1):
                low, high = down[4 * z + 2 * k], down[4 * z + 2 * k + 1]
                send_a[to, k] = jnp.where(at[0] == 0, high, low)
                rest_a[to, k] = jnp.where(at[0] == 0, low, high)
                low, high = mix[4 * z + k], mix[4 * z + 2 + k]
                send_b[to, k] = jnp.where(at[1] == 0, high, low)
                rest_b[to, k] = jnp.where(at[1] == 0, low, high)


def fold_body(at, keep_a, got_a, keep_b, got_b, send_a, rest_a, send_b, rest_b):
    for index, keep, got, send, rest in (
        (1, keep_a, got_a, send_a, rest_a),
        (0, keep_b, got_b, send_b, rest_b),
    ):
        for z in range(keep.shape[0]):
            low = keep[z, 0].astype(F32) + got[z, 0].astype(F32)
            high = keep[z, 1].astype(F32) + got[z, 1].astype(F32)
            send[z] = jnp.where(at[index] == 0, high, low).astype(BF)
            rest[z] = jnp.where(at[index] == 0, low, high).astype(BF)


def folded(rows, height):
    if rows.shape[0] == height:
        return rows
    return jnp.concatenate([rows[:height], rows[height:]], axis=1)


def unfolded(rows):
    half = rows.shape[1] // 2
    return jnp.concatenate([rows[:, :half], rows[:, half:]], axis=0)


def z_start_body(at, *refs):
    summands, (far, near) = refs[:-2], refs[-2:]
    height = far.shape[1]
    first = 0
    for one, two in zip(summands[::2], summands[1::2]):
        width = one.shape[1] * one.shape[2] // height
        for out, half in ((near, at[2] // 2), (far, 1 - at[2] // 2)):
            for j in (0, 1):
                total = one[2 * half + j].astype(F32) + two[2 * half + j].astype(F32)
                out[j, :, first : first + width] = folded(total, height).astype(BF)
        first += width


def z_across_body(far, got, out):
    for j in (0, 1):
        out[j] = (far[j].astype(F32) + got[j].astype(F32)).astype(BF)


def z_last_body(at, near, got, send, keep):
    low = near[0].astype(F32) + got[0].astype(F32)
    high = near[1].astype(F32) + got[1].astype(F32)
    even = at[2] % 2 == 0
    send[...] = jnp.where(even, high, low).astype(BF)
    keep[...] = jnp.where(even, low, high).astype(BF)


def add_body(*refs):
    summands, out = refs[:-1], refs[-1]
    height = out.shape[1]
    first = 0
    for one, two in zip(summands[::2], summands[1::2]):
        width = one.shape[1] * one.shape[2] // height
        for z in range(out.shape[0]):
            total = one[z].astype(F32) + two[z].astype(F32)
            out[z, :, first : first + width] = folded(total, height).astype(BF)
        first += width


def choose_body(at, blocks, keep, got, mine, away):
    one = sum(blocks[z].astype(F32) for z in range(blocks.shape[0]))
    two = keep[...].astype(F32) + got[...].astype(F32)
    mine[...] = jnp.where(at[3] == 0, one, two)
    away[...] = jnp.where(at[3] == 0, two, one)


def late_grads_body(at, mine, got, gate_up, down, attn, rest):
    height = attn.shape[0]
    for core in (0, 1):
        for k in (0, 1):
            to = (2 * k + core) * FFH
            from_ = slice(k * FFH, (k + 1) * FFH)
            gate_up[:, to : to + FFH] = jnp.where(at[3] == core, mine[:, from_], got[:, from_])
        here = slice(core * HALF, (core + 1) * HALF)
        from_ = slice(2 * FFH, 2 * FFH + 2 * HALF)
        down[:, here] = unfolded(jnp.where(at[3] == core, mine[:, from_], got[:, from_]))
        from_ = slice(2 * FFH + 2 * HALF, 2 * FFH + 4 * HALF)
        both = unfolded(jnp.where(at[3] == core, mine[:, from_], got[:, from_]))
        attn[:, here] = both[:height]
        rest[:, here] = both[height:]


def early_grads_body(at, mine, got, qkv, into, steps, gain):
    halves_ = [jnp.where(at[3] == core, mine[...], got[...]) for core in (0, 1)]
    rest = [v[:, DI : DI + REST] for v in halves_]
    for core in (0, 1):
        qkv[:, core * QW : (core + 1) * QW] = rest[core][:, :QW]
        into[:, core * DI : (core + 1) * DI] = halves_[core][:, :DI]
        into[:, (2 + core) * DI : (3 + core) * DI] = halves_[core][:, DI + REST :]
    kv = [v[:, QW : QW + 2 * HEAD_SIZE] for v in rest]
    low = lanes(kv[0].shape) < HEAD_SIZE
    turned = [pltpu.roll(v, HEAD_SIZE, 1) for v in kv]
    qkv[:, 2 * QW : 2 * QW + 2 * HEAD_SIZE] = jnp.where(low, kv[0], turned[1])
    qkv[:, 2 * QW + 2 * HEAD_SIZE :] = jnp.where(low, turned[0], kv[1])
    bc_at = QW + 2 * HEAD_SIZE
    into[:, 4 * DI :] = rest[0][:, bc_at : bc_at + 2 * N] + rest[1][:, bc_at : bc_at + 2 * N]
    dt = [v[:, bc_at + 2 * N :] for v in rest]
    gain[...] = dt[0] + dt[1]
    dt = [jnp.where(lanes(v.shape) < HEADS, v, 0.0) for v in dt]
    steps[...] = dt[0] + pltpu.roll(dt[1], HEADS, 1)


def weight_grad(operand, grad_rows):
    return lax.dot_general(
        operand, grad_rows, (((0,), (0,)), ((), ())), preferred_element_type=F32
    ).astype(BF)


def layer_forward(
    kernel, hidden, entering, rows_held, feeding, gains, taps, heads, tables, grad=None
):
    here = lax.axis_index("seq").astype(jnp.int32).reshape(1)
    count = lax.axis_size("seq")
    rows = hidden.shape[0]
    span = rows // 2
    cosine, sine = tables
    w_a, w_b = entering()
    normed, q, kv, raw, z, steps_raw = kernel(
        enter_body,
        [((rows, D), BF), ((rows, QW), BF), ((count, 2, span + 16, N), BF),
         ((rows, DI + 2 * N), BF), ((rows, DI), BF), ((rows, N), F32)],
        hidden, gains[0], w_a, w_b, cosine, sine, heads,
        flops=2 * rows * D * (w_a.shape[1] + w_b.shape[1]),
    )
    kv = to_all(kv)
    tails = raw.reshape(2, span, -1)[:, span - 16 :]
    edge = lax.ppermute(tails, "seq", [(k, k + 1) for k in range(count - 1)])
    w_attn, w_out, w_down = rows_held()
    y_local, c_low, states, running = kernel(
        local_body,
        [((rows, DI), F32), ((rows, N), BF), ((2 * DI, N), BF), ((rows, N), F32)],
        raw, edge, taps, steps_raw, heads, flops=2 * rows * span * DI * 4,
    )
    blocks = to_all(states.reshape(count, -1, N))
    att, logs = kernel(
        attend_body, [((rows, QW), BF), ((count, 2 * N), F32)], here * span, q, kv,
        flops=4 * rows * QW * 2 * count * span,
    )
    (carried,) = kernel(
        chain_body, [(blocks.shape, BF)], here, blocks, logs, flops=blocks.size
    )
    carried = to_all(carried).reshape(2 * DI, N)
    y, gated, part = kernel(
        mix_body, [((rows, DI), F32), ((rows, DI), BF), ((rows, D), F32)],
        y_local, running, c_low, carried, z, att, w_attn, w_out, flops=4 * rows * D * D,
    )
    other = swap(part)
    w_gate, w_up = feeding()
    given = (hidden, part, other, gains[1], w_gate, w_up, w_down)
    wide, low, half = ((rows, D), F32), ((rows, D), BF), ((rows, FFH), BF)
    if grad is None:
        halves_up = ((rows, FFH), F32)
        middle, normed_two, gate, up, act, more = kernel(
            feed_body, [wide, low, halves_up, halves_up, half, wide], *given
        )
        turned = None
    else:
        gate = up = None
        middle, normed_two, act, more, *turned = kernel(
            turn_body, [wide, low, half, wide, low, half, half, wide], *given, grad
        )
    kept = (
        hidden, normed, q, kv, logs, raw, edge, steps_raw, c_low, running, carried, y, z, att,
        gated, middle, normed_two, gate, up, act,
    )
    weights = (w_a, w_b, w_attn, w_out, w_gate, w_up, w_down)
    return (middle, more, swap(more)), kept, weights, turned


def layer_backward(
    kernel, grad_result, turned, kept, weights, gains, taps, heads, tables, reduces, sums=None, before=None,
    owed=None, spread=None,
):
    (
        hidden, normed, q, kv, logs, raw, edge, steps_raw, c_low, running, carried, y, z, att,
        gated, middle, normed_two, gate, up, act,
    ) = kept
    w_a, w_b, w_attn, w_out, w_gate, w_up, w_down = weights
    here = lax.axis_index("seq").astype(jnp.int32).reshape(1)
    count = lax.axis_size("seq")
    rows = hidden.shape[0]
    span = rows // 2
    cosine, sine = tables
    z_a = w_a.shape[1] - REST
    low_down, dgate, dup, part = turned
    other = swap(part)
    result = None
    if owed:
        owed["z"] = reduces.fold(owed["z"])
        late_1 = reduces.z_start(owed["feed"], owed["mixed"])
    else:
        (result,) = kernel(sum_body, [((rows, D), F32)], *sums)
    feed = reduces.open_plain(normed_two, dgate, normed_two, dup)
    if owed:
        reduces.settle(owed["z"])
    dmid, low, datt, dy, dz, into, dgain_two = kernel(
        mix_back_body,
        [((rows, D), F32), ((rows, D), BF), ((rows, QW), BF), ((rows, DI), F32), ((rows, DI), BF),
         ((2 * DI, N), BF), ((1, D), F32)],
        grad_result, part, other, middle, gains[1], w_attn, w_out, z, y, c_low, running,
        flops=4 * rows * D * D,
    )
    blocks = to_all(into.reshape(count, -1, N))
    columns = reduces.columns(act, att, gated, (low_down, low))
    if owed:
        owed["enter"] = reduces.fold(owed["enter"])
        late_1 = reduces.z_across(late_1)
    dq, dkv = kernel(
        attend_back_body, [((rows, QW), BF), ((count, 2, span, N), BF)],
        here * span, q, kv, datt, cosine, sine, flops=10 * rows * QW * 2 * count * span,
    )
    mixed = reduces.open_columns(columns)
    if owed:
        reduces.settle(owed["enter"])
    (back,) = kernel(
        chain_back_body, [((count, 2 * span + blocks.shape[1], N), BF)],
        here, blocks, logs, dkv, flops=blocks.size,
    )
    back = to_all(back)
    later = back[:, 2 * span :].reshape(2 * DI, N)
    feed = reduces.fold(feed)
    if owed:
        late_1 = reduces.z_last(late_1)
    if owed:
        early_1 = reduces.z_start(owed["z"], owed["enter"])
    draw, dedge, dtaps, dsteps, dheads = kernel(
        scan_back_body,
        [((rows, DI + 2 * N), F32), ((2, 16, DI + 2 * N), BF), ((8, DI + 2 * N), F32),
         ((rows, N), BF), ((8, N), F32)],
        raw, edge, taps, steps_raw, heads, carried, later, dy, flops=20 * rows * span * DI,
    )
    dedge = lax.ppermute(dedge, "seq", [(k + 1, k) for k in range(count - 1)])
    small = (dgain_two, dtaps[: CONV + 1], dheads[:3, :HEADS])
    if owed:
        small = spread(small)
    mixed = reduces.fold(mixed)
    reduces.settle(feed)
    if not owed:
        gate_part = reduces.open_plain(normed, dz[:, :z_a], normed, dz[:, z_a:])
    if owed:
        early_1 = reduces.z_across(early_1)
    drest, dxs, part, dgain_one = kernel(
        enter_back_body,
        [((rows, REST), BF), ((rows, DI), BF), ((rows, D), F32), ((16, D), BF)],
        draw, dedge, dq, back, dsteps, dz, cosine, sine, w_a, w_b, hidden,
        flops=2 * rows * D * (w_a.shape[1] + w_b.shape[1]),
    )
    other = swap(part)
    enter = reduces.open_plain(normed, drest, normed, dxs, dgain_one)
    reduces.settle(mixed)
    if owed:
        late = reduces.z_once(feed, mixed)
        gate_part = reduces.open_plain(normed, dz[:, :z_a], normed, dz[:, z_a:])
    given = (dmid, part, other, hidden, gains[0])
    if owed:
        (grad,) = kernel(leave_back_body, [((rows, D), F32)], *given)
    else:
        low, half = ((rows, D), BF), ((rows, FFH), BF)
        grad, *turned = kernel(
            pass_back_body, [((rows, D), F32), low, half, half, ((rows, D), F32)], *given, *before
        )
    if not owed:
        states = {"feed": feed, "mixed": mixed, "z": gate_part, "enter": enter, "result": result}
        return (grad, turned), states, small
    enter = reduces.fold(enter)
    gate_part = reduces.fold(gate_part)
    early_1 = reduces.z_last(early_1)
    early = reduces.z_once(gate_part, enter)
    late = reduces.own(late, late_1)
    return grad, {"late": late, "early": reduces.own(early, early_1)}, small


def halves(array, sizes, at):
    out = []
    for core in (0, 1):
        parts, start = [], at
        for width in sizes:
            half = width // 2
            parts.append(array[:, start + core * half : start + (core + 1) * half])
            start += width
        out.append(parts)
    return out


def rotation_tables(positions):
    half = HEAD_SIZE // 2
    frequency = ROPE_BASE ** (-jnp.arange(half, dtype=F32) / half)
    angles = positions.astype(F32)[:, None] * frequency[None, :]
    cosine, sine = jnp.cos(angles), jnp.sin(angles)
    still = jnp.zeros((positions.shape[0], HEAD_SIZE), F32)
    cosine = jnp.tile(jnp.concatenate([cosine, cosine], axis=1), (1, QH + 1))
    sine = jnp.tile(jnp.concatenate([-sine, sine], axis=1), (1, QH + 1))
    return (
        jnp.tile(jnp.concatenate([cosine, still + 1.0], axis=1), (2, 1)),
        jnp.tile(jnp.concatenate([sine, still], axis=1), (2, 1)),
    )


def columns_home(whole):
    first = lax.axis_index("section") == 0
    blocks = whole.reshape(lax.axis_size("seq") // 2, -1, D)
    left, right = blocks[..., :HALF], blocks[..., HALF:]
    keep = jnp.where(first, left, right)
    got = swap(jnp.where(first, right, left))
    return jnp.concatenate([jnp.where(first, keep, got), jnp.where(first, got, keep)], axis=0)


def by_chip(whole):
    return whole.reshape(lax.axis_size("seq"), -1, whole.shape[1])


NAMES = ("first", "second", "mix", "down", "gate", "up")


def per_device(
    boundary, lengths, norm_gains, w_qkv, w_attn, w_in, w_dt, conv_params, head_params, w_out, w_gate_up, w_down,
):
    core = lax.axis_index("section")
    here = lax.axis_index("seq")
    count = lax.axis_size("seq")
    first = core == 0
    span = boundary.shape[2]
    rows = 2 * span

    qkv = halves(w_qkv[0], (QW * 2, 2 * HEAD_SIZE, 2 * HEAD_SIZE), 0)
    into = halves(w_in[0], (2 * DI, 2 * DI), 0)
    both_bc = w_in[0][:, 4 * DI :]
    steps = halves(w_dt[0], (SH,), 0)
    ups = halves(w_gate_up[0], (2 * FFH, 2 * FFH), 0)
    mix = jnp.concatenate([w_attn[0], w_out[0]], axis=0)
    cut = []
    for k in (0, 1):
        step = jnp.pad(steps[k][0], ((0, 0), (0, N - HEADS)))
        z_k = into[k][0]
        z_a = z_k.shape[1] // 2
        cut.append(
            {
                "first": jnp.concatenate(qkv[k] + [both_bc, step, z_k[:, :z_a]], axis=1),
                "second": jnp.concatenate([z_k[:, z_a:], into[k][1]], axis=1),
                "mix": mix[:, k * HALF : (k + 1) * HALF],
                "gate": ups[k][0],
                "up": ups[k][1],
                "down": w_down[0][:, k * HALF : (k + 1) * HALF],
            }
        )
    layers = ({}, {})
    for name in NAMES:
        own = jnp.where(first, cut[0][name], cut[1][name])
        got = swap(jnp.where(first, cut[1][name], cut[0][name]))
        layers[0][name] = jnp.where(first, own, got)
        layers[1][name] = jnp.where(first, got, own)

    kernel = Order()
    gathers = Gathers([(layers[0]["first"], layers[0]["second"])], kernel)
    rest_0 = Whole(layers[0], kernel, NAMES[2:])
    all_1 = Whole(layers[1], kernel, NAMES)
    rest_0.start()
    all_1.start()
    small = jnp.concatenate([norm_gains[0].reshape(-1), conv_params[0].reshape(-1)])
    small_other = swap(small)
    small = jnp.stack([jnp.where(first, small, small_other), jnp.where(first, small_other, small)])
    small = to_all(jnp.broadcast_to(small[None], (count,) + small.shape))
    small = small.swapaxes(0, 1).astype(F32)
    width = norm_gains.shape[2]
    gains = small[:, :, : 2 * width].reshape(2, count, 2, width).swapaxes(1, 2).reshape(2, 2, D)
    taps = small[:, :, 2 * width :].reshape(2, count, CONV + 1, -1).swapaxes(1, 2)
    taps = taps.reshape(2, CONV + 1, 4 * DI // 2 + 2 * N)
    taps = jnp.concatenate(
        [jnp.where(first, taps[..., :DI], taps[..., DI : 2 * DI]), taps[..., 2 * DI :]], axis=-1
    )
    heads_other = swap(head_params[0])
    heads = jnp.stack(
        [
            jnp.where(first, head_params[0], heads_other),
            jnp.where(first, heads_other, head_params[0]),
        ]
    )
    heads = jnp.where(first, heads[..., :HEADS], heads[..., HEADS:])
    heads = jnp.pad(heads, ((0, 0), (0, 5), (0, N - HEADS)))
    gains = gains.reshape(2, 2, 1, D)
    taps = jnp.pad(taps, ((0, 0), (0, 8 - CONV - 1), (0, 0)))

    other = swap(boundary[0])
    inputs = jnp.where(first, boundary[0], other).reshape(rows, D).astype(F32)
    positions = here * span + jnp.arange(span, dtype=jnp.int32)
    live = (positions[None, :] < lengths[:, None]).astype(F32)
    cotangent = jnp.where(first, other, boundary[0]).astype(F32) * live[..., None]
    cotangent = cotangent.reshape(rows, D)
    tables = rotation_tables(positions)

    reduces = Reduces(kernel)
    def pair(whole, one, two):
        return lambda: (whole.part(one), whole.part(two))

    sums, kept_0, weights_0, _ = layer_forward(
        kernel, inputs, lambda: gathers.get(0), rest_0.rows, pair(rest_0, "gate", "up"),
        gains[0], taps[0], heads[0], tables,
    )
    (handed,) = kernel(hand_body, [((rows, D), F32)], *sums)
    sums, kept_1, weights_1, turned = layer_forward(
        kernel, handed, pair(all_1, "first", "second"), all_1.rows, pair(all_1, "gate", "up"),
        gains[1], taps[1], heads[1], tables, cotangent,
    )
    conv_width = conv_params.shape[2]

    def spread(small_0, small_1):
        grad_gains, grad_taps, grad_heads = (jnp.stack(v) for v in zip(small_0, small_1))
        xs_part, none = grad_taps[..., :DI], jnp.zeros((2, CONV + 1, DI), F32)
        wide = jnp.concatenate(
            [jnp.where(first, xs_part, none), jnp.where(first, none, xs_part), grad_taps[..., DI:]],
            axis=2,
        )
        none = jnp.zeros((2, 3, HEADS), F32)
        head_wide = jnp.concatenate(
            [jnp.where(first, grad_heads, none), jnp.where(first, none, grad_heads)], axis=2
        )
        gains_once = jnp.where(first, grad_gains, 0.0)
        flat = jnp.concatenate(
            [
                gains_once.reshape(2, count, width).swapaxes(0, 1),
                wide.reshape(2, CONV + 1, count, conv_width)
                .transpose(2, 0, 1, 3)
                .reshape(count, 2, -1),
                jnp.broadcast_to(head_wide.reshape(1, 2, -1), (count, 2, 3 * SH)),
            ],
            axis=2,
        )
        flat = jnp.pad(flat, ((0, 0), (0, 0), (0, -flat.shape[2] % N)))
        return to_all(flat)

    kernel.weight = WEIGHT
    (grad_handed, turned), grads_1, small_1 = layer_backward(
        kernel, cotangent, turned, kept_1, weights_1, gains[1], taps[1], heads[1], tables, reduces,
        sums, kept_0[-3:-1] + weights_0[-3:],
    )
    grad_inputs, grads_0, small_0 = layer_backward(
        kernel, grad_handed, turned, kept_0, weights_0, gains[0], taps[0], heads[0], tables, reduces, owed=grads_1,
        spread=lambda small_0: spread(small_0, small_1),
    )

    at = corner()
    height = w_qkv.shape[1]
    grad_gu, grad_down, grad_attn, grad_out = kernel(
        late_grads_body,
        [(v.shape[1:], F32) for v in (w_gate_up, w_down, w_attn, w_out)], at, *grads_0["late"],
    )
    grad_qkv, grad_in, grad_dt, gain_one = kernel(
        early_grads_body,
        [((height, w_qkv.shape[2]), F32), ((height, w_in.shape[2]), F32), ((height, N), F32),
         ((height, N), F32)],
        at, *grads_0["early"],
    )

    flat = jnp.sum(small_0, axis=0)
    flat = jnp.where(first, flat[0], flat[1]) + swap(jnp.where(first, flat[1], flat[0]))
    taps_at = width
    heads_at = taps_at + (CONV + 1) * conv_width
    grad_gains = jnp.stack([gain_one[:, N - 1], flat[:taps_at]])
    grad_conv = flat[taps_at:heads_at].reshape(CONV + 1, conv_width)
    total_heads = flat[heads_at : heads_at + 3 * SH].reshape(3, SH)

    ends = jnp.where(first, grad_inputs, grads_1["result"]).reshape(2, span, D)
    outs = (
        ends, grad_gains, grad_qkv, grad_attn, grad_in, grad_dt[:, :SH], grad_conv, total_heads,
        grad_out, grad_gu, grad_down,
    )
    return tuple(out[None] for out in outs)


def solution(mesh):
    by_rows = P("section", "seq", None)
    by_columns = P("section", None, "seq")
    whole = P("section", None, None)
    ends = P("section", None, "seq", None)
    in_specs = (
        ends, P(), by_columns, by_rows, by_rows, by_rows, by_rows, by_columns, whole, by_rows,
        by_rows, by_rows,
    )
    out_specs = (
        ends, by_columns, by_rows, by_rows, by_rows, by_rows, by_columns, whole, by_rows, by_rows,
        by_rows,
    )
    return jax.shard_map(
        per_device, mesh=mesh, in_specs=in_specs, out_specs=out_specs, check_vma=False
    )
```
